32 devices in a mesh: groups: 2 (over y), field: 4 (over x, core), wave: 4 (over z).
Axes of the slice: x: 2, y: 2, z: 4, core: 2. Of those that a mesh axis runs over, the one named last changes fastest.
Arguments:
- mode_basis: bfloat16 [22, 512, 512], P(None, 'wave'), may hold values from -6 to 6
- coef_table: bfloat16 [4096, 22], replicated, may hold values from -1.5 to 1.5
- table_index: int32 [64], P(('groups', 'field')), parts along dimension 0, may hold values from 0 to 4095
- wave_lengths: float32 [8], P('wave'), may hold values from 0.32 to 1.05
- sed_table: float32 [1024, 8], replicated, may hold values from 0.05 to 1
- template_ids: int32 [64, 8], P(('groups', 'field')), parts along dimension 0, may hold values from 0 to 1023
Outputs:
- mixed: bfloat16 [64, 8, 256, 256], P(('groups', 'field'), None, 'wave'), parts along dimension 0
The draws below stay inside these ranges and needn't reach their ends.
There are 2 independent parts, one for each index of `groups`. The reference program is written for one: setup_inputs(seed, part) draws one part's arguments, and reference() takes and returns one part's arrays. A program takes and returns all parts, laid end to end along the dimension named above; an argument that names none is the same for every part. Nothing has to cross between parts.
All inputs are finite; a program needn't handle non-finite values.
Results may differ from the reference program's by a relative error of at most 0.0065.
Values may be sent and summed in bfloat16 or wider, within the bound.
No kernel may reach another device: no remote copies, remote signals or barrier semaphores. Data moves between devices by JAX's collectives and lax.ppermute only.
A program may use at most 128 MiB of HBM per device.

```python
import math
import jax
import jax.numpy as jnp
from jax import lax

PUP = 512
PIX = 256
K = 22
NTAB = 4096
NSED = 1024
J = 8
F = 32
W = 8


def with_ends(values, rng, least, largest):
    longest = values.shape.index(max(values.shape))
    spots = []
    for shift in (0, 1):
        where = [jax.random.randint(jax.random.fold_in(rng, axis), (), 0, length) for axis, length in enumerate(values.shape)]
        where[longest] = (where[longest] + shift) % values.shape[longest]
        spots.append(tuple(where))
    return values.at[spots[0]].set(least).at[spots[1]].set(largest)


def levels(key, extent, pieces, least, largest):
    level = 1.0
    for position, shards_of in pieces:
        steps = jax.random.uniform(jax.random.fold_in(jax.random.fold_in(key, 6), position), (shards_of,), jnp.float32, least / len(pieces), largest / len(pieces))
        level = level * jnp.repeat(jnp.exp(steps), extent[position] // shards_of).reshape((-1,) + (1,) * (len(extent) - 1 - position))
    return level


def gaussian(own_key, shape, deviation, reach, shards=(), held_as=jnp.bfloat16):
    array = jax.random.normal(own_key, shape, jnp.float32) * deviation
    if len(shards) > 0:
        array = levels(own_key, shape, shards, -0.22, 0.18) * array
    return jnp.clip(array, min=-reach, max=reach).astype(held_as)


def setup_inputs(seed: int = 0, part: int = 0) -> dict:
    key_list = jax.random.split(jax.random.key(seed), 7)
    part_keys = jax.random.split(jax.random.fold_in(key_list[6], part), 7)
    mode_basis = gaussian(key_list[0], (K, PUP, PUP), 1.0, 6.0, ((1, 4),))
    coef_table = gaussian(key_list[1], (NTAB, K), 0.25, 1.5)
    table_index = with_ends(jax.random.randint(part_keys[2], (F,), 0, NTAB), jax.random.fold_in(part_keys[2], 1), 0, NTAB - 1).astype(jnp.int32)
    wave_lengths = jnp.clip(jnp.exp(math.log(1.05) - 1.1882244 * jax.random.uniform(key_list[3], (W,), jnp.float32) ** levels(key_list[3], (W,), ((0, 4),), -0.2, 0.2)), 0.32, 1.05)
    sed_table = jnp.clip(jnp.exp(jax.random.uniform(key_list[4], (NSED, W), jnp.float32, math.log(0.05), math.log(1.0))), 0.05, 1.0)
    template_ids = with_ends(jax.random.randint(part_keys[5], (F, J), 0, NSED), jax.random.fold_in(part_keys[5], 1), 0, NSED - 1).astype(jnp.int32)
    return dict(mode_basis=mode_basis, coef_table=coef_table, table_index=table_index, wave_lengths=wave_lengths, sed_table=sed_table, template_ids=template_ids)


TWO_PI = 2.0 * math.pi
SAMPLING = 0.25
EPSILON = 1e-6


def transform_table(wave_lengths, pixels, pupil_side):
    pixel_offset = jnp.arange(pixels, dtype=jnp.int32) - pixels // 2
    pupil_offset = 2 * jnp.arange(pupil_side, dtype=jnp.int32) - pupil_side + 1
    products = (pixel_offset[:, None] * pupil_offset[None, :]).astype(jnp.float32)
    factor = (TWO_PI * SAMPLING / (2.0 * pupil_side)) / wave_lengths
    angles = products[None, :, :] * factor[:, None, None]
    cosine = jnp.cos(angles)
    sine_part = jnp.sin(angles)
    upper_half = jnp.concatenate([cosine, sine_part], axis=2)
    lower_half = jnp.concatenate([-sine_part, cosine], axis=2)
    return jnp.concatenate([upper_half, lower_half], axis=1).astype(jnp.bfloat16)


def aperture_rows(row_start, row_count, pupil_side):
    row_pos = 2 * (row_start + jnp.arange(row_count, dtype=jnp.int32)) - pupil_side + 1
    col_pos = 2 * jnp.arange(pupil_side, dtype=jnp.int32) - pupil_side + 1
    radius_sq = row_pos[:, None] * row_pos[:, None] + col_pos[None, :] * col_pos[None, :]
    inner_edge = (61 * pupil_side) // 100
    inside = (radius_sq <= pupil_side * pupil_side) & (radius_sq >= inner_edge * inner_edge)
    return inside.astype(jnp.float32)


def pupil_section(path_rows, wave_lengths, kernel_table):
    row_count = path_rows.shape[1]
    pupil_side = path_rows.shape[2]
    opening = aperture_rows(0, row_count, pupil_side)
    phase_map = path_rows[:, None, :, :] * (TWO_PI / wave_lengths)[None, :, None, None]
    field_real = opening * jnp.cos(phase_map)
    field_imag = opening * jnp.sin(phase_map)
    pupil_field = jnp.concatenate([field_real, field_imag], axis=3).astype(jnp.bfloat16)
    first_pass = jnp.einsum("flxy,luy->flxu", pupil_field.astype(jnp.float32), kernel_table.astype(jnp.float32))
    return first_pass.astype(jnp.bfloat16)


def finish_section(first_pass, kernel_table):
    pixels = first_pass.shape[3] // 2
    stacked = jnp.concatenate([first_pass[..., :pixels], first_pass[..., pixels:]], axis=2)
    image_field = jnp.einsum("lux,flxv->fluv", kernel_table.astype(jnp.float32), stacked.astype(jnp.float32))
    intensity = image_field[:, :, :pixels] * image_field[:, :, :pixels] + image_field[:, :, pixels:] * image_field[:, :, pixels:]
    mean_level = jnp.mean(intensity, axis=(2, 3), keepdims=True)
    return (intensity / (mean_level + EPSILON)).astype(jnp.bfloat16)


def reference(mode_basis, coef_table, table_index, wave_lengths, sed_table, template_ids):
    kernel_table = transform_table(wave_lengths, PIX, PUP)
    flat_basis = mode_basis.reshape(K, PUP * PUP)

    def one_position(inputs):
        index_value, id_row = inputs
        coeffs = coef_table[index_value]
        path_diff = jnp.dot(coeffs[None, :], flat_basis, preferred_element_type=jnp.float32).reshape(1, PUP, PUP)
        first_pass = pupil_section(path_diff, wave_lengths, kernel_table)
        spectra = finish_section(first_pass, kernel_table)
        raw_weights = sed_table[id_row]
        weights = (raw_weights / jnp.sum(raw_weights, axis=1, keepdims=True)).astype(jnp.bfloat16)
        mixed = jnp.einsum("jl,lrp->jrp", weights.astype(jnp.float32), spectra[0].astype(jnp.float32))
        return mixed.astype(jnp.bfloat16)

    return lax.map(one_position, (table_index, template_ids))
```

```python
import functools
import math

import jax
import jax.numpy as jnp
import numpy as np
from jax import lax
from jax.experimental import pallas as pl
from jax.experimental.pallas import tpu as pltpu
from jax.sharding import PartitionSpec as P

PUP = 512
PIX = 256
TWO_PI = 2.0 * math.pi
SAMPLING = 0.25
EPSILON = 1e-06
INNER = 61 * PUP // 100
BAND = 128
BANDS = PUP // BAND
ROWS = 16
LANES = 128
UNITS = BAND // ROWS
SHARES = 8

SIN_POLY = (4.4428679, -7.30744341, 3.59478797, -0.78437376)
COS_POLY = (1.4142135, -6.97885099, 5.73946117, -1.88356298, 0.31069817)


def band_rows(band):
    low, high = PUP // 2 - 64 * (band + 1), PUP // 2 + 64 * band
    return [low + ROWS * i for i in range(4)] + [high + ROWS * i for i in range(4)]


def band_columns(band):
    low, high = PUP // 2 - 64 * (band + 1), PUP // 2 + 64 * band
    sides = (high, low) if band % 2 == 0 else (low, high)
    return np.concatenate([side + np.arange(64) for side in sides])


def unit_open(row, band):
    a = 2 * (row + np.arange(ROWS)) - PUP + 1
    b = 2 * band_columns(band) - PUP + 1
    radius = a[:, None] ** 2 + b[None, :] ** 2
    return bool(np.any((radius <= PUP * PUP) & (radius >= INNER * INNER)))


CHUNKS = [
    (band, rows)
    for band in range(BANDS)
    for rows in range(BANDS)
    if any(unit_open(row, band) for row in band_rows(rows))
]


@functools.lru_cache(None)
def layout(waves, modes):
    per = PUP // waves
    lists = []
    for wave in range(waves):
        lists.append(
            [
                (band, row)
                for band in range(BANDS)
                for row in range(wave * per, (wave + 1) * per, ROWS)
                if unit_open(row, band)
            ]
        )
    count = max(len(one) for one in lists)
    half = -(-count * modes // (2 * SHARES))
    slabs = 2 * SHARES * half
    pack = np.zeros((waves, count, 3), np.int32)
    for wave, one in enumerate(lists):
        for i, (band, row) in enumerate(one):
            columns = band_columns(band)
            pack[wave, i] = (columns[0] // LANES * LANES, columns[64] // LANES * LANES, row - wave * per)
    place = np.zeros((len(CHUNKS) * UNITS, 4), np.int32)
    for c, (band, rows) in enumerate(CHUNKS):
        columns = band_columns(band)
        for j, row in enumerate(band_rows(rows)):
            wave = row // per
            slab = 0
            if (band, row) in lists[wave]:
                slab = wave * slabs + lists[wave].index((band, row)) * modes
            place[c * UNITS + j] = (slab, row, columns[0], columns[64] - 64)
    return count, half, slabs, pack, place


def pack_kernel(count, modes, table, basis, out):
    left = lax.broadcasted_iota(jnp.int32, (ROWS, LANES), 1) < 64

    def unit(i, carry):
        first = pl.multiple_of(table[i, 0], LANES)
        second = pl.multiple_of(table[i, 1], LANES)
        row = pl.multiple_of(table[i, 2], ROWS)
        for k in range(modes):
            one = basis[k, pl.ds(row, ROWS), pl.ds(first, LANES)].astype(jnp.float32)
            two = basis[k, pl.ds(row, ROWS), pl.ds(second, LANES)].astype(jnp.float32)
            out[i * modes + k] = jnp.where(left, one, two).astype(out.dtype)
        return carry

    lax.fori_loop(0, count, unit, 0)
    for n in range(count * modes, out.shape[0]):
        out[n] = jnp.zeros((ROWS, LANES), out.dtype)


def pack_rows(basis, table, slabs):
    modes = basis.shape[0]
    return pl.pallas_call(
        functools.partial(pack_kernel, table.shape[0], modes),
        out_shape=jax.ShapeDtypeStruct((slabs, ROWS, LANES), basis.dtype),
        in_specs=[pl.BlockSpec(memory_space=pltpu.SMEM), pl.BlockSpec(memory_space=pltpu.VMEM)],
        out_specs=pl.BlockSpec(memory_space=pltpu.VMEM),
        compiler_params=pltpu.CompilerParams(vmem_limit_bytes=24 * 2**20),
    )(table, basis)


def gather_rows(own, half, waves):
    groups, fields = lax.axis_size("groups"), lax.axis_size("field")
    share = (lax.axis_index("groups") % 2) * 4 + lax.axis_index("field") % 4

    def swap(x, mask):
        pairs = [
            (g * fields + f, (g ^ (mask >> 2)) * fields + (f ^ (mask & 3)))
            for g in range(groups)
            for f in range(fields)
        ]
        return lax.ppermute(x, ("groups", "field"), pairs)

    got = {}
    for h in range(2):
        piece = lax.dynamic_slice_in_dim(own, (2 * share + h) * half, half, axis=0)
        parts = [
            lax.ppermute(piece, "wave", [(i, (i + s) % waves) for i in range(waves)])
            for s in range(1, waves)
        ]
        got[0, h] = jnp.stack(parts)
    first, second = 2, 4
    for h in range(2):
        one, two = (first, second) if h == 0 else (second, first)
        got[one, h] = swap(got[0, h], one)
        got[two, h] = swap(got[0, h], two)
        got[one | two, h] = swap(got[one, h], two)
    for h in range(2):
        for mask in (0, 2, 4, 6):
            got[mask | 1, h] = swap(got[mask, h], 1)
    return got


def field_kernel(sizes, place_ref, where_ref, inverse_ref, *refs):
    positions, rows, modes, waves, half, slabs, keys = sizes
    parts = refs[: 1 + len(keys)]
    spread_ref, row_ref, column_ref, image_ref, sum_ref = refs[1 + len(keys) : 6 + len(keys)]
    basis, path, opening, pupil, total, first, sems = refs[6 + len(keys) :]
    wave = where_ref[0]
    share = where_ref[1]

    @pl.when(pl.program_id(0) == 0)
    def _():
        copies = [
            pltpu.make_async_copy(parts[0], basis.at[pl.ds(wave * slabs, slabs)], sems.at[0])
        ]
        n = 1
        for key, part in zip(keys, parts[1:]):
            mask, h = key
            for s in range(1, waves):
                source = lax.rem(wave + (waves - s), waves)
                start = source * slabs + (share ^ mask) * (2 * half) + h * half
                copies.append(
                    pltpu.make_async_copy(part.at[s - 1], basis.at[pl.ds(start, half)], sems.at[n])
                )
                n += 1
        for copy in copies:
            copy.start()
        for copy in copies:
            copy.wait()

        lane = lax.broadcasted_iota(jnp.int32, (ROWS, LANES), 1)
        line = lax.broadcasted_iota(jnp.int32, (ROWS, LANES), 0)

        def unit(u, carry):
            slab, row = place_ref[u, 0], place_ref[u, 1]
            a = 2 * (line + row) - (PUP - 1)
            b = 2 * (lane + jnp.where(lane < 64, place_ref[u, 2], place_ref[u, 3])) - (PUP - 1)
            radius = a * a + b * b
            inside = (radius <= PUP * PUP) & (radius >= INNER * INNER)
            values = basis[pl.ds(slab, modes)].reshape(modes * ROWS, LANES)
            found = jnp.dot(spread_ref[...], values, preferred_element_type=jnp.float32)
            opening[u] = jnp.where(inside, 1.0, 0.0)
            for f in range(positions):
                path[u, f * ROWS : (f + 1) * ROWS] = jnp.where(
                    inside, found[f * ROWS : (f + 1) * ROWS], 0.0
                )
            return carry

        lax.fori_loop(0, len(CHUNKS) * UNITS, unit, 0)

    inverse = inverse_ref[pl.program_id(0)]
    magic = jnp.float32(12582912.0)
    total[...] = jnp.zeros_like(total)

    def chunk(c, carry):
        band, rows_band = place_ref[c * UNITS, 4], place_ref[c * UNITS, 5]
        for j in range(UNITS):
            u = c * UNITS + j
            inside = opening[u]
            for f in range(positions):
                turns = path[u, f * ROWS : (f + 1) * ROWS] * inverse
                r = turns - ((turns + magic) - magic)
                z = r * r
                s = SIN_POLY[-1]
                for value in SIN_POLY[-2::-1]:
                    s = s * z + value
                s = s * r
                k = COS_POLY[-1]
                for value in COS_POLY[-2::-1]:
                    k = k * z + value
                columns = slice(f * LANES, (f + 1) * LANES)
                pupil[2 * ROWS * j : 2 * ROWS * j + ROWS, columns] = (inside - s * s).astype(
                    jnp.bfloat16
                )
                pupil[2 * ROWS * j + ROWS : 2 * ROWS * (j + 1), columns] = (s * k).astype(
                    jnp.bfloat16
                )
        total[band] += jnp.dot(
            row_ref[0, rows_band], pupil[...], preferred_element_type=jnp.float32
        )
        return carry

    lax.fori_loop(0, len(CHUNKS), chunk, 0)

    for band in range(BANDS):
        for f in range(positions):
            for part in range(2):
                first[
                    f * rows : (f + 1) * rows,
                    part * PUP + band * LANES : part * PUP + (band + 1) * LANES,
                ] = total[
                    band, part * rows : (part + 1) * rows, f * LANES : (f + 1) * LANES
                ].astype(jnp.bfloat16)
    for f in range(positions):
        both = jnp.dot(
            first[f * rows : (f + 1) * rows], column_ref[0], preferred_element_type=jnp.float32
        )
        real, imag = both[:, :PIX], both[:, PIX:]
        intensity = real * real + imag * imag
        image_ref[0, f * rows : (f + 1) * rows] = intensity.astype(jnp.bfloat16)
        sum_ref[0, f : f + 1] = jnp.sum(intensity, axis=0, keepdims=True)


def fields(own, got, spread, place, inverse, row_table, column_table, positions, rows, sizes):
    modes, waves, half, slabs = sizes
    keys = sorted(got)
    lengths = row_table.shape[0]
    units = place.shape[0]
    where = jnp.stack(
        [
            lax.axis_index("wave"),
            (lax.axis_index("groups") % 2) * 4 + lax.axis_index("field") % 4,
        ]
    ).astype(jnp.int32)
    place = jnp.concatenate(
        [place, np.repeat(np.array(CHUNKS, np.int32), UNITS, axis=0)], axis=1
    )
    smem = pl.BlockSpec(memory_space=pltpu.SMEM)
    hbm = pl.BlockSpec(memory_space=pl.ANY)
    return pl.pallas_call(
        functools.partial(
            field_kernel, (positions, rows, modes, waves, half, slabs, tuple(keys))
        ),
        grid=(lengths,),
        out_shape=(
            jax.ShapeDtypeStruct((lengths, positions * rows, PIX), jnp.bfloat16),
            jax.ShapeDtypeStruct((lengths, positions, PIX), jnp.float32),
        ),
        in_specs=[smem, smem, smem, hbm]
        + [hbm] * len(keys)
        + [
            pl.BlockSpec(spread.shape, lambda l: (0, 0)),
            pl.BlockSpec((1,) + row_table.shape[1:], lambda l: (l, 0, 0, 0)),
            pl.BlockSpec((1,) + column_table.shape[1:], lambda l: (l, 0, 0)),
        ],
        out_specs=(
            pl.BlockSpec((1, positions * rows, PIX), lambda l: (l, 0, 0)),
            pl.BlockSpec((1, positions, PIX), lambda l: (l, 0, 0)),
        ),
        scratch_shapes=[
            pltpu.VMEM((waves * slabs, ROWS, LANES), jnp.bfloat16),
            pltpu.VMEM((units, positions * ROWS, LANES), jnp.float32),
            pltpu.VMEM((units, ROWS, LANES), jnp.float32),
            pltpu.VMEM((2 * BAND, positions * LANES), jnp.bfloat16),
            pltpu.VMEM((BANDS, 2 * rows, positions * LANES), jnp.float32),
            pltpu.VMEM((positions * rows, 2 * PUP), jnp.bfloat16),
            pltpu.SemaphoreType.DMA((1 + len(keys) * (waves - 1),)),
        ],
        compiler_params=pltpu.CompilerParams(vmem_limit_bytes=56 * 2**20),
    )(place, where, inverse, own, *[got[key] for key in keys], spread, row_table, column_table)


def mix_kernel(weight_ref, image_ref, out_ref):
    f = pl.program_id(0)
    templates = out_ref.shape[1]
    lengths = image_ref.shape[0]
    for start in range(0, image_ref.shape[1], ROWS):
        rows = slice(start, start + ROWS)
        sums = [None] * templates
        for l in range(lengths):
            values = image_ref[l, rows].astype(jnp.float32)
            for j in range(templates):
                term = weight_ref[f, j * lengths + l] * values
                sums[j] = term if l == 0 else sums[j] + term
        for j in range(templates):
            out_ref[0, j, rows] = sums[j].astype(jnp.bfloat16)


def mix(weights, images, rows):
    positions, templates, lengths = weights.shape
    return pl.pallas_call(
        mix_kernel,
        grid=(positions,),
        out_shape=jax.ShapeDtypeStruct((positions, templates, rows, PIX), jnp.bfloat16),
        in_specs=[
            pl.BlockSpec(memory_space=pltpu.SMEM),
            pl.BlockSpec((lengths, rows, PIX), lambda f: (0, f, 0)),
        ],
        out_specs=pl.BlockSpec((1, templates, rows, PIX), lambda f: (f, 0, 0, 0)),
    )(weights.reshape(positions, templates * lengths), images)


def tables(wave_lengths, rows):
    factor = (TWO_PI * SAMPLING / (2.0 * PUP)) / wave_lengths
    y = 2 * np.concatenate([band_columns(band) for band in range(BANDS)]) - PUP + 1
    v = np.arange(PIX) - PIX // 2
    angles = (y[:, None] * v[None, :]).astype(np.float32)[None] * factor[:, None, None]
    cosine, sine = jnp.cos(angles), jnp.sin(angles)
    column_table = jnp.concatenate(
        [
            jnp.concatenate([cosine, -sine], axis=2),
            jnp.concatenate([sine, cosine], axis=2),
        ],
        axis=1,
    ).astype(jnp.bfloat16)
    u = lax.axis_index("wave") * rows + jnp.arange(rows, dtype=jnp.int32) - PIX // 2
    x = np.array(
        [[row + i for row in band_rows(band) for i in range(ROWS)] for band in range(BANDS)]
    )
    x = np.repeat(x.reshape(BANDS, UNITS, 1, ROWS), 2, axis=2).reshape(BANDS, 1, 2 * BAND)
    imag = ((np.arange(2 * BAND) // ROWS) % 2 == 1)[None, None, None, :]
    products = (u[None, :, None] * (2 * x - PUP + 1).astype(np.int32)).astype(jnp.float32)
    angles = products[None] * factor[:, None, None, None]
    cosine, sine = jnp.cos(angles), jnp.sin(angles)
    row_table = jnp.concatenate(
        [jnp.where(imag, sine, cosine), jnp.where(imag, cosine, -sine)], axis=2
    ).astype(jnp.bfloat16)
    return row_table, column_table


def local(mode_basis, coef_table, table_index, wave_lengths, sed_table, template_ids):
    waves = lax.axis_size("wave")
    modes = mode_basis.shape[0]
    positions = table_index.shape[0]
    rows = PIX // waves
    count, half, slabs, pack, place = layout(waves, modes)

    table = jnp.asarray(pack)[lax.axis_index("wave")]
    own = pack_rows(mode_basis, table, slabs)
    got = gather_rows(own, half, waves)

    every = lax.all_gather(wave_lengths, "wave", axis=0, tiled=True)
    row_table, column_table = tables(every, rows)

    selector = (
        table_index[:, None] == jnp.arange(coef_table.shape[0], dtype=jnp.int32)[None, :]
    ).astype(jnp.bfloat16)
    coeffs = jnp.dot(selector, coef_table, preferred_element_type=jnp.float32)
    spread = (
        (coeffs[:, None, :, None] * np.eye(ROWS, dtype=np.float32)[None, :, None, :])
        .reshape(positions * ROWS, modes * ROWS)
        .astype(jnp.bfloat16)
    )

    images, sums = fields(
        own,
        got,
        spread,
        place,
        1.0 / every,
        row_table,
        column_table,
        positions,
        rows,
        (modes, waves, half, slabs),
    )
    level = lax.psum(jnp.sum(sums, axis=2), "wave") / (PIX * PIX)

    one_hot = (
        template_ids[:, :, None]
        == jnp.arange(sed_table.shape[0], dtype=jnp.int32)[None, None, :]
    ).astype(jnp.float32)
    raw_weights = jnp.einsum("fjn,nl->fjl", one_hot, sed_table, precision=lax.Precision.HIGHEST)
    weights = (raw_weights / jnp.sum(raw_weights, axis=2, keepdims=True)).astype(jnp.bfloat16)
    weights = weights.astype(jnp.float32) / (level.T[:, None, :] + EPSILON)
    return mix(weights, images, rows)


def solution(mesh):
    return jax.shard_map(
        local,
        mesh=mesh,
        in_specs=(
            P(None, "wave", None),
            P(),
            P(("groups", "field")),
            P("wave"),
            P(),
            P(("groups", "field"), None),
        ),
        out_specs=P(("groups", "field"), None, "wave", None),
        check_vma=False,
    )
```

```python
import functools
import math

import jax
import jax.numpy as jnp
import numpy as np
from jax import lax
from jax.experimental import pallas as pl
from jax.experimental.pallas import tpu as pltpu
from jax.sharding import PartitionSpec as P

PUP = 512
PIX = 256
TWO_PI = 2.0 * math.pi
SAMPLING = 0.25
EPSILON = 1e-06
INNER = 61 * PUP // 100
BAND = 128
BANDS = PUP // BAND
ROWS = 16
LANES = 128
UNITS = BAND // ROWS
SHARES = 8

SIN_POLY = (4.4428679, -7.30744341, 3.59478797, -0.78437376)
COS_POLY = (1.4142135, -6.97885099, 5.73946117, -1.88356298, 0.31069817)


def half_turn(turns):
    magic = jnp.float32(12582912.0)
    r = turns - ((turns + magic) - magic)
    z = r * r
    s = jnp.float32(SIN_POLY[-1])
    for value in SIN_POLY[-2::-1]:
        s = s * z + value
    k = jnp.float32(COS_POLY[-1])
    for value in COS_POLY[-2::-1]:
        k = k * z + value
    return s * r, k


def band_rows(band):
    low, high = PUP // 2 - 64 * (band + 1), PUP // 2 + 64 * band
    return [low + ROWS * i for i in range(4)] + [high + ROWS * i for i in range(4)]


def band_columns(band):
    low, high = PUP // 2 - 64 * (band + 1), PUP // 2 + 64 * band
    sides = (high, low) if band % 2 == 0 else (low, high)
    return np.concatenate([side + np.arange(64) for side in sides])


def unit_open(row, band):
    a = 2 * (row + np.arange(ROWS)) - PUP + 1
    b = 2 * band_columns(band) - PUP + 1
    radius = a[:, None] ** 2 + b[None, :] ** 2
    return bool(np.any((radius <= PUP * PUP) & (radius >= INNER * INNER)))


CHUNKS = [
    (band, rows)
    for band in range(BANDS)
    for rows in range(BANDS)
    if any(unit_open(row, band) for row in band_rows(rows))
]


@functools.lru_cache(None)
def layout(waves, modes):
    per = PUP // waves
    lists = []
    for wave in range(waves):
        lists.append(
            [
                (band, row)
                for band in range(BANDS)
                for row in range(wave * per, (wave + 1) * per, ROWS)
                if unit_open(row, band)
            ]
        )
    count = max(len(one) for one in lists)
    half = -(-count * modes // (2 * SHARES))
    slabs = 2 * SHARES * half
    pack = np.zeros((waves, count, 3), np.int32)
    for wave, one in enumerate(lists):
        for i, (band, row) in enumerate(one):
            columns = band_columns(band)
            pack[wave, i] = (columns[0] // LANES * LANES, columns[64] // LANES * LANES, row - wave * per)
    place = np.zeros((len(CHUNKS) * UNITS, 4), np.int32)
    for c, (band, rows) in enumerate(CHUNKS):
        columns = band_columns(band)
        for j, row in enumerate(band_rows(rows)):
            wave = row // per
            slab = 0
            if (band, row) in lists[wave]:
                slab = wave * slabs + lists[wave].index((band, row)) * modes
            place[c * UNITS + j] = (slab, row, columns[0], columns[64] - 64)
    return count, half, slabs, pack, place


def pack_kernel(count, modes, table, basis, out):
    left = lax.broadcasted_iota(jnp.int32, (ROWS, LANES), 1) < 64

    def unit(i, carry):
        first = pl.multiple_of(table[i, 0], LANES)
        second = pl.multiple_of(table[i, 1], LANES)
        row = pl.multiple_of(table[i, 2], ROWS)
        for k in range(modes):
            one = basis[k, pl.ds(row, ROWS), pl.ds(first, LANES)].astype(jnp.float32)
            two = basis[k, pl.ds(row, ROWS), pl.ds(second, LANES)].astype(jnp.float32)
            out[i * modes + k] = jnp.where(left, one, two).astype(out.dtype)
        return carry

    lax.fori_loop(0, count, unit, 0)
    for n in range(count * modes, out.shape[0]):
        out[n] = jnp.zeros((ROWS, LANES), out.dtype)


def pack_rows(basis, table, slabs):
    modes = basis.shape[0]
    return pl.pallas_call(
        functools.partial(pack_kernel, table.shape[0], modes),
        out_shape=jax.ShapeDtypeStruct((slabs, ROWS, LANES), basis.dtype),
        in_specs=[pl.BlockSpec(memory_space=pltpu.SMEM), pl.BlockSpec(memory_space=pltpu.VMEM)],
        out_specs=pl.BlockSpec(memory_space=pltpu.VMEM),
        compiler_params=pltpu.CompilerParams(vmem_limit_bytes=24 * 2**20),
    )(table, basis)


def gather_rows(own, half, waves):
    groups, fields = lax.axis_size("groups"), lax.axis_size("field")
    share = (lax.axis_index("groups") % 2) * 4 + lax.axis_index("field") % 4

    def swap(x, mask):
        pairs = [
            (g * fields + f, (g ^ (mask >> 2)) * fields + (f ^ (mask & 3)))
            for g in range(groups)
            for f in range(fields)
        ]
        return lax.ppermute(x, ("groups", "field"), pairs)

    got = {}
    for h in range(2):
        piece = lax.dynamic_slice_in_dim(own, (2 * share + h) * half, half, axis=0)
        parts = [
            lax.ppermute(piece, "wave", [(i, (i + s) % waves) for i in range(waves)])
            for s in range(1, waves)
        ]
        got[0, h] = jnp.stack(parts)
    first, second = 2, 4
    for h in range(2):
        one, two = (first, second) if h == 0 else (second, first)
        got[one, h] = swap(got[0, h], one)
        got[two, h] = swap(got[0, h], two)
        got[one | two, h] = swap(got[one, h], two)
    for h in range(2):
        for mask in (0, 2, 4, 6):
            got[mask | 1, h] = swap(got[mask, h], 1)
    return got


def field_kernel(sizes, place_ref, where_ref, inverse_ref, *refs):
    positions, rows, modes, waves, half, slabs, keys = sizes
    parts = refs[: 1 + len(keys)]
    spread_ref, row_ref, column_ref, image_ref, sum_ref = refs[1 + len(keys) : 6 + len(keys)]
    basis, path, opening, even, odd, total, first, sems = refs[6 + len(keys) :]
    wave = where_ref[0]
    share = where_ref[1]

    @pl.when(pl.program_id(0) == 0)
    def _():
        copies = [
            pltpu.make_async_copy(parts[0], basis.at[pl.ds(wave * slabs, slabs)], sems.at[0])
        ]
        n = 1
        for key, part in zip(keys, parts[1:]):
            mask, h = key
            for s in range(1, waves):
                source = lax.rem(wave + (waves - s), waves)
                start = source * slabs + (share ^ mask) * (2 * half) + h * half
                copies.append(
                    pltpu.make_async_copy(part.at[s - 1], basis.at[pl.ds(start, half)], sems.at[n])
                )
                n += 1
        for copy in copies:
            copy.start()
        for copy in copies:
            copy.wait()

        lane = lax.broadcasted_iota(jnp.int32, (ROWS, LANES), 1)
        line = lax.broadcasted_iota(jnp.int32, (ROWS, LANES), 0)

        def chunk(c, carry):
            values = jnp.concatenate(
                [
                    basis[pl.ds(place_ref[c * UNITS + j, 0], modes)].reshape(modes * ROWS, LANES)
                    for j in range(UNITS)
                ],
                axis=1,
            )
            found = jnp.dot(spread_ref[...], values, preferred_element_type=jnp.float32)
            for j in range(UNITS):
                u = c * UNITS + j
                a = 2 * (line + place_ref[u, 1]) - (PUP - 1)
                b = 2 * (lane + jnp.where(lane < 64, place_ref[u, 2], place_ref[u, 3])) - (PUP - 1)
                radius = a * a + b * b
                inside = (radius <= PUP * PUP) & (radius >= INNER * INNER)
                opening[u] = jnp.where(inside, 1.0, 0.0)
                for f in range(positions):
                    path[u, f * ROWS : (f + 1) * ROWS] = jnp.where(
                        inside, found[f * ROWS : (f + 1) * ROWS, j * LANES : (j + 1) * LANES], 0.0
                    )
            return carry

        lax.fori_loop(0, len(CHUNKS), chunk, 0)

    inverse = inverse_ref[pl.program_id(0)]
    total[...] = jnp.zeros_like(total)
    odd[...] = jnp.zeros_like(odd)

    def form(c, pupil, before, held):
        band, rows_band = place_ref[before * UNITS, 4], place_ref[before * UNITS, 5]
        for j in range(UNITS):
            u = c * UNITS + j
            inside = opening[u]
            for f in range(positions):
                turns = path[u, f * ROWS : (f + 1) * ROWS] * inverse
                s, k = half_turn(turns)
                columns = slice(f * LANES, (f + 1) * LANES)
                pupil[2 * ROWS * j : 2 * ROWS * j + ROWS, columns] = (inside - s * s).astype(
                    jnp.bfloat16
                )
                pupil[2 * ROWS * j + ROWS : 2 * ROWS * (j + 1), columns] = (s * k).astype(
                    jnp.bfloat16
                )
            width = positions * LANES // UNITS
            if j % 2 == 1:
                columns = slice((j - 1) * width, (j + 1) * width)
                total[band, :, columns] += jnp.dot(
                    row_ref[0, rows_band], held[:, columns], preferred_element_type=jnp.float32
                )

    def pair(i, carry):
        form(2 * i, even, jnp.maximum(2 * i - 1, 0), odd)
        form(2 * i + 1, odd, 2 * i, even)
        return carry

    lax.fori_loop(0, len(CHUNKS) // 2, pair, 0)
    band, rows_band = CHUNKS[-1]
    total[band] += jnp.dot(row_ref[0, rows_band], odd[...], preferred_element_type=jnp.float32)

    for band in range(BANDS):
        for f in range(positions):
            for part in range(2):
                first[
                    f * rows : (f + 1) * rows,
                    part * PUP + band * LANES : part * PUP + (band + 1) * LANES,
                ] = total[
                    band, part * rows : (part + 1) * rows, f * LANES : (f + 1) * LANES
                ].astype(jnp.bfloat16)
    real = jnp.dot(first[...], column_ref[0, :, :PIX], preferred_element_type=jnp.float32)
    imag = jnp.dot(first[...], column_ref[0, :, PIX:], preferred_element_type=jnp.float32)
    intensity = real * real + imag * imag
    image_ref[0] = intensity.astype(jnp.bfloat16)
    sum_ref[0] = jnp.sum(intensity.reshape(positions, rows, PIX), axis=1)


def fields(own, got, spread, place, inverse, row_table, column_table, positions, rows, sizes):
    modes, waves, half, slabs = sizes
    keys = sorted(got)
    lengths = row_table.shape[0]
    units = place.shape[0]
    where = jnp.stack(
        [
            lax.axis_index("wave"),
            (lax.axis_index("groups") % 2) * 4 + lax.axis_index("field") % 4,
        ]
    ).astype(jnp.int32)
    place = jnp.concatenate(
        [place, np.repeat(np.array(CHUNKS, np.int32), UNITS, axis=0)], axis=1
    )
    smem = pl.BlockSpec(memory_space=pltpu.SMEM)
    hbm = pl.BlockSpec(memory_space=pl.ANY)
    return pl.pallas_call(
        functools.partial(
            field_kernel, (positions, rows, modes, waves, half, slabs, tuple(keys))
        ),
        grid=(lengths,),
        out_shape=(
            jax.ShapeDtypeStruct((lengths, positions * rows, PIX), jnp.bfloat16),
            jax.ShapeDtypeStruct((lengths, positions, PIX), jnp.float32),
        ),
        in_specs=[smem, smem, smem, hbm]
        + [hbm] * len(keys)
        + [
            pl.BlockSpec(spread.shape, lambda l: (0, 0)),
            pl.BlockSpec((1,) + row_table.shape[1:], lambda l: (l, 0, 0, 0)),
            pl.BlockSpec((1,) + column_table.shape[1:], lambda l: (l, 0, 0)),
        ],
        out_specs=(
            pl.BlockSpec((1, positions * rows, PIX), lambda l: (l, 0, 0)),
            pl.BlockSpec((1, positions, PIX), lambda l: (l, 0, 0)),
        ),
        scratch_shapes=[
            pltpu.VMEM((waves * slabs, ROWS, LANES), jnp.bfloat16),
            pltpu.VMEM((units, positions * ROWS, LANES), jnp.float32),
            pltpu.VMEM((units, ROWS, LANES), jnp.float32),
            pltpu.VMEM((2 * BAND, positions * LANES), jnp.bfloat16),
            pltpu.VMEM((2 * BAND, positions * LANES), jnp.bfloat16),
            pltpu.VMEM((BANDS, 2 * rows, positions * LANES), jnp.float32),
            pltpu.VMEM((positions * rows, 2 * PUP), jnp.bfloat16),
            pltpu.SemaphoreType.DMA((1 + len(keys) * (waves - 1),)),
        ],
        compiler_params=pltpu.CompilerParams(vmem_limit_bytes=56 * 2**20),
    )(place, where, inverse, own, *[got[key] for key in keys], spread, row_table, column_table)


def mix_kernel(weight_ref, image_ref, out_ref):
    f = pl.program_id(0)
    templates = out_ref.shape[1]
    lengths = image_ref.shape[0]
    for start in range(0, image_ref.shape[1], ROWS):
        rows = slice(start, start + ROWS)
        sums = [None] * templates
        for l in range(lengths):
            values = image_ref[l, rows].astype(jnp.float32)
            for j in range(templates):
                term = weight_ref[f, j * lengths + l] * values
                sums[j] = term if l == 0 else sums[j] + term
        for j in range(templates):
            out_ref[0, j, rows] = sums[j].astype(jnp.bfloat16)


def mix(weights, images, rows):
    positions, templates, lengths = weights.shape
    return pl.pallas_call(
        mix_kernel,
        grid=(positions,),
        out_shape=jax.ShapeDtypeStruct((positions, templates, rows, PIX), jnp.bfloat16),
        in_specs=[
            pl.BlockSpec(memory_space=pltpu.SMEM),
            pl.BlockSpec((lengths, rows, PIX), lambda f: (0, f, 0)),
        ],
        out_specs=pl.BlockSpec((1, templates, rows, PIX), lambda f: (f, 0, 0, 0)),
    )(weights.reshape(positions, templates * lengths), images)


def table_kernel(scale_ref, y_ref, v_ref, u_ref, x_ref, row_ref, column_ref):
    scale = scale_ref[pl.program_id(0)]
    for start in range(0, PUP, ROWS):
        s, k = half_turn((y_ref[start : start + ROWS] * v_ref[...]) * scale)
        cosine, sine = 1.0 - s * s, s * k
        lower = slice(start, start + ROWS)
        upper = slice(PUP + start, PUP + start + ROWS)
        column_ref[0, lower, :PIX] = cosine.astype(jnp.bfloat16)
        column_ref[0, lower, PIX:] = (-sine).astype(jnp.bfloat16)
        column_ref[0, upper, :PIX] = sine.astype(jnp.bfloat16)
        column_ref[0, upper, PIX:] = cosine.astype(jnp.bfloat16)
    rows = u_ref.shape[0]
    imag = (lax.broadcasted_iota(jnp.int32, (ROWS, 2 * BAND), 1) // ROWS) % 2 == 1
    for band in range(BANDS):
        for start in range(0, rows, ROWS):
            s, k = half_turn((u_ref[start : start + ROWS] * x_ref[band]) * scale)
            cosine, sine = 1.0 - s * s, s * k
            row_ref[0, band, start : start + ROWS] = jnp.where(imag, sine, cosine).astype(
                jnp.bfloat16
            )
            row_ref[0, band, rows + start : rows + start + ROWS] = jnp.where(
                imag, cosine, -sine
            ).astype(jnp.bfloat16)


def tables(wave_lengths, rows):
    lengths = wave_lengths.shape[0]
    scale = (SAMPLING / (2.0 * PUP)) / wave_lengths
    y = 2 * np.concatenate([band_columns(band) for band in range(BANDS)]) - PUP + 1
    v = np.arange(PIX) - PIX // 2
    u = lax.axis_index("wave") * rows + jnp.arange(rows, dtype=jnp.int32) - PIX // 2
    x = np.array(
        [[row + i for row in band_rows(band) for i in range(ROWS)] for band in range(BANDS)]
    )
    x = np.repeat(x.reshape(BANDS, UNITS, 1, ROWS), 2, axis=2).reshape(BANDS, 1, 2 * BAND)
    whole = lambda *shape: pl.BlockSpec(shape, lambda l: (0,) * len(shape))
    return pl.pallas_call(
        table_kernel,
        grid=(lengths,),
        out_shape=(
            jax.ShapeDtypeStruct((lengths, BANDS, 2 * rows, 2 * BAND), jnp.bfloat16),
            jax.ShapeDtypeStruct((lengths, 2 * PUP, 2 * PIX), jnp.bfloat16),
        ),
        in_specs=[
            pl.BlockSpec(memory_space=pltpu.SMEM),
            whole(PUP, 1),
            whole(1, PIX),
            whole(rows, 1),
            whole(BANDS, 1, 2 * BAND),
        ],
        out_specs=(
            pl.BlockSpec((1, BANDS, 2 * rows, 2 * BAND), lambda l: (l, 0, 0, 0)),
            pl.BlockSpec((1, 2 * PUP, 2 * PIX), lambda l: (l, 0, 0)),
        ),
        cost_estimate=pl.CostEstimate(
            flops=lengths * 30 * PUP * PIX, bytes_accessed=lengths * 4 * PUP * PIX * 2, transcendentals=0
        ),
        compiler_params=pltpu.CompilerParams(vmem_limit_bytes=24 * 2**20),
    )(
        scale,
        jnp.asarray(y[:, None].astype(np.float32)),
        jnp.asarray(v[None, :].astype(np.float32)),
        u.astype(jnp.float32)[:, None],
        jnp.asarray((2 * x - PUP + 1).astype(np.float32)),
    )


def every_length(wave_lengths, waves):
    mine = lax.axis_index("wave")
    count = wave_lengths.shape[0]
    out = jnp.zeros((waves * count,), wave_lengths.dtype)
    for s in range(waves):
        part = wave_lengths
        if s > 0:
            part = lax.ppermute(part, "wave", [(i, (i + s) % waves) for i in range(waves)])
        out = lax.dynamic_update_slice(out, part, (((mine - s) % waves) * count,))
    return out


def local(mode_basis, coef_table, table_index, wave_lengths, sed_table, template_ids):
    waves = lax.axis_size("wave")
    modes = mode_basis.shape[0]
    positions = table_index.shape[0]
    rows = PIX // waves
    count, half, slabs, pack, place = layout(waves, modes)

    every = every_length(wave_lengths, waves)
    table = jnp.asarray(pack)[lax.axis_index("wave")]
    own = pack_rows(mode_basis, table, slabs)
    got = gather_rows(own, half, waves)

    row_table, column_table = tables(every, rows)

    selector = (
        table_index[:, None] == jnp.arange(coef_table.shape[0], dtype=jnp.int32)[None, :]
    ).astype(jnp.bfloat16)
    coeffs = jnp.dot(selector, coef_table, preferred_element_type=jnp.float32)
    spread = (
        (coeffs[:, None, :, None] * np.eye(ROWS, dtype=np.float32)[None, :, None, :])
        .reshape(positions * ROWS, modes * ROWS)
        .astype(jnp.bfloat16)
    )

    images, sums = fields(
        own,
        got,
        spread,
        place,
        1.0 / every,
        row_table,
        column_table,
        positions,
        rows,
        (modes, waves, half, slabs),
    )
    level = lax.psum(jnp.sum(sums, axis=2), "wave") / (PIX * PIX)

    one_hot = (
        template_ids[:, :, None]
        == jnp.arange(sed_table.shape[0], dtype=jnp.int32)[None, None, :]
    ).astype(jnp.float32)
    raw_weights = jnp.einsum("fjn,nl->fjl", one_hot, sed_table, precision=lax.Precision.HIGHEST)
    weights = (raw_weights / jnp.sum(raw_weights, axis=2, keepdims=True)).astype(jnp.bfloat16)
    weights = weights.astype(jnp.float32) / (level.T[:, None, :] + EPSILON)
    return mix(weights, images, rows)


def solution(mesh):
    return jax.shard_map(
        local,
        mesh=mesh,
        in_specs=(
            P(None, "wave", None),
            P(),
            P(("groups", "field")),
            P("wave"),
            P(),
            P(("groups", "field"), None),
        ),
        out_specs=P(("groups", "field"), None, "wave", None),
        check_vma=False,
    )
```

```python
import functools
import math

import jax
import jax.numpy as jnp
import numpy as np
from jax import lax
from jax.experimental import pallas as pl
from jax.experimental.pallas import tpu as pltpu
from jax.sharding import PartitionSpec as P

PUP = 512
PIX = 256
TWO_PI = 2.0 * math.pi
SAMPLING = 0.25
EPSILON = 1e-06
INNER = 61 * PUP // 100
BAND = 128
BANDS = PUP // BAND
ROWS = 16
LANES = 128
UNITS = BAND // ROWS
SHARES = 8

SIN_POLY = (4.4428679, -7.30744341, 3.59478797, -0.78437376)
COS_POLY = (1.4142135, -6.97885099, 5.73946117, -1.88356298, 0.31069817)


def half_turn(turns):
    magic = jnp.float32(12582912.0)
    r = turns - ((turns + magic) - magic)
    z = r * r
    s = jnp.float32(SIN_POLY[-1])
    for value in SIN_POLY[-2::-1]:
        s = s * z + value
    k = jnp.float32(COS_POLY[-1])
    for value in COS_POLY[-2::-1]:
        k = k * z + value
    return s * r, k


def band_rows(band):
    low, high = PUP // 2 - 64 * (band + 1), PUP // 2 + 64 * band
    return [low + ROWS * i for i in range(4)] + [high + ROWS * i for i in range(4)]


def band_columns(band):
    low, high = PUP // 2 - 64 * (band + 1), PUP // 2 + 64 * band
    sides = (high, low) if band % 2 == 0 else (low, high)
    return np.concatenate([side + np.arange(64) for side in sides])


def unit_open(row, band):
    a = 2 * (row + np.arange(ROWS)) - PUP + 1
    b = 2 * band_columns(band) - PUP + 1
    radius = a[:, None] ** 2 + b[None, :] ** 2
    return bool(np.any((radius <= PUP * PUP) & (radius >= INNER * INNER)))


CHUNKS = [
    (band, rows)
    for band in range(BANDS)
    for rows in range(BANDS)
    if any(unit_open(row, band) for row in band_rows(rows))
]


@functools.lru_cache(None)
def layout(waves, modes):
    per = PUP // waves
    lists = []
    for wave in range(waves):
        lists.append(
            [
                (band, row)
                for band in range(BANDS)
                for row in range(wave * per, (wave + 1) * per, ROWS)
                if unit_open(row, band)
            ]
        )
    count = max(len(one) for one in lists)
    half = -(-count * modes // (2 * SHARES))
    slabs = 2 * SHARES * half
    pack = np.zeros((waves, count, 3), np.int32)
    for wave, one in enumerate(lists):
        for i, (band, row) in enumerate(one):
            columns = band_columns(band)
            pack[wave, i] = (columns[0] // LANES * LANES, columns[64] // LANES * LANES, row - wave * per)
    place = np.zeros((len(CHUNKS) * UNITS, 4), np.int32)
    for c, (band, rows) in enumerate(CHUNKS):
        columns = band_columns(band)
        for j, row in enumerate(band_rows(rows)):
            wave = row // per
            slab = 0
            if (band, row) in lists[wave]:
                slab = wave * slabs + lists[wave].index((band, row)) * modes
            place[c * UNITS + j] = (slab, row, columns[0], columns[64] - 64)
    return count, half, slabs, pack, place


def pack_kernel(count, modes, table, basis, out):
    left = lax.broadcasted_iota(jnp.int32, (ROWS, LANES), 1) < 64

    def unit(i, carry):
        first = pl.multiple_of(table[i, 0], LANES)
        second = pl.multiple_of(table[i, 1], LANES)
        row = pl.multiple_of(table[i, 2], ROWS)
        for k in range(modes):
            one = basis[k, pl.ds(row, ROWS), pl.ds(first, LANES)].astype(jnp.float32)
            two = basis[k, pl.ds(row, ROWS), pl.ds(second, LANES)].astype(jnp.float32)
            out[i * modes + k] = jnp.where(left, one, two).astype(out.dtype)
        return carry

    lax.fori_loop(0, count, unit, 0)
    for n in range(count * modes, out.shape[0]):
        out[n] = jnp.zeros((ROWS, LANES), out.dtype)


def pack_rows(basis, table, slabs):
    modes = basis.shape[0]
    return pl.pallas_call(
        functools.partial(pack_kernel, table.shape[0], modes),
        out_shape=jax.ShapeDtypeStruct((slabs, ROWS, LANES), basis.dtype),
        in_specs=[pl.BlockSpec(memory_space=pltpu.SMEM), pl.BlockSpec(memory_space=pltpu.VMEM)],
        out_specs=pl.BlockSpec(memory_space=pltpu.VMEM),
        compiler_params=pltpu.CompilerParams(vmem_limit_bytes=24 * 2**20),
    )(table, basis)


def gather_rows(own, half, waves):
    groups, fields = lax.axis_size("groups"), lax.axis_size("field")
    share = (lax.axis_index("groups") % 2) * 4 + lax.axis_index("field") % 4

    def swap(x, mask):
        pairs = [
            (g * fields + f, (g ^ (mask >> 2)) * fields + (f ^ (mask & 3)))
            for g in range(groups)
            for f in range(fields)
        ]
        return lax.ppermute(x, ("groups", "field"), pairs)

    got = {}
    for h in range(2):
        piece = lax.dynamic_slice_in_dim(own, (2 * share + h) * half, half, axis=0)
        parts = [
            lax.ppermute(piece, "wave", [(i, (i + s) % waves) for i in range(waves)])
            for s in range(1, waves)
        ]
        got[0, h] = jnp.stack(parts)
    first, second = 2, 4
    for h in range(2):
        one, two = (first, second) if h == 0 else (second, first)
        got[one, h] = swap(got[0, h], one)
        got[two, h] = swap(got[0, h], two)
        got[one | two, h] = swap(got[one, h], two)
    for h in range(2):
        for mask in (0, 2, 4, 6):
            got[mask | 1, h] = swap(got[mask, h], 1)
    return got


def path_kernel(sizes, place_ref, where_ref, *refs):
    positions, modes, waves, half, slabs, keys = sizes
    parts = refs[: 1 + len(keys)]
    spread_ref = refs[1 + len(keys)]
    path, opening, basis, sems = refs[-4:]
    wave = where_ref[0]
    share = where_ref[1]
    copies = [pltpu.make_async_copy(parts[0], basis.at[pl.ds(wave * slabs, slabs)], sems.at[0])]
    n = 1
    for key, part in zip(keys, parts[1:]):
        mask, h = key
        for s in range(1, waves):
            source = lax.rem(wave + (waves - s), waves)
            start = source * slabs + (share ^ mask) * (2 * half) + h * half
            copies.append(
                pltpu.make_async_copy(part.at[s - 1], basis.at[pl.ds(start, half)], sems.at[n])
            )
            n += 1
    for copy in copies:
        copy.start()
    for copy in copies:
        copy.wait()

    lane = lax.broadcasted_iota(jnp.int32, (ROWS, LANES), 1)
    line = lax.broadcasted_iota(jnp.int32, (ROWS, LANES), 0)

    def chunk(c, carry):
        values = jnp.concatenate(
            [
                basis[pl.ds(place_ref[c * UNITS + j, 0], modes)].reshape(modes * ROWS, LANES)
                for j in range(UNITS)
            ],
            axis=1,
        )
        found = jnp.dot(spread_ref[...], values, preferred_element_type=jnp.float32)
        for j in range(UNITS):
            u = c * UNITS + j
            a = 2 * (line + place_ref[u, 1]) - (PUP - 1)
            b = 2 * (lane + jnp.where(lane < 64, place_ref[u, 2], place_ref[u, 3])) - (PUP - 1)
            radius = a * a + b * b
            inside = (radius <= PUP * PUP) & (radius >= INNER * INNER)
            opening[u] = jnp.where(inside, 1.0, 0.0)
            for f in range(positions):
                path[u, f * ROWS : (f + 1) * ROWS] = jnp.where(
                    inside, found[f * ROWS : (f + 1) * ROWS, j * LANES : (j + 1) * LANES], 0.0
                )
        return carry

    lax.fori_loop(0, len(CHUNKS), chunk, 0)


def paths(own, got, spread, place, after, positions, sizes):
    modes, waves, half, slabs = sizes
    keys = sorted(got)
    units = place.shape[0]
    where = jnp.stack(
        [
            lax.axis_index("wave"),
            (lax.axis_index("groups") % 2) * 4 + lax.axis_index("field") % 4,
        ]
    ).astype(jnp.int32)
    smem = pl.BlockSpec(memory_space=pltpu.SMEM)
    hbm = pl.BlockSpec(memory_space=pl.ANY)
    vmem = pl.BlockSpec(memory_space=pltpu.VMEM)
    return pl.pallas_call(
        functools.partial(path_kernel, (positions, modes, waves, half, slabs, tuple(keys))),
        out_shape=(
            jax.ShapeDtypeStruct((units, positions * ROWS, LANES), jnp.float32),
            jax.ShapeDtypeStruct((units, ROWS, LANES), jnp.float32),
        ),
        in_specs=[smem, smem, hbm] + [hbm] * len(keys) + [vmem] + [hbm] * len(after),
        out_specs=(vmem, vmem),
        scratch_shapes=[
            pltpu.VMEM((waves * slabs, ROWS, LANES), jnp.bfloat16),
            pltpu.SemaphoreType.DMA((1 + len(keys) * (waves - 1),)),
        ],
        compiler_params=pltpu.CompilerParams(vmem_limit_bytes=32 * 2**20),
    )(place, where, own, *[got[key] for key in keys], spread, *after)


def field_kernel(sizes, inverse_ref, path, opening, row_ref, column_ref, *refs):
    positions, rows, parts = sizes
    image_ref = refs[0]
    even, odd, total, first = refs[-4:]
    inverse = inverse_ref[pl.program_id(0)]
    total[...] = jnp.zeros_like(total)
    odd[...] = jnp.zeros_like(odd)
    batch = max(1, positions // 2)

    def form(c, pupil, band, rows_band, held):
        for j in range(UNITS):
            u = c * UNITS + j
            inside = opening[u]
            for f0 in range(0, positions, batch):
                s, k = half_turn(path[u, f0 * ROWS : (f0 + batch) * ROWS] * inverse)
                sine = s * k
                square = s * s
                for f in range(f0, f0 + batch):
                    columns = slice(f * LANES, (f + 1) * LANES)
                    lines = slice((f - f0) * ROWS, (f - f0 + 1) * ROWS)
                    pupil[2 * ROWS * j : 2 * ROWS * j + ROWS, columns] = (
                        inside - square[lines]
                    ).astype(jnp.bfloat16)
                    pupil[2 * ROWS * j + ROWS : 2 * ROWS * (j + 1), columns] = sine[lines].astype(
                        jnp.bfloat16
                    )
            width = positions * LANES // UNITS
            if j % 2 == 1:
                columns = slice((j - 1) * width, (j + 1) * width)
                total[band, :, columns] += jnp.dot(
                    row_ref[0, rows_band], held[:, columns], preferred_element_type=jnp.float32
                )

    def chunk_bands(c):
        band, rows_band = jnp.int32(CHUNKS[0][0]), jnp.int32(CHUNKS[0][1])
        for n, (one, two) in enumerate(CHUNKS[1:]):
            band = jnp.where(c > n, one, band)
            rows_band = jnp.where(c > n, two, rows_band)
        return band, rows_band

    def pair(i, carry):
        form(2 * i, even, *chunk_bands(2 * i - 1), odd)
        form(2 * i + 1, odd, *chunk_bands(2 * i), even)
        return carry

    lax.fori_loop(0, len(CHUNKS) // 2, pair, 0)
    band, rows_band = CHUNKS[-1]
    total[band] += jnp.dot(row_ref[0, rows_band], odd[...], preferred_element_type=jnp.float32)

    for band in range(BANDS):
        for f in range(positions):
            for part in range(2):
                first[
                    f * rows : (f + 1) * rows,
                    part * PUP + band * LANES : part * PUP + (band + 1) * LANES,
                ] = total[
                    band, part * rows : (part + 1) * rows, f * LANES : (f + 1) * LANES
                ].astype(jnp.bfloat16)
    if parts == 1:
        sum_ref = refs[1]
        real = jnp.dot(first[...], column_ref[0, :, :PIX], preferred_element_type=jnp.float32)
        imag = jnp.dot(first[...], column_ref[0, :, PIX:], preferred_element_type=jnp.float32)
        intensity = real * real + imag * imag
        image_ref[0] = intensity
        sum_ref[0] = jnp.sum(intensity.reshape(positions, rows, PIX), axis=1)
    else:
        share = rows // parts
        for f in range(positions):
            lines = first[f * rows : (f + 1) * rows]
            real = jnp.dot(lines, column_ref[0, :, :PIX], preferred_element_type=jnp.float32)
            imag = jnp.dot(lines, column_ref[0, :, PIX:], preferred_element_type=jnp.float32)
            intensity = real * real + imag * imag
            level = jnp.sum(
                jnp.sum(intensity, axis=0, keepdims=True), axis=1, keepdims=True
            ) / (rows * PIX)
            spectra = (intensity / (level + EPSILON)).astype(jnp.bfloat16)
            for part in range(parts):
                image_ref[part, 0, f * share : (f + 1) * share] = spectra[
                    part * share : (part + 1) * share
                ]


def fields(path, opening, inverse, row_table, column_table, positions, parts):
    lengths = row_table.shape[0]
    rows = row_table.shape[2] // 2
    if parts == 1:
        out_shape = (
            jax.ShapeDtypeStruct((lengths, positions * rows, PIX), jnp.float32),
            jax.ShapeDtypeStruct((lengths, positions, PIX), jnp.float32),
        )
        out_specs = (
            pl.BlockSpec((1, positions * rows, PIX), lambda l: (l, 0, 0)),
            pl.BlockSpec((1, positions, PIX), lambda l: (l, 0, 0)),
        )
    else:
        share = positions * rows // parts
        out_shape = jax.ShapeDtypeStruct((parts, lengths, share, PIX), jnp.bfloat16)
        out_specs = pl.BlockSpec((parts, 1, share, PIX), lambda l: (0, l, 0, 0))
    return pl.pallas_call(
        functools.partial(field_kernel, (positions, rows, parts)),
        grid=(lengths,),
        out_shape=out_shape,
        in_specs=[
            pl.BlockSpec(memory_space=pltpu.SMEM),
            pl.BlockSpec(memory_space=pltpu.VMEM),
            pl.BlockSpec(memory_space=pltpu.VMEM),
            pl.BlockSpec((1,) + row_table.shape[1:], lambda l: (l, 0, 0, 0)),
            pl.BlockSpec((1,) + column_table.shape[1:], lambda l: (l, 0, 0)),
        ],
        out_specs=out_specs,
        scratch_shapes=[
            pltpu.VMEM((2 * BAND, positions * LANES), jnp.bfloat16),
            pltpu.VMEM((2 * BAND, positions * LANES), jnp.bfloat16),
            pltpu.VMEM((BANDS, 2 * rows, positions * LANES), jnp.float32),
            pltpu.VMEM((positions * rows, 2 * PUP), jnp.bfloat16),
        ],
        cost_estimate=pl.CostEstimate(
            flops=lengths * positions * (rows * 8 * PUP * PUP + rows * 8 * PUP * PIX + 10**8),
            bytes_accessed=8 * 2**20,
            transcendentals=0,
        ),
        compiler_params=pltpu.CompilerParams(vmem_limit_bytes=44 * 2**20),
    )(inverse, path, opening, row_table, column_table)


def mix_kernel(inverse_ref, weight_ref, sent_ref, image_ref, out_ref):
    f = pl.program_id(0)
    templates, rows = out_ref.shape[1], out_ref.shape[2]
    for start in range(0, rows, ROWS):
        lines = slice(start, start + ROWS)
        values = [sent_ref[l, lines] for l in range(sent_ref.shape[0])] + [
            (image_ref[l, lines] * inverse_ref[l, f]).astype(jnp.bfloat16)
            for l in range(image_ref.shape[0])
        ]
        mixed = jnp.dot(
            weight_ref[0], jnp.concatenate(values, axis=0), preferred_element_type=jnp.float32
        )
        for j in range(templates):
            out_ref[0, j, lines] = mixed[j * ROWS : (j + 1) * ROWS].astype(jnp.bfloat16)


def mix(weights, inverse, sent, images, rows):
    positions, templates, lengths = weights.shape
    spread = (
        weights[:, :, None, :, None].astype(jnp.float32)
        * np.eye(ROWS, dtype=np.float32)[None, None, :, None, :]
    ).reshape(positions, templates * ROWS, lengths * ROWS).astype(jnp.bfloat16)
    return pl.pallas_call(
        mix_kernel,
        grid=(positions,),
        out_shape=jax.ShapeDtypeStruct((positions, templates, rows, PIX), jnp.bfloat16),
        in_specs=[
            pl.BlockSpec(memory_space=pltpu.SMEM),
            pl.BlockSpec((1,) + spread.shape[1:], lambda f: (f, 0, 0)),
            pl.BlockSpec((sent.shape[0], rows, PIX), lambda f: (0, f, 0)),
            pl.BlockSpec((images.shape[0], rows, PIX), lambda f: (0, f, 0)),
        ],
        out_specs=pl.BlockSpec((1, templates, rows, PIX), lambda f: (f, 0, 0, 0)),
    )(inverse, spread, sent, images)


def table_kernel(scale_ref, y_ref, v_ref, u_ref, x_ref, row_ref, column_ref):
    scale = scale_ref[pl.program_id(0)]
    for start in range(0, PUP, ROWS):
        s, k = half_turn((y_ref[start : start + ROWS] * v_ref[...]) * scale)
        cosine, sine = 1.0 - s * s, s * k
        lower = slice(start, start + ROWS)
        upper = slice(PUP + start, PUP + start + ROWS)
        column_ref[0, lower, :PIX] = cosine.astype(jnp.bfloat16)
        column_ref[0, lower, PIX:] = (-sine).astype(jnp.bfloat16)
        column_ref[0, upper, :PIX] = sine.astype(jnp.bfloat16)
        column_ref[0, upper, PIX:] = cosine.astype(jnp.bfloat16)
    rows = u_ref.shape[0]
    imag = (lax.broadcasted_iota(jnp.int32, (ROWS, 2 * BAND), 1) // ROWS) % 2 == 1
    for band in range(BANDS):
        for start in range(0, rows, ROWS):
            s, k = half_turn((u_ref[start : start + ROWS] * x_ref[band]) * scale)
            cosine, sine = 1.0 - s * s, s * k
            row_ref[0, band, start : start + ROWS] = jnp.where(imag, sine, cosine).astype(
                jnp.bfloat16
            )
            row_ref[0, band, rows + start : rows + start + ROWS] = jnp.where(
                imag, cosine, -sine
            ).astype(jnp.bfloat16)


def tables(wave_lengths, first_row, rows):
    lengths = wave_lengths.shape[0]
    scale = (SAMPLING / (2.0 * PUP)) / wave_lengths
    y = 2 * np.concatenate([band_columns(band) for band in range(BANDS)]) - PUP + 1
    v = np.arange(PIX) - PIX // 2
    u = first_row + jnp.arange(rows, dtype=jnp.int32) - PIX // 2
    x = np.array(
        [[row + i for row in band_rows(band) for i in range(ROWS)] for band in range(BANDS)]
    )
    x = np.repeat(x.reshape(BANDS, UNITS, 1, ROWS), 2, axis=2).reshape(BANDS, 1, 2 * BAND)
    whole = lambda *shape: pl.BlockSpec(shape, lambda l: (0,) * len(shape))
    return pl.pallas_call(
        table_kernel,
        grid=(lengths,),
        out_shape=(
            jax.ShapeDtypeStruct((lengths, BANDS, 2 * rows, 2 * BAND), jnp.bfloat16),
            jax.ShapeDtypeStruct((lengths, 2 * PUP, 2 * PIX), jnp.bfloat16),
        ),
        in_specs=[
            pl.BlockSpec(memory_space=pltpu.SMEM),
            whole(PUP, 1),
            whole(1, PIX),
            whole(rows, 1),
            whole(BANDS, 1, 2 * BAND),
        ],
        out_specs=(
            pl.BlockSpec((1, BANDS, 2 * rows, 2 * BAND), lambda l: (l, 0, 0, 0)),
            pl.BlockSpec((1, 2 * PUP, 2 * PIX), lambda l: (l, 0, 0)),
        ),
        cost_estimate=pl.CostEstimate(
            flops=lengths * 30 * PUP * PIX, bytes_accessed=lengths * 4 * PUP * PIX * 2, transcendentals=0
        ),
        compiler_params=pltpu.CompilerParams(vmem_limit_bytes=24 * 2**20),
    )(
        scale,
        jnp.asarray(y[:, None].astype(np.float32)),
        jnp.asarray(v[None, :].astype(np.float32)),
        u.astype(jnp.float32)[:, None],
        jnp.asarray((2 * x - PUP + 1).astype(np.float32)),
    )


def shifts(x, waves):
    return [x] + [
        lax.ppermute(x, "wave", [(i, (i + s) % waves) for i in range(waves)])
        for s in range(1, waves)
    ]


def local(mode_basis, coef_table, table_index, wave_lengths, sed_table, template_ids):
    waves = lax.axis_size("wave")
    mine = lax.axis_index("wave")
    modes = mode_basis.shape[0]
    positions = table_index.shape[0]
    rows = PIX // waves
    count, half, slabs, pack, place = layout(waves, modes)
    sent_lengths = wave_lengths.shape[0] // 2
    kept = wave_lengths.shape[0] - sent_lengths

    table = jnp.asarray(pack)[mine]
    own = pack_rows(mode_basis, table, slabs)
    got = gather_rows(own, half, waves)

    own_tables = tables(wave_lengths[:sent_lengths], 0, PIX)
    every = jnp.zeros((waves * kept,), wave_lengths.dtype)
    for s, part in enumerate(shifts(wave_lengths[sent_lengths:], waves)):
        every = lax.dynamic_update_slice(every, part, (((mine - s) % waves) * kept,))
    all_tables = tables(every, mine * rows, rows)

    selector = (
        table_index[:, None] == jnp.arange(coef_table.shape[0], dtype=jnp.int32)[None, :]
    ).astype(jnp.bfloat16)
    coeffs = jnp.dot(selector, coef_table, preferred_element_type=jnp.float32)
    spread = (
        (coeffs[:, None, :, None] * np.eye(ROWS, dtype=np.float32)[None, :, None, :])
        .reshape(positions * ROWS, modes * ROWS)
        .astype(jnp.bfloat16)
    )
    one_hot = (
        template_ids[:, :, None]
        == jnp.arange(sed_table.shape[0], dtype=jnp.int32)[None, None, :]
    ).astype(jnp.float32)
    raw_weights = jnp.einsum("fjn,nl->fjl", one_hot, sed_table, precision=lax.Precision.HIGHEST)
    weights = (raw_weights / jnp.sum(raw_weights, axis=2, keepdims=True)).astype(jnp.bfloat16)
    order = weights.reshape(weights.shape[:2] + (waves, sent_lengths + kept))
    weights = jnp.concatenate(
        [
            order[..., :sent_lengths].reshape(weights.shape[:2] + (-1,)),
            order[..., sent_lengths:].reshape(weights.shape[:2] + (-1,)),
        ],
        axis=2,
    )

    path, opening = paths(
        own, got, spread, place, own_tables + all_tables, positions, (modes, waves, half, slabs)
    )
    spectra = fields(
        path, opening, 1.0 / wave_lengths[:sent_lengths], *own_tables, positions, waves
    )
    sent = lax.all_to_all(spectra, "wave", split_axis=0, concat_axis=0, tiled=True)
    sent = sent.reshape(waves * sent_lengths, positions * rows, PIX)

    images, sums = fields(path, opening, 1.0 / every, *all_tables, positions, 1)
    level = sum(shifts(jnp.sum(sums, axis=2), waves)) / (PIX * PIX)
    return mix(weights, 1.0 / (level + EPSILON), sent, images, rows)


def solution(mesh):
    return jax.shard_map(
        local,
        mesh=mesh,
        in_specs=(
            P(None, "wave", None),
            P(),
            P(("groups", "field")),
            P("wave"),
            P(),
            P(("groups", "field"), None),
        ),
        out_specs=P(("groups", "field"), None, "wave", None),
        check_vma=False,
    )
```

```python
import functools
import math

import jax
import jax.numpy as jnp
import numpy as np
from jax import lax
from jax.experimental import pallas as pl
from jax.experimental.pallas import tpu as pltpu
from jax.sharding import PartitionSpec as P

PUP = 512
PIX = 256
TWO_PI = 2.0 * math.pi
SAMPLING = 0.25
EPSILON = 1e-06
INNER = 61 * PUP // 100
BAND = 128
BANDS = PUP // BAND
ROWS = 16
LANES = 128
UNITS = BAND // ROWS
SHARES = 8

SIN_POLY = (4.4428679, -7.30744341, 3.59478797, -0.78437376)
COS_POLY = (1.4142135, -6.97885099, 5.73946117, -1.88356298, 0.31069817)


def half_turn(turns):
    magic = jnp.float32(12582912.0)
    r = turns - ((turns + magic) - magic)
    z = r * r
    s = jnp.float32(SIN_POLY[-1])
    for value in SIN_POLY[-2::-1]:
        s = s * z + value
    k = jnp.float32(COS_POLY[-1])
    for value in COS_POLY[-2::-1]:
        k = k * z + value
    return s * r, k


def band_rows(band):
    low, high = PUP // 2 - 64 * (band + 1), PUP // 2 + 64 * band
    return [low + ROWS * i for i in range(4)] + [high + ROWS * i for i in range(4)]


def band_columns(band):
    low, high = PUP // 2 - 64 * (band + 1), PUP // 2 + 64 * band
    sides = (high, low) if band % 2 == 0 else (low, high)
    return np.concatenate([side + np.arange(64) for side in sides])


def unit_open(row, band):
    a = 2 * (row + np.arange(ROWS)) - PUP + 1
    b = 2 * band_columns(band) - PUP + 1
    radius = a[:, None] ** 2 + b[None, :] ** 2
    return bool(np.any((radius <= PUP * PUP) & (radius >= INNER * INNER)))


CHUNKS = [
    (band, rows)
    for band in range(BANDS)
    for rows in range(BANDS)
    if any(unit_open(row, band) for row in band_rows(rows))
]


@functools.lru_cache(None)
def layout(waves, modes):
    per = PUP // waves
    lists = []
    for wave in range(waves):
        lists.append(
            [
                (band, row)
                for band in range(BANDS)
                for row in range(wave * per, (wave + 1) * per, ROWS)
                if unit_open(row, band)
            ]
        )
    count = max(len(one) for one in lists)
    half = -(-count * modes // (2 * SHARES))
    slabs = 2 * SHARES * half
    pack = np.zeros((waves, count, 3), np.int32)
    for wave, one in enumerate(lists):
        for i, (band, row) in enumerate(one):
            columns = band_columns(band)
            pack[wave, i] = (columns[0] // LANES * LANES, columns[64] // LANES * LANES, row - wave * per)
    place = np.zeros((len(CHUNKS) * UNITS, 4), np.int32)
    for c, (band, rows) in enumerate(CHUNKS):
        columns = band_columns(band)
        for j, row in enumerate(band_rows(rows)):
            wave = row // per
            slab = 0
            if (band, row) in lists[wave]:
                slab = wave * slabs + lists[wave].index((band, row)) * modes
            place[c * UNITS + j] = (slab, row, columns[0], columns[64] - 64)
    return count, half, slabs, pack, place


def pack_kernel(count, modes, half, where, table, lengths, basis, own, piece):
    left = lax.broadcasted_iota(jnp.int32, (ROWS, LANES), 1) < 64
    wave, share = where[0], where[1]

    def unit(i, carry):
        first = pl.multiple_of(table[wave * count + i, 0], LANES)
        second = pl.multiple_of(table[wave * count + i, 1], LANES)
        row = pl.multiple_of(table[wave * count + i, 2], ROWS)
        for k in range(modes):
            one = basis[k, pl.ds(row, ROWS), pl.ds(first, LANES)].astype(jnp.float32)
            two = basis[k, pl.ds(row, ROWS), pl.ds(second, LANES)].astype(jnp.float32)
            own[i * modes + k] = jnp.where(left, one, two).astype(own.dtype)
        return carry

    lax.fori_loop(0, count, unit, 0)
    for n in range(count * modes, own.shape[0]):
        own[n] = jnp.zeros((ROWS, LANES), own.dtype)
    piece[: 2 * half] = own[pl.ds(share * (2 * half), 2 * half)]
    line = lax.broadcasted_iota(jnp.int32, (ROWS, LANES), 0)
    slab = jnp.zeros((ROWS, LANES), jnp.float32)
    for i in range(lengths.shape[0]):
        rest = jnp.full((ROWS, LANES), lengths[i], jnp.float32)
        for limb in range(3):
            value = rest.astype(jnp.bfloat16).astype(jnp.float32)
            slab = jnp.where(line == 3 * i + limb, value, slab)
            rest = rest - value
    piece[2 * half] = slab.astype(piece.dtype)


def pack_rows(basis, wave_lengths, table, where, half, slabs):
    modes = basis.shape[0]
    waves, count, _ = table.shape
    smem = pl.BlockSpec(memory_space=pltpu.SMEM)
    vmem = pl.BlockSpec(memory_space=pltpu.VMEM)
    return pl.pallas_call(
        functools.partial(pack_kernel, count, modes, half),
        out_shape=(
            jax.ShapeDtypeStruct((slabs, ROWS, LANES), basis.dtype),
            jax.ShapeDtypeStruct((2 * half + 1, ROWS, LANES), basis.dtype),
        ),
        in_specs=[smem, smem, smem, vmem],
        out_specs=(vmem, vmem),
        compiler_params=pltpu.CompilerParams(vmem_limit_bytes=24 * 2**20),
    )(where, table.reshape(waves * count, 3), wave_lengths, basis)


def gather_rows(piece, half, waves):
    groups, fields = lax.axis_size("groups"), lax.axis_size("field")

    def swap(x, mask):
        pairs = [
            (g * fields + f, (g ^ (mask >> 2)) * fields + (f ^ (mask & 3)))
            for g in range(groups)
            for f in range(fields)
        ]
        return lax.ppermute(x, ("groups", "field"), pairs)

    parts = [
        lax.ppermute(piece, "wave", [(i, (i + s) % waves) for i in range(waves)])
        for s in range(1, waves)
    ]
    got = []
    for h, (one, two) in enumerate(((2, 4), (4, 2))):
        mine = jnp.concatenate([part[h * half : (h + 1) * half] for part in parts])
        both = jnp.concatenate([mine, swap(mine, one)])
        far = swap(both, two)
        got.append((h, both, (0, one)))
        got.append((h, far, (two, one | two)))
        got.append((h, swap(both, 1), (1, one | 1)))
        got.append((h, swap(far, 1), (two | 1, one | two | 1)))
    return parts, got


def spread_kernel(*refs):
    count = len(refs) // 2
    for small_ref, big_ref in zip(refs[:count], refs[count:]):
        _, many, wide = small_ref.shape
        tall, long = many * ROWS, wide * ROWS
        down = lax.broadcasted_iota(jnp.int32, (tall, many), 0) // ROWS
        down = (down == lax.broadcasted_iota(jnp.int32, (tall, many), 1)).astype(jnp.float32)
        along = lax.broadcasted_iota(jnp.int32, (wide, long), 1) // ROWS
        along = (along == lax.broadcasted_iota(jnp.int32, (wide, long), 0)).astype(jnp.float32)
        same = (lax.broadcasted_iota(jnp.int32, (tall, long), 0) % ROWS) == (
            lax.broadcasted_iota(jnp.int32, (tall, long), 1) % ROWS
        )
        down, along = down.astype(jnp.bfloat16), along.astype(jnp.bfloat16)
        for i in range(small_ref.shape[0]):
            half = jnp.dot(down, small_ref[i], preferred_element_type=jnp.float32)
            whole = jnp.dot(half.astype(jnp.bfloat16), along, preferred_element_type=jnp.float32)
            big_ref[i] = jnp.where(same, whole, 0.0).astype(jnp.bfloat16)


def spreads(*matrices):
    return pl.pallas_call(
        spread_kernel,
        out_shape=tuple(
            jax.ShapeDtypeStruct((m.shape[0], m.shape[1] * ROWS, m.shape[2] * ROWS), jnp.bfloat16)
            for m in matrices
        ),
    )(*matrices)


def form_paths(sizes, where, place, parts, spread, path, opening, basis, sems):
    positions, modes, waves, half, slabs, keys = sizes
    wave, share = where[0], where[1]
    copies = [pltpu.make_async_copy(parts[0], basis.at[pl.ds(wave * slabs, slabs)], sems.at[0])]
    n = 1
    for (h, masks), part in zip(keys, parts[1:]):
        for m, mask in enumerate(masks):
            for s in range(1, waves):
                source = lax.rem(wave + (waves - s), waves)
                start = source * slabs + (share ^ mask) * (2 * half) + h * half
                copies.append(
                    pltpu.make_async_copy(
                        part.at[pl.ds((m * (waves - 1) + s - 1) * half, half)],
                        basis.at[pl.ds(start, half)],
                        sems.at[n],
                    )
                )
                n += 1
    for copy in copies:
        copy.start()
    for copy in copies:
        copy.wait()

    lane = lax.broadcasted_iota(jnp.int32, (ROWS, LANES), 1)
    line = lax.broadcasted_iota(jnp.int32, (ROWS, LANES), 0)

    def chunk(c, carry):
        values = jnp.concatenate(
            [
                basis[pl.ds(place[c * UNITS + j, 0], modes)].reshape(modes * ROWS, LANES)
                for j in range(UNITS)
            ],
            axis=1,
        )
        found = jnp.dot(spread[0], values, preferred_element_type=jnp.float32)
        for j in range(UNITS):
            u = c * UNITS + j
            a = 2 * (line + place[u, 1]) - (PUP - 1)
            b = 2 * (lane + jnp.where(lane < 64, place[u, 2], place[u, 3])) - (PUP - 1)
            radius = a * a + b * b
            inside = (radius <= PUP * PUP) & (radius >= INNER * INNER)
            opening[u] = jnp.where(inside, 1.0, 0.0)
            for f in range(positions):
                path[u, f * ROWS : (f + 1) * ROWS] = jnp.where(
                    inside, found[f * ROWS : (f + 1) * ROWS, j * LANES : (j + 1) * LANES], 0.0
                )
        return carry

    lax.fori_loop(0, len(CHUNKS), chunk, 0)


def transform(positions, rows, inverse, path, opening, row_ref, column_ref, scratch):
    pupils, total, first = scratch[:2], scratch[2], scratch[3]
    batch = max(1, positions // 2)
    width = 2 * positions * LANES // UNITS

    def finish(band, columns, value):
        for f in range(columns.start // LANES, columns.stop // LANES):
            lanes = slice(f * LANES - columns.start, (f + 1) * LANES - columns.start)
            for part in range(2):
                first[
                    f * rows : (f + 1) * rows,
                    part * PUP + band * LANES : part * PUP + (band + 1) * LANES,
                ] = value[part * rows : (part + 1) * rows, lanes].astype(jnp.bfloat16)

    def product(c, columns):
        band, rows_band = CHUNKS[c]
        value = jnp.dot(
            row_ref[0, rows_band], pupils[c % 2][:, columns], preferred_element_type=jnp.float32
        )
        if c > 0 and CHUNKS[c - 1][0] == band:
            value = value + total[:, columns]
        if c + 1 < len(CHUNKS) and CHUNKS[c + 1][0] == band:
            total[:, columns] = value
        else:
            finish(band, columns, value)

    for c, (band, rows_band) in enumerate(CHUNKS):
        pupil = pupils[c % 2]
        for j, row in enumerate(band_rows(rows_band)):
            real_lines = slice(2 * ROWS * j, 2 * ROWS * j + ROWS)
            imag_lines = slice(2 * ROWS * j + ROWS, 2 * ROWS * (j + 1))
            if unit_open(row, band):
                u = c * UNITS + j
                inside = opening[u]
                for f0 in range(0, positions, batch):
                    s, k = half_turn(path[u, f0 * ROWS : (f0 + batch) * ROWS] * inverse)
                    sine = s * k
                    square = s * s
                    for f in range(f0, f0 + batch):
                        columns = slice(f * LANES, (f + 1) * LANES)
                        lines = slice((f - f0) * ROWS, (f - f0 + 1) * ROWS)
                        pupil[real_lines, columns] = (inside - square[lines]).astype(jnp.bfloat16)
                        pupil[imag_lines, columns] = sine[lines].astype(jnp.bfloat16)
            else:
                empty = jnp.zeros((ROWS, positions * LANES), jnp.bfloat16)
                pupil[real_lines] = empty
                pupil[imag_lines] = empty
            if c > 0 and j % 2 == 1:
                product(c - 1, slice(j // 2 * width, (j // 2 + 1) * width))
    for n in range(positions * LANES // width):
        product(len(CHUNKS) - 1, slice(n * width, (n + 1) * width))


def whole_kernel(sizes, tokens, inverse_ref, place, where, *refs):
    positions, modes, waves, half, slabs, keys = sizes
    parts, refs = refs[: 1 + len(keys)], refs[1 + len(keys) :]
    spread, row_ref, column_ref = refs[:3]
    image_ref, path, opening = refs[3 + tokens : 6 + tokens]
    basis, sems = refs[6 + tokens : 8 + tokens]
    scratch = refs[8 + tokens :]

    @pl.when(pl.program_id(0) == 0)
    def _():
        form_paths(sizes, where, place, parts, spread, path, opening, basis, sems)

    inverse = inverse_ref[pl.program_id(0)]
    rows = PIX
    transform(positions, rows, inverse, path, opening, row_ref, column_ref, scratch)
    first = scratch[3]
    share = rows // waves
    for f in range(positions):
        lines = first[f * rows : (f + 1) * rows]
        real = jnp.dot(lines, column_ref[0, :, :PIX], preferred_element_type=jnp.float32)
        imag = jnp.dot(lines, column_ref[0, :, PIX:], preferred_element_type=jnp.float32)
        intensity = real * real + imag * imag
        level = jnp.sum(
            jnp.sum(intensity, axis=0, keepdims=True), axis=1, keepdims=True
        ) / (rows * PIX)
        spectra = (intensity / (level + EPSILON)).astype(jnp.bfloat16)
        for part in range(waves):
            image_ref[part, 0, f * share : (f + 1) * share] = spectra[
                part * share : (part + 1) * share
            ]


def rows_kernel(positions, rows, inverse_ref, path, opening, row_ref, column_ref, *refs):
    image_ref, sum_ref = refs[:2]
    scratch = refs[2:]
    inverse = inverse_ref[pl.program_id(0)]
    transform(positions, rows, inverse, path, opening, row_ref, column_ref, scratch)
    first = scratch[3]
    real = jnp.dot(first[...], column_ref[0, :, :PIX], preferred_element_type=jnp.float32)
    imag = jnp.dot(first[...], column_ref[0, :, PIX:], preferred_element_type=jnp.float32)
    intensity = real * real + imag * imag
    image_ref[0] = intensity
    sum_ref[0] = jnp.sum(intensity.reshape(positions, rows, PIX), axis=1)


def transform_scratch(positions, rows):
    return [
        pltpu.VMEM((2 * BAND, positions * LANES), jnp.bfloat16),
        pltpu.VMEM((2 * BAND, positions * LANES), jnp.bfloat16),
        pltpu.VMEM((2 * rows, positions * LANES), jnp.float32),
        pltpu.VMEM((positions * rows, 2 * PUP), jnp.bfloat16),
    ]


def transform_cost(lengths, positions, rows):
    return pl.CostEstimate(
        flops=lengths * positions * (rows * 8 * PUP * PUP + rows * 8 * PUP * PIX + 10**8),
        bytes_accessed=8 * 2**20,
        transcendentals=0,
    )


SMEM = pl.BlockSpec(memory_space=pltpu.SMEM)
VMEM = pl.BlockSpec(memory_space=pltpu.VMEM)


def table_specs(row_table, column_table):
    return [
        pl.BlockSpec((1,) + row_table.shape[1:], lambda l: (l, 0, 0, 0)),
        pl.BlockSpec((1,) + column_table.shape[1:], lambda l: (l, 0, 0)),
    ]


def whole_fields(own, got, spread, place, where, inverse, row_table, column_table, tokens, sizes):
    positions, modes, waves, half, slabs = sizes
    keys = tuple((h, masks) for h, _, masks in got)
    arrays = [array for _, array, _ in got]
    lengths = row_table.shape[0]
    units = place.shape[0]
    share = positions * PIX // waves
    any_memory = pl.BlockSpec(memory_space=pl.ANY)
    return pl.pallas_call(
        functools.partial(
            whole_kernel, (positions, modes, waves, half, slabs, keys), len(tokens)
        ),
        grid=(lengths,),
        out_shape=(
            jax.ShapeDtypeStruct((waves, lengths, share, PIX), jnp.bfloat16),
            jax.ShapeDtypeStruct((units, positions * ROWS, LANES), jnp.float32),
            jax.ShapeDtypeStruct((units, ROWS, LANES), jnp.float32),
        ),
        in_specs=[SMEM, SMEM, SMEM]
        + [any_memory] * (1 + len(keys))
        + [VMEM]
        + table_specs(row_table, column_table)
        + [VMEM] * len(tokens),
        out_specs=(pl.BlockSpec((waves, 1, share, PIX), lambda l: (0, l, 0, 0)), VMEM, VMEM),
        scratch_shapes=[
            pltpu.VMEM((waves * slabs, ROWS, LANES), jnp.bfloat16),
            pltpu.SemaphoreType.DMA((1 + sum(len(masks) for _, masks in keys) * (waves - 1),)),
        ]
        + transform_scratch(positions, PIX),
        cost_estimate=transform_cost(lengths, positions, PIX),
        compiler_params=pltpu.CompilerParams(vmem_limit_bytes=48 * 2**20),
    )(inverse, place, where, own, *arrays, spread, row_table, column_table, *tokens)


def row_fields(path, opening, inverse, row_table, column_table, positions):
    lengths = row_table.shape[0]
    rows = row_table.shape[2] // 2
    return pl.pallas_call(
        functools.partial(rows_kernel, positions, rows),
        grid=(lengths,),
        out_shape=(
            jax.ShapeDtypeStruct((lengths, positions * rows, PIX), jnp.float32),
            jax.ShapeDtypeStruct((lengths, positions, PIX), jnp.float32),
        ),
        in_specs=[SMEM, VMEM, VMEM] + table_specs(row_table, column_table),
        out_specs=(
            pl.BlockSpec((1, positions * rows, PIX), lambda l: (l, 0, 0)),
            pl.BlockSpec((1, positions, PIX), lambda l: (l, 0, 0)),
        ),
        scratch_shapes=transform_scratch(positions, rows),
        cost_estimate=transform_cost(lengths, positions, rows),
        compiler_params=pltpu.CompilerParams(vmem_limit_bytes=30 * 2**20),
    )(inverse, path, opening, row_table, column_table)


def mix_kernel(inverse_ref, weight_ref, sent_ref, image_ref, out_ref):
    f = pl.program_id(0)
    templates, rows = out_ref.shape[1], out_ref.shape[2]
    blocks = []
    for start in range(0, rows, ROWS):
        lines = slice(start, start + ROWS)
        blocks.append(
            jnp.concatenate(
                [sent_ref[l, lines] for l in range(sent_ref.shape[0])]
                + [
                    (image_ref[l, lines] * inverse_ref[l, f]).astype(jnp.bfloat16)
                    for l in range(image_ref.shape[0])
                ],
                axis=0,
            )
        )
    mixed = jnp.dot(
        weight_ref[0], jnp.concatenate(blocks, axis=1), preferred_element_type=jnp.float32
    ).astype(jnp.bfloat16)
    for n in range(len(blocks)):
        for j in range(templates):
            out_ref[0, j, n * ROWS : (n + 1) * ROWS] = mixed[
                j * ROWS : (j + 1) * ROWS, n * PIX : (n + 1) * PIX
            ]


def mix(spread, inverse, sent, images, templates, rows):
    positions = spread.shape[0]
    return pl.pallas_call(
        mix_kernel,
        grid=(positions,),
        out_shape=jax.ShapeDtypeStruct((positions, templates, rows, PIX), jnp.bfloat16),
        in_specs=[
            SMEM,
            pl.BlockSpec((1,) + spread.shape[1:], lambda f: (f, 0, 0)),
            pl.BlockSpec((sent.shape[0], rows, PIX), lambda f: (0, f, 0)),
            pl.BlockSpec((images.shape[0], rows, PIX), lambda f: (0, f, 0)),
        ],
        out_specs=pl.BlockSpec((1, templates, rows, PIX), lambda f: (f, 0, 0, 0)),
    )(inverse, spread, sent, images)


def table_kernel(scale_ref, y_ref, v_ref, u_ref, x_ref, row_ref, column_ref, token_ref):
    scale = scale_ref[pl.program_id(0)]
    token_ref[...] = jnp.zeros_like(token_ref)
    for start in range(0, PUP, ROWS):
        s, k = half_turn((y_ref[start : start + ROWS] * v_ref[...]) * scale)
        cosine, sine = 1.0 - s * s, s * k
        lower = slice(start, start + ROWS)
        upper = slice(PUP + start, PUP + start + ROWS)
        column_ref[0, lower, :PIX] = cosine.astype(jnp.bfloat16)
        column_ref[0, lower, PIX:] = (-sine).astype(jnp.bfloat16)
        column_ref[0, upper, :PIX] = sine.astype(jnp.bfloat16)
        column_ref[0, upper, PIX:] = cosine.astype(jnp.bfloat16)
    rows = u_ref.shape[0]
    imag = (lax.broadcasted_iota(jnp.int32, (ROWS, 2 * BAND), 1) // ROWS) % 2 == 1
    for band in range(BANDS):
        for start in range(0, rows, ROWS):
            s, k = half_turn((u_ref[start : start + ROWS] * x_ref[band]) * scale)
            cosine, sine = 1.0 - s * s, s * k
            row_ref[0, band, start : start + ROWS] = jnp.where(imag, sine, cosine).astype(
                jnp.bfloat16
            )
            row_ref[0, band, rows + start : rows + start + ROWS] = jnp.where(
                imag, cosine, -sine
            ).astype(jnp.bfloat16)


def tables(wave_lengths, first_row, rows):
    lengths = wave_lengths.shape[0]
    scale = (SAMPLING / (2.0 * PUP)) / wave_lengths
    y = 2 * np.concatenate([band_columns(band) for band in range(BANDS)]) - PUP + 1
    v = np.arange(PIX) - PIX // 2
    u = first_row + jnp.arange(rows, dtype=jnp.int32) - PIX // 2
    x = np.array(
        [[row + i for row in band_rows(band) for i in range(ROWS)] for band in range(BANDS)]
    )
    x = np.repeat(x.reshape(BANDS, UNITS, 1, ROWS), 2, axis=2).reshape(BANDS, 1, 2 * BAND)
    whole = lambda *shape: pl.BlockSpec(shape, lambda l: (0,) * len(shape))
    return pl.pallas_call(
        table_kernel,
        grid=(lengths,),
        out_shape=(
            jax.ShapeDtypeStruct((lengths, BANDS, 2 * rows, 2 * BAND), jnp.bfloat16),
            jax.ShapeDtypeStruct((lengths, 2 * PUP, 2 * PIX), jnp.bfloat16),
            jax.ShapeDtypeStruct((8, LANES), jnp.float32),
        ),
        in_specs=[
            SMEM,
            whole(PUP, 1),
            whole(1, PIX),
            whole(rows, 1),
            whole(BANDS, 1, 2 * BAND),
        ],
        out_specs=(
            pl.BlockSpec((1, BANDS, 2 * rows, 2 * BAND), lambda l: (l, 0, 0, 0)),
            pl.BlockSpec((1, 2 * PUP, 2 * PIX), lambda l: (l, 0, 0)),
            whole(8, LANES),
        ),
        cost_estimate=pl.CostEstimate(
            flops=lengths * 30 * PUP * PIX, bytes_accessed=lengths * 4 * PUP * PIX * 2, transcendentals=0
        ),
        compiler_params=pltpu.CompilerParams(vmem_limit_bytes=24 * 2**20),
    )(
        scale,
        jnp.asarray(y[:, None].astype(np.float32)),
        jnp.asarray(v[None, :].astype(np.float32)),
        u.astype(jnp.float32)[:, None],
        jnp.asarray((2 * x - PUP + 1).astype(np.float32)),
    )


def add_over_wave(x, waves):
    step = 1
    while step < waves:
        x = x + lax.ppermute(x, "wave", [(i, i ^ step) for i in range(waves)])
        step *= 2
    return x


def local(mode_basis, coef_table, table_index, wave_lengths, sed_table, template_ids):
    waves = lax.axis_size("wave")
    mine = lax.axis_index("wave")
    modes = mode_basis.shape[0]
    positions = table_index.shape[0]
    rows = PIX // waves
    count, half, slabs, pack, place = layout(waves, modes)
    lengths = wave_lengths.shape[0]
    sent_lengths = lengths // 2

    share = (lax.axis_index("groups") % 2) * 4 + lax.axis_index("field") % 4
    where = jnp.stack([mine, share]).astype(jnp.int32)
    own, piece = pack_rows(mode_basis, wave_lengths, pack, where, half, slabs)
    parts, got = gather_rows(piece, half, waves)

    limbs = jnp.stack([part[2 * half, : 3 * lengths, 0] for part in parts])
    others = jnp.sum(limbs.astype(jnp.float32).reshape(waves - 1, lengths, 3), axis=2)
    known = jnp.concatenate([wave_lengths[None], others])
    order = (mine - jnp.arange(waves)) % waves
    every = jnp.sum(
        jnp.where((order[:, None] == jnp.arange(waves)[None, :])[:, :, None], known[None], 0.0),
        axis=1,
    )[:, sent_lengths:].reshape(-1)
    own_row, own_column, own_token = tables(wave_lengths[:sent_lengths], 0, PIX)
    all_row, all_column, all_token = tables(every, mine * rows, rows)

    selector = (
        table_index[:, None] == jnp.arange(coef_table.shape[0], dtype=jnp.int32)[None, :]
    ).astype(jnp.bfloat16)
    coeffs = jnp.dot(selector, coef_table, preferred_element_type=jnp.float32)
    one_hot = (
        template_ids[:, :, None]
        == jnp.arange(sed_table.shape[0], dtype=jnp.int32)[None, None, :]
    ).astype(jnp.float32)
    raw_weights = jnp.einsum("fjn,nl->fjl", one_hot, sed_table, precision=lax.Precision.HIGHEST)
    weights = (raw_weights / jnp.sum(raw_weights, axis=2, keepdims=True)).astype(jnp.bfloat16)
    templates = weights.shape[1]
    split = weights.reshape(positions, templates, waves, lengths)
    weights = jnp.concatenate(
        [
            split[..., :sent_lengths].reshape(positions, templates, -1),
            split[..., sent_lengths:].reshape(positions, templates, -1),
        ],
        axis=2,
    )
    path_spread, mix_spread = spreads(coeffs.astype(jnp.bfloat16)[None], weights)

    spectra, path, opening = whole_fields(
        own,
        got,
        path_spread,
        place,
        where,
        1.0 / wave_lengths[:sent_lengths],
        own_row,
        own_column,
        (all_token,),
        (positions, modes, waves, half, slabs),
    )
    sent = lax.all_to_all(spectra, "wave", split_axis=0, concat_axis=0, tiled=True)
    sent = sent.reshape(waves * sent_lengths, positions * rows, PIX)

    images, sums = row_fields(path, opening, 1.0 / every, all_row, all_column, positions)
    level = add_over_wave(jnp.sum(sums, axis=2), waves) / (PIX * PIX)
    return mix(mix_spread, 1.0 / (level + EPSILON), sent, images, templates, rows)


def solution(mesh):
    return jax.shard_map(
        local,
        mesh=mesh,
        in_specs=(
            P(None, "wave", None),
            P(),
            P(("groups", "field")),
            P("wave"),
            P(),
            P(("groups", "field"), None),
        ),
        out_specs=P(("groups", "field"), None, "wave", None),
        check_vma=False,
    )
```

```python
import functools
import math

import jax
import jax.numpy as jnp
import numpy as np
from jax import lax
from jax.experimental import pallas as pl
from jax.experimental.pallas import tpu as pltpu
from jax.sharding import PartitionSpec as P

PUP = 512
PIX = 256
TWO_PI = 2.0 * math.pi
SAMPLING = 0.25
EPSILON = 1e-06
INNER = 61 * PUP // 100
BAND = 128
BANDS = PUP // BAND
ROWS = 16
LANES = 128
UNITS = BAND // ROWS
VMEM_BYTES = 60 * 2**20
SHARES = 8

SMEM = pl.BlockSpec(memory_space=pltpu.SMEM)
VMEM = pl.BlockSpec(memory_space=pltpu.VMEM)
LENGTH = pl.BlockSpec((1, 8, LANES), lambda l: (l, 0, 0))

SIN_POLY = (4.4428679, -7.30744341, 3.59478797, -0.78437376)
COS_POLY = (1.4142135, -6.97885099, 5.73946117, -1.88356298, 0.31069817)


def half_turn(turns):
    magic = jnp.float32(12582912.0)
    r = turns - ((turns + magic) - magic)
    z = r * r
    s = jnp.float32(SIN_POLY[-1])
    for value in SIN_POLY[-2::-1]:
        s = s * z + value
    k = jnp.float32(COS_POLY[-1])
    for value in COS_POLY[-2::-1]:
        k = k * z + value
    return s * r, k


def band_rows(band):
    low, high = PUP // 2 - 64 * (band + 1), PUP // 2 + 64 * band
    return [low + ROWS * i for i in range(4)] + [high + ROWS * i for i in range(4)]


def band_columns(band):
    low, high = PUP // 2 - 64 * (band + 1), PUP // 2 + 64 * band
    sides = (high, low) if band % 2 == 0 else (low, high)
    return np.concatenate([side + np.arange(64) for side in sides])


def unit_open(row, band):
    a = 2 * (row + np.arange(ROWS)) - PUP + 1
    b = 2 * band_columns(band) - PUP + 1
    radius = a[:, None] ** 2 + b[None, :] ** 2
    return bool(np.any((radius <= PUP * PUP) & (radius >= INNER * INNER)))


CHUNKS = [
    (band, rows)
    for band in range(BANDS)
    for rows in range(BANDS)
    if any(unit_open(row, band) for row in band_rows(rows))
]


@functools.lru_cache(None)
def layout(waves, modes):
    per = PUP // waves
    lists = []
    for wave in range(waves):
        lists.append(
            [
                (band, row)
                for band in range(BANDS)
                for row in range(wave * per, (wave + 1) * per, ROWS)
                if unit_open(row, band)
            ]
        )
    count = max(len(one) for one in lists)
    half = -(-count * modes // (2 * SHARES))
    slabs = 2 * SHARES * half
    pack = np.zeros((waves, count, 3), np.int32)
    for wave, one in enumerate(lists):
        for i, (band, row) in enumerate(one):
            columns = band_columns(band)
            pack[wave, i] = (columns[0] // LANES * LANES, columns[64] // LANES * LANES, row - wave * per)
    place = np.zeros((len(CHUNKS) * UNITS, 4), np.int32)
    for c, (band, rows) in enumerate(CHUNKS):
        columns = band_columns(band)
        for j, row in enumerate(band_rows(rows)):
            wave = row // per
            slab = 0
            if (band, row) in lists[wave]:
                slab = wave * slabs + lists[wave].index((band, row)) * modes
            place[c * UNITS + j] = (slab, row, columns[0], columns[64] - 64)
    return count, half, slabs, pack, place


def pack_kernel(count, modes, half, where, table, lengths, basis, own, piece):
    left = lax.broadcasted_iota(jnp.int32, (ROWS, LANES), 1) < 64
    wave, share = where[0], where[1]

    def unit(i, carry):
        first = pl.multiple_of(table[wave * count + i, 0], LANES)
        second = pl.multiple_of(table[wave * count + i, 1], LANES)
        row = pl.multiple_of(table[wave * count + i, 2], ROWS)
        for k in range(modes):
            one = basis[k, pl.ds(row, ROWS), pl.ds(first, LANES)].astype(jnp.float32)
            two = basis[k, pl.ds(row, ROWS), pl.ds(second, LANES)].astype(jnp.float32)
            own[i * modes + k] = jnp.where(left, one, two).astype(own.dtype)
        return carry

    lax.fori_loop(0, count, unit, 0)
    for n in range(count * modes, own.shape[0]):
        own[n] = jnp.zeros((ROWS, LANES), own.dtype)
    piece[: 2 * half] = own[pl.ds(share * (2 * half), 2 * half)]
    line = lax.broadcasted_iota(jnp.int32, (ROWS, LANES), 0)
    slab = jnp.zeros((ROWS, LANES), jnp.float32)
    for i in range(lengths.shape[0]):
        rest = jnp.full((ROWS, LANES), lengths[i], jnp.float32)
        for limb in range(3):
            value = rest.astype(jnp.bfloat16).astype(jnp.float32)
            slab = jnp.where(line == 3 * i + limb, value, slab)
            rest = rest - value
    piece[2 * half] = slab.astype(piece.dtype)


def pack_rows(basis, wave_lengths, table, where, half, slabs):
    modes = basis.shape[0]
    waves, count, _ = table.shape
    smem = pl.BlockSpec(memory_space=pltpu.SMEM)
    vmem = pl.BlockSpec(memory_space=pltpu.VMEM)
    return pl.pallas_call(
        functools.partial(pack_kernel, count, modes, half),
        out_shape=(
            jax.ShapeDtypeStruct((slabs, ROWS, LANES), basis.dtype),
            jax.ShapeDtypeStruct((2 * half + 1, ROWS, LANES), basis.dtype),
        ),
        in_specs=[smem, smem, smem, vmem],
        out_specs=(vmem, vmem),
        compiler_params=pltpu.CompilerParams(vmem_limit_bytes=VMEM_BYTES),
    )(where, table.reshape(waves * count, 3), wave_lengths, basis)


def split_kernel(half, sent, where, own_lengths, *refs):
    parts, (low_ref, high_ref, length_ref) = refs[:-3], refs[-3:]
    wave, waves = where[0], len(parts) + 1
    kept = own_lengths.shape[0] - sent
    for s in range(waves):
        for i in range(kept):
            if s == 0:
                value = jnp.full((8, LANES), own_lengths[sent + i], jnp.float32)
            else:
                slab = parts[s - 1][2 * half].astype(jnp.float32)
                line = 3 * (sent + i)
                value = (slab[line : line + 1] + slab[line + 1 : line + 2]) + slab[
                    line + 2 : line + 3
                ]
                value = jnp.broadcast_to(value, (8, LANES))
            length_ref[lax.rem(wave + (waves - s), waves) * kept + i] = value
    for s, part in enumerate(parts):
        low_ref[s * half : (s + 1) * half] = part[:half]
        high_ref[s * half : (s + 1) * half] = part[half : 2 * half]


def split_parts(parts, where, wave_lengths, half, sent):
    count = (len(parts) + 1) * (wave_lengths.shape[0] - sent)
    slabs = jax.ShapeDtypeStruct((len(parts) * half, ROWS, LANES), parts[0].dtype)
    return pl.pallas_call(
        functools.partial(split_kernel, half, sent),
        out_shape=(slabs, slabs, jax.ShapeDtypeStruct((count, 8, LANES), jnp.float32)),
        in_specs=[SMEM, SMEM] + [VMEM] * len(parts),
        out_specs=(VMEM,) * 3,
        compiler_params=pltpu.CompilerParams(vmem_limit_bytes=VMEM_BYTES),
    )(where, wave_lengths, *parts)


def join_kernel(one_ref, two_ref, token_ref, out_ref):
    count = one_ref.shape[0]
    out_ref[:count] = one_ref[...]
    out_ref[count:] = two_ref[...]


def join(one, two, token):
    return pl.pallas_call(
        join_kernel,
        out_shape=jax.ShapeDtypeStruct((2 * one.shape[0],) + one.shape[1:], one.dtype),
        in_specs=[VMEM] * 3,
        out_specs=VMEM,
        compiler_params=pltpu.CompilerParams(vmem_limit_bytes=VMEM_BYTES),
    )(one, two, token)


def along_wave(piece, waves):
    return [
        lax.ppermute(piece, "wave", [(i, (i + s) % waves) for i in range(waves)])
        for s in range(1, waves)
    ]


def gather_rows(halves, token):
    groups, fields = lax.axis_size("groups"), lax.axis_size("field")

    def swap(x, mask):
        pairs = [
            (g * fields + f, (g ^ (mask >> 2)) * fields + (f ^ (mask & 3)))
            for g in range(groups)
            for f in range(fields)
        ]
        return lax.ppermute(x, ("groups", "field"), pairs)

    got = []
    for h, (one, two) in enumerate(((2, 4), (4, 2))):
        mine = halves[h]
        both = join(mine, swap(mine, one), token)
        far = swap(both, two)
        got.append((h, both, (0, one)))
        got.append((h, far, (two, one | two)))
        got.append((h, swap(both, 1), (1, one | 1)))
        got.append((h, swap(far, 1), (two | 1, one | two | 1)))
    return got


def spread_kernel(*refs):
    count = len(refs) // 2
    for small_ref, big_ref in zip(refs[:count], refs[count:]):
        _, many, wide = small_ref.shape
        tall, long = many * ROWS, wide * ROWS
        down = lax.broadcasted_iota(jnp.int32, (tall, many), 0) // ROWS
        down = (down == lax.broadcasted_iota(jnp.int32, (tall, many), 1)).astype(jnp.float32)
        along = lax.broadcasted_iota(jnp.int32, (wide, long), 1) // ROWS
        along = (along == lax.broadcasted_iota(jnp.int32, (wide, long), 0)).astype(jnp.float32)
        same = (lax.broadcasted_iota(jnp.int32, (tall, long), 0) % ROWS) == (
            lax.broadcasted_iota(jnp.int32, (tall, long), 1) % ROWS
        )
        down, along = down.astype(jnp.bfloat16), along.astype(jnp.bfloat16)
        for i in range(small_ref.shape[0]):
            half = jnp.dot(down, small_ref[i], preferred_element_type=jnp.float32)
            whole = jnp.dot(half.astype(jnp.bfloat16), along, preferred_element_type=jnp.float32)
            big_ref[i] = jnp.where(same, whole, 0.0).astype(jnp.bfloat16)


def spreads(*matrices):
    return pl.pallas_call(
        spread_kernel,
        out_shape=tuple(
            jax.ShapeDtypeStruct((m.shape[0], m.shape[1] * ROWS, m.shape[2] * ROWS), jnp.bfloat16)
            for m in matrices
        ),
        compiler_params=pltpu.CompilerParams(vmem_limit_bytes=VMEM_BYTES),
    )(*matrices)


def form_paths(sizes, where, place, parts, spread, path, opening, basis, sems):
    positions, modes, waves, half, slabs, keys = sizes
    wave, share = where[0], where[1]
    copies = [pltpu.make_async_copy(parts[0], basis.at[pl.ds(wave * slabs, slabs)], sems.at[0])]
    n = 1
    for (h, masks), part in zip(keys, parts[1:]):
        for m, mask in enumerate(masks):
            for s in range(1, waves):
                source = lax.rem(wave + (waves - s), waves)
                start = source * slabs + (share ^ mask) * (2 * half) + h * half
                copies.append(
                    pltpu.make_async_copy(
                        part.at[pl.ds((m * (waves - 1) + s - 1) * half, half)],
                        basis.at[pl.ds(start, half)],
                        sems.at[n],
                    )
                )
                n += 1
    for copy in copies:
        copy.start()
    for copy in copies:
        copy.wait()

    lane = lax.broadcasted_iota(jnp.int32, (ROWS, LANES), 1)
    line = lax.broadcasted_iota(jnp.int32, (ROWS, LANES), 0)

    def chunk(c, carry):
        values = jnp.concatenate(
            [
                basis[pl.ds(place[c * UNITS + j, 0], modes)].reshape(modes * ROWS, LANES)
                for j in range(UNITS)
            ],
            axis=1,
        )
        found = jnp.dot(spread[0], values, preferred_element_type=jnp.float32)
        for j in range(UNITS):
            u = c * UNITS + j
            a = 2 * (line + place[u, 1]) - (PUP - 1)
            b = 2 * (lane + jnp.where(lane < 64, place[u, 2], place[u, 3])) - (PUP - 1)
            radius = a * a + b * b
            inside = (radius <= PUP * PUP) & (radius >= INNER * INNER)
            opening[u] = jnp.where(inside, 1.0, 0.0)
            for f in range(positions):
                path[u, f * ROWS : (f + 1) * ROWS] = jnp.where(
                    inside, found[f * ROWS : (f + 1) * ROWS, j * LANES : (j + 1) * LANES], 0.0
                )
        return carry

    lax.fori_loop(0, len(CHUNKS), chunk, 0)


def transform(positions, rows, inverse, path, opening, row_ref, column_ref, scratch):
    pupils, total, first = scratch[:2], scratch[2], scratch[3]
    batch = max(1, positions // 2)
    width = 2 * positions * LANES // UNITS

    def finish(band, columns, value):
        for f in range(columns.start // LANES, columns.stop // LANES):
            lanes = slice(f * LANES - columns.start, (f + 1) * LANES - columns.start)
            for part in range(2):
                first[
                    f * rows : (f + 1) * rows,
                    part * PUP + band * LANES : part * PUP + (band + 1) * LANES,
                ] = value[part * rows : (part + 1) * rows, lanes].astype(jnp.bfloat16)

    def product(c, columns):
        band, rows_band = CHUNKS[c]
        value = jnp.dot(
            row_ref[0, rows_band], pupils[c % 2][:, columns], preferred_element_type=jnp.float32
        )
        if c > 0 and CHUNKS[c - 1][0] == band:
            value = value + total[:, columns]
        if c + 1 < len(CHUNKS) and CHUNKS[c + 1][0] == band:
            total[:, columns] = value
        else:
            finish(band, columns, value)

    for c, (band, rows_band) in enumerate(CHUNKS):
        pupil = pupils[c % 2]
        for j, row in enumerate(band_rows(rows_band)):
            real_lines = slice(2 * ROWS * j, 2 * ROWS * j + ROWS)
            imag_lines = slice(2 * ROWS * j + ROWS, 2 * ROWS * (j + 1))
            if unit_open(row, band):
                u = c * UNITS + j
                inside = opening[u]
                for f0 in range(0, positions, batch):
                    s, k = half_turn(path[u, f0 * ROWS : (f0 + batch) * ROWS] * inverse)
                    sine = s * k
                    square = s * s
                    for f in range(f0, f0 + batch):
                        columns = slice(f * LANES, (f + 1) * LANES)
                        lines = slice((f - f0) * ROWS, (f - f0 + 1) * ROWS)
                        pupil[real_lines, columns] = (inside - square[lines]).astype(jnp.bfloat16)
                        pupil[imag_lines, columns] = sine[lines].astype(jnp.bfloat16)
            else:
                empty = jnp.zeros((ROWS, positions * LANES), jnp.bfloat16)
                pupil[real_lines] = empty
                pupil[imag_lines] = empty
            if c > 0 and j % 2 == 1:
                product(c - 1, slice(j // 2 * width, (j // 2 + 1) * width))
    for n in range(positions * LANES // width):
        product(len(CHUNKS) - 1, slice(n * width, (n + 1) * width))


def whole_kernel(sizes, length_ref, place, where, *refs):
    positions, modes, waves, half, slabs, keys = sizes
    parts, refs = refs[: 1 + len(keys)], refs[1 + len(keys) :]
    spread, row_ref, column_ref = refs[:3]
    image_ref, path, opening = refs[3:6]
    basis, sems = refs[6:8]
    scratch = refs[8:]

    @pl.when(pl.program_id(0) == 0)
    def _():
        form_paths(sizes, where, place, parts, spread, path, opening, basis, sems)

    inverse = 1.0 / length_ref[0, :1]
    rows = PIX
    transform(positions, rows, inverse, path, opening, row_ref, column_ref, scratch)
    first = scratch[3]
    share = rows // waves
    for f in range(positions):
        lines = first[f * rows : (f + 1) * rows]
        real = jnp.dot(lines, column_ref[0, :, :PIX], preferred_element_type=jnp.float32)
        imag = jnp.dot(lines, column_ref[0, :, PIX:], preferred_element_type=jnp.float32)
        intensity = real * real + imag * imag
        level = jnp.sum(
            jnp.sum(intensity, axis=0, keepdims=True), axis=1, keepdims=True
        ) / (rows * PIX)
        spectra = (intensity / (level + EPSILON)).astype(jnp.bfloat16)
        for part in range(waves):
            image_ref[part, 0, f * share : (f + 1) * share] = spectra[
                part * share : (part + 1) * share
            ]


def rows_kernel(positions, rows, length_ref, path, opening, row_ref, column_ref, *refs):
    image_ref, sum_ref = refs[:2]
    scratch = refs[2:]
    inverse = 1.0 / length_ref[0, :1]
    transform(positions, rows, inverse, path, opening, row_ref, column_ref, scratch)
    first = scratch[3]
    real = jnp.dot(first[...], column_ref[0, :, :PIX], preferred_element_type=jnp.float32)
    imag = jnp.dot(first[...], column_ref[0, :, PIX:], preferred_element_type=jnp.float32)
    intensity = real * real + imag * imag
    image_ref[0] = intensity
    sum_ref[0] = jnp.sum(intensity.reshape(positions, rows, PIX), axis=1)


def transform_scratch(positions, rows):
    return [
        pltpu.VMEM((2 * BAND, positions * LANES), jnp.bfloat16),
        pltpu.VMEM((2 * BAND, positions * LANES), jnp.bfloat16),
        pltpu.VMEM((2 * rows, positions * LANES), jnp.float32),
        pltpu.VMEM((positions * rows, 2 * PUP), jnp.bfloat16),
    ]


def transform_cost(lengths, positions, rows):
    return pl.CostEstimate(
        flops=lengths * positions * (rows * 8 * PUP * PUP + rows * 8 * PUP * PIX + 10**8),
        bytes_accessed=8 * 2**20,
        transcendentals=0,
    )


def table_specs(row_table, column_table):
    return [
        pl.BlockSpec((1,) + row_table.shape[1:], lambda l: (l, 0, 0, 0)),
        pl.BlockSpec((1,) + column_table.shape[1:], lambda l: (l, 0, 0)),
    ]


def whole_fields(own, got, spread, place, where, length, row_table, column_table, sizes):
    positions, modes, waves, half, slabs = sizes
    keys = tuple((h, masks) for h, _, masks in got)
    arrays = [array for _, array, _ in got]
    lengths = row_table.shape[0]
    units = place.shape[0]
    share = positions * PIX // waves
    any_memory = pl.BlockSpec(memory_space=pl.ANY)
    return pl.pallas_call(
        functools.partial(
            whole_kernel, (positions, modes, waves, half, slabs, keys)
        ),
        grid=(lengths,),
        out_shape=(
            jax.ShapeDtypeStruct((waves, lengths, share, PIX), jnp.bfloat16),
            jax.ShapeDtypeStruct((units, positions * ROWS, LANES), jnp.float32),
            jax.ShapeDtypeStruct((units, ROWS, LANES), jnp.float32),
        ),
        in_specs=[LENGTH, SMEM, SMEM]
        + [any_memory] * (1 + len(keys))
        + [VMEM]
        + table_specs(row_table, column_table),
        out_specs=(pl.BlockSpec((waves, 1, share, PIX), lambda l: (0, l, 0, 0)), VMEM, VMEM),
        scratch_shapes=[
            pltpu.VMEM((waves * slabs, ROWS, LANES), jnp.bfloat16),
            pltpu.SemaphoreType.DMA((1 + sum(len(masks) for _, masks in keys) * (waves - 1),)),
        ]
        + transform_scratch(positions, PIX),
        cost_estimate=transform_cost(lengths, positions, PIX),
        compiler_params=pltpu.CompilerParams(vmem_limit_bytes=VMEM_BYTES),
    )(length, place, where, own, *arrays, spread, row_table, column_table)


def row_fields(path, opening, length, row_table, column_table, positions):
    lengths = row_table.shape[0]
    rows = row_table.shape[2] // 2
    return pl.pallas_call(
        functools.partial(rows_kernel, positions, rows),
        grid=(lengths,),
        out_shape=(
            jax.ShapeDtypeStruct((lengths, positions * rows, PIX), jnp.float32),
            jax.ShapeDtypeStruct((lengths, positions, PIX), jnp.float32),
        ),
        in_specs=[LENGTH, VMEM, VMEM] + table_specs(row_table, column_table),
        out_specs=(
            pl.BlockSpec((1, positions * rows, PIX), lambda l: (l, 0, 0)),
            pl.BlockSpec((1, positions, PIX), lambda l: (l, 0, 0)),
        ),
        scratch_shapes=transform_scratch(positions, rows),
        cost_estimate=transform_cost(lengths, positions, rows),
        compiler_params=pltpu.CompilerParams(vmem_limit_bytes=VMEM_BYTES),
    )(length, path, opening, row_table, column_table)


def mix_kernel(inverse_ref, weight_ref, sent_ref, image_ref, out_ref):
    count, templates, rows = out_ref.shape[:3]
    for i in range(count):
        f = pl.program_id(0) * count + i
        blocks = []
        for start in range(i * rows, (i + 1) * rows, ROWS):
            lines = slice(start, start + ROWS)
            blocks.append(
                jnp.concatenate(
                    [sent_ref[l, lines] for l in range(sent_ref.shape[0])]
                    + [
                        (image_ref[l, lines] * inverse_ref[l, f]).astype(jnp.bfloat16)
                        for l in range(image_ref.shape[0])
                    ],
                    axis=0,
                )
            )
        mixed = jnp.dot(
            weight_ref[i], jnp.concatenate(blocks, axis=1), preferred_element_type=jnp.float32
        ).astype(jnp.bfloat16)
        for n in range(len(blocks)):
            for j in range(templates):
                out_ref[i, j, n * ROWS : (n + 1) * ROWS] = mixed[
                    j * ROWS : (j + 1) * ROWS, n * PIX : (n + 1) * PIX
                ]


def mix(spread, inverse, sent, images, templates, rows):
    positions = spread.shape[0]
    count = 2 if positions % 2 == 0 else 1
    return pl.pallas_call(
        mix_kernel,
        grid=(positions // count,),
        out_shape=jax.ShapeDtypeStruct((positions, templates, rows, PIX), jnp.bfloat16),
        in_specs=[
            SMEM,
            pl.BlockSpec((count,) + spread.shape[1:], lambda f: (f, 0, 0)),
            pl.BlockSpec((sent.shape[0], count * rows, PIX), lambda f: (0, f, 0)),
            pl.BlockSpec((images.shape[0], count * rows, PIX), lambda f: (0, f, 0)),
        ],
        out_specs=pl.BlockSpec((count, templates, rows, PIX), lambda f: (f, 0, 0, 0)),
        compiler_params=pltpu.CompilerParams(vmem_limit_bytes=VMEM_BYTES),
    )(inverse, spread, sent, images)


def table_kernel(length_ref, y_ref, v_ref, u_ref, x_ref, row_ref, column_ref, token_ref):
    scale = (SAMPLING / (2.0 * PUP)) / length_ref[0, :1]
    scale = jnp.concatenate([scale] * (PIX // LANES), axis=1)
    token_ref[...] = jnp.zeros_like(token_ref)
    for start in range(0, PUP, ROWS):
        s, k = half_turn((y_ref[start : start + ROWS] * v_ref[...]) * scale)
        cosine, sine = 1.0 - s * s, s * k
        lower = slice(start, start + ROWS)
        upper = slice(PUP + start, PUP + start + ROWS)
        column_ref[0, lower, :PIX] = cosine.astype(jnp.bfloat16)
        column_ref[0, lower, PIX:] = (-sine).astype(jnp.bfloat16)
        column_ref[0, upper, :PIX] = sine.astype(jnp.bfloat16)
        column_ref[0, upper, PIX:] = cosine.astype(jnp.bfloat16)
    rows = u_ref.shape[0]
    imag = (lax.broadcasted_iota(jnp.int32, (ROWS, 2 * BAND), 1) // ROWS) % 2 == 1
    for band in range(BANDS):
        for start in range(0, rows, ROWS):
            s, k = half_turn((u_ref[start : start + ROWS] * x_ref[band]) * scale)
            cosine, sine = 1.0 - s * s, s * k
            row_ref[0, band, start : start + ROWS] = jnp.where(imag, sine, cosine).astype(
                jnp.bfloat16
            )
            row_ref[0, band, rows + start : rows + start + ROWS] = jnp.where(
                imag, cosine, -sine
            ).astype(jnp.bfloat16)


def tables(length, first_row, rows):
    lengths = length.shape[0]
    y = 2 * np.concatenate([band_columns(band) for band in range(BANDS)]) - PUP + 1
    v = np.arange(PIX) - PIX // 2
    u = first_row + jnp.arange(rows, dtype=jnp.int32) - PIX // 2
    x = np.array(
        [[row + i for row in band_rows(band) for i in range(ROWS)] for band in range(BANDS)]
    )
    x = np.repeat(x.reshape(BANDS, UNITS, 1, ROWS), 2, axis=2).reshape(BANDS, 1, 2 * BAND)
    whole = lambda *shape: pl.BlockSpec(shape, lambda l: (0,) * len(shape))
    return pl.pallas_call(
        table_kernel,
        grid=(lengths,),
        out_shape=(
            jax.ShapeDtypeStruct((lengths, BANDS, 2 * rows, 2 * BAND), jnp.bfloat16),
            jax.ShapeDtypeStruct((lengths, 2 * PUP, 2 * PIX), jnp.bfloat16),
            jax.ShapeDtypeStruct((8, LANES), jnp.float32),
        ),
        in_specs=[
            LENGTH,
            whole(PUP, 1),
            whole(1, PIX),
            whole(rows, 1),
            whole(BANDS, 1, 2 * BAND),
        ],
        out_specs=(
            pl.BlockSpec((1, BANDS, 2 * rows, 2 * BAND), lambda l: (l, 0, 0, 0)),
            pl.BlockSpec((1, 2 * PUP, 2 * PIX), lambda l: (l, 0, 0)),
            whole(8, LANES),
        ),
        cost_estimate=pl.CostEstimate(
            flops=lengths * 30 * PUP * PIX, bytes_accessed=lengths * 4 * PUP * PIX * 2, transcendentals=0
        ),
        compiler_params=pltpu.CompilerParams(vmem_limit_bytes=VMEM_BYTES),
    )(
        length,
        jnp.asarray(y[:, None].astype(np.float32)),
        jnp.asarray(v[None, :].astype(np.float32)),
        u.astype(jnp.float32)[:, None],
        jnp.asarray((2 * x - PUP + 1).astype(np.float32)),
    )


def add_over_wave(x, waves):
    copies = jnp.broadcast_to(x[None], (waves,) + x.shape)
    return jnp.sum(lax.all_to_all(copies, "wave", split_axis=0, concat_axis=0, tiled=True), axis=0)


def local(mode_basis, coef_table, table_index, wave_lengths, sed_table, template_ids):
    waves = lax.axis_size("wave")
    mine = lax.axis_index("wave")
    modes = mode_basis.shape[0]
    positions = table_index.shape[0]
    rows = PIX // waves
    count, half, slabs, pack, place = layout(waves, modes)
    lengths = wave_lengths.shape[0]
    sent_lengths = lengths // 2

    share = (lax.axis_index("groups") % 2) * 4 + lax.axis_index("field") % 4
    where = jnp.stack([mine, share]).astype(jnp.int32)
    own, piece = pack_rows(mode_basis, wave_lengths, pack, where, half, slabs)
    parts = along_wave(piece, waves)
    low, high, every = split_parts(parts, where, wave_lengths, half, sent_lengths)
    own_length = jnp.broadcast_to(
        wave_lengths[:sent_lengths, None, None], (sent_lengths, 8, LANES)
    )
    own_row, own_column, _ = tables(own_length, 0, PIX)
    all_row, all_column, token = tables(every, mine * rows, rows)
    got = gather_rows((low, high), token)

    selector = (
        table_index[:, None] == jnp.arange(coef_table.shape[0], dtype=jnp.int32)[None, :]
    ).astype(jnp.bfloat16)
    coeffs = jnp.dot(selector, coef_table, preferred_element_type=jnp.float32)
    one_hot = (
        template_ids[:, :, None]
        == jnp.arange(sed_table.shape[0], dtype=jnp.int32)[None, None, :]
    ).astype(jnp.float32)
    raw_weights = jnp.einsum("fjn,nl->fjl", one_hot, sed_table, precision=lax.Precision.HIGHEST)
    weights = (raw_weights / jnp.sum(raw_weights, axis=2, keepdims=True)).astype(jnp.bfloat16)
    templates = weights.shape[1]
    split = weights.reshape(positions, templates, waves, lengths)
    weights = jnp.concatenate(
        [
            split[..., :sent_lengths].reshape(positions, templates, -1),
            split[..., sent_lengths:].reshape(positions, templates, -1),
        ],
        axis=2,
    )
    path_spread, mix_spread = spreads(coeffs.astype(jnp.bfloat16)[None], weights)

    spectra, path, opening = whole_fields(
        own,
        got,
        path_spread,
        place,
        where,
        own_length,
        own_row,
        own_column,
        (positions, modes, waves, half, slabs),
    )
    sent = lax.all_to_all(spectra, "wave", split_axis=0, concat_axis=0, tiled=True)
    sent = sent.reshape(waves * sent_lengths, positions * rows, PIX)

    images, sums = row_fields(path, opening, every, all_row, all_column, positions)
    level = add_over_wave(jnp.sum(sums, axis=2), waves) / (PIX * PIX)
    return mix(mix_spread, 1.0 / (level + EPSILON), sent, images, templates, rows)


def solution(mesh):
    return jax.shard_map(
        local,
        mesh=mesh,
        in_specs=(
            P(None, "wave", None),
            P(),
            P(("groups", "field")),
            P("wave"),
            P(),
            P(("groups", "field"), None),
        ),
        out_specs=P(("groups", "field"), None, "wave", None),
        check_vma=False,
    )
```

```python
import functools
import math

import jax
import jax.numpy as jnp
import numpy as np
from jax import lax
from jax.experimental import pallas as pl
from jax.experimental.pallas import tpu as pltpu
from jax.sharding import PartitionSpec as P

PUP = 512
PIX = 256
TWO_PI = 2.0 * math.pi
SAMPLING = 0.25
EPSILON = 1e-06
INNER = 61 * PUP // 100
BAND = 128
BANDS = PUP // BAND
ROWS = 16
LANES = 128
UNITS = BAND // ROWS
VMEM_BYTES = 60 * 2**20
SHARES = 8

SMEM = pl.BlockSpec(memory_space=pltpu.SMEM)
VMEM = pl.BlockSpec(memory_space=pltpu.VMEM)

SIN_POLY = (4.4428679, -7.30744341, 3.59478797, -0.78437376)
COS_POLY = (1.4142135, -6.97885099, 5.73946117, -1.88356298, 0.31069817)


def half_turn(turns):
    magic = jnp.float32(12582912.0)
    r = turns - ((turns + magic) - magic)
    z = r * r
    s = jnp.float32(SIN_POLY[-1])
    for value in SIN_POLY[-2::-1]:
        s = s * z + value
    k = jnp.float32(COS_POLY[-1])
    for value in COS_POLY[-2::-1]:
        k = k * z + value
    return s * r, k


def band_rows(band):
    low, high = PUP // 2 - 64 * (band + 1), PUP // 2 + 64 * band
    return [low + ROWS * i for i in range(4)] + [high + ROWS * i for i in range(4)]


def band_columns(band):
    low, high = PUP // 2 - 64 * (band + 1), PUP // 2 + 64 * band
    sides = (high, low) if band % 2 == 0 else (low, high)
    return np.concatenate([side + np.arange(64) for side in sides])


def unit_open(row, band):
    a = 2 * (row + np.arange(ROWS)) - PUP + 1
    b = 2 * band_columns(band) - PUP + 1
    radius = a[:, None] ** 2 + b[None, :] ** 2
    return bool(np.any((radius <= PUP * PUP) & (radius >= INNER * INNER)))


STAGES = ((0, 3), (1, 2))
WIDE = BANDS // len(STAGES) * LANES


def chunks_of(stage):
    return [
        (band, rows)
        for band in STAGES[stage]
        for rows in range(BANDS)
        if any(unit_open(row, band) for row in band_rows(rows))
    ]


@functools.lru_cache(None)
def layout(waves, modes, stage):
    per = PUP // waves
    lists = []
    for wave in range(waves):
        lists.append(
            [
                (band, row)
                for band in STAGES[stage]
                for row in range(wave * per, (wave + 1) * per, ROWS)
                if unit_open(row, band)
            ]
        )
    count = max(len(one) for one in lists)
    half = -(-count * modes // (2 * SHARES))
    slabs = 2 * SHARES * half
    pack = np.zeros((waves, count, 3), np.int32)
    for wave, one in enumerate(lists):
        for i, (band, row) in enumerate(one):
            columns = band_columns(band)
            pack[wave, i] = (columns[0] // LANES * LANES, columns[64] // LANES * LANES, row - wave * per)
    chunks = chunks_of(stage)
    place = np.zeros((len(chunks) * UNITS, 4), np.int32)
    for c, (band, rows) in enumerate(chunks):
        columns = band_columns(band)
        for j, row in enumerate(band_rows(rows)):
            wave = row // per
            slab = 0
            if (band, row) in lists[wave]:
                slab = wave * slabs + lists[wave].index((band, row)) * modes
            place[c * UNITS + j] = (slab, row, columns[0], columns[64] - 64)
    return half, slabs, pack, place


def pack_kernel(count, modes, half, with_lengths, where, table, lengths, basis, own, piece):
    left = lax.broadcasted_iota(jnp.int32, (ROWS, LANES), 1) < 64
    wave, share = where[0], where[1]

    def unit(i, carry):
        first = pl.multiple_of(table[wave * count + i, 0], LANES)
        second = pl.multiple_of(table[wave * count + i, 1], LANES)
        row = pl.multiple_of(table[wave * count + i, 2], ROWS)
        for k in range(modes):
            one = basis[k, pl.ds(row, ROWS), pl.ds(first, LANES)].astype(jnp.float32)
            two = basis[k, pl.ds(row, ROWS), pl.ds(second, LANES)].astype(jnp.float32)
            own[i * modes + k] = jnp.where(left, one, two).astype(own.dtype)
        return carry

    lax.fori_loop(0, count, unit, 0)
    for n in range(count * modes, own.shape[0]):
        own[n] = jnp.zeros((ROWS, LANES), own.dtype)
    piece[: 2 * half] = own[pl.ds(share * (2 * half), 2 * half)]
    if not with_lengths:
        return
    line = lax.broadcasted_iota(jnp.int32, (ROWS, LANES), 0)
    slab = jnp.zeros((ROWS, LANES), jnp.float32)
    for i in range(lengths.shape[0]):
        rest = jnp.full((ROWS, LANES), lengths[i], jnp.float32)
        for limb in range(3):
            value = rest.astype(jnp.bfloat16).astype(jnp.float32)
            slab = jnp.where(line == 3 * i + limb, value, slab)
            rest = rest - value
    piece[2 * half] = slab.astype(piece.dtype)


def pack_rows(basis, wave_lengths, table, where, half, slabs, with_lengths):
    modes = basis.shape[0]
    waves, count, _ = table.shape
    smem = pl.BlockSpec(memory_space=pltpu.SMEM)
    vmem = pl.BlockSpec(memory_space=pltpu.VMEM)
    return pl.pallas_call(
        functools.partial(pack_kernel, count, modes, half, with_lengths),
        out_shape=(
            jax.ShapeDtypeStruct((slabs, ROWS, LANES), basis.dtype),
            jax.ShapeDtypeStruct((2 * half + int(with_lengths), ROWS, LANES), basis.dtype),
        ),
        in_specs=[smem, smem, smem, vmem],
        out_specs=(vmem, vmem),
        compiler_params=pltpu.CompilerParams(vmem_limit_bytes=VMEM_BYTES),
    )(where, table.reshape(waves * count, 3), wave_lengths, basis)


def split_kernel(half, sent, parts_count, where, own_lengths, *refs):
    parts, (low_ref, high_ref, length_ref) = refs[:parts_count], refs[-3:]
    wave, waves = where[0], parts_count + 1
    kept = own_lengths.shape[0] - sent
    for s in range(waves):
        for i in range(kept):
            if s == 0:
                value = jnp.full((8, LANES), own_lengths[sent + i], jnp.float32)
            else:
                slab = parts[s - 1][2 * half].astype(jnp.float32)
                line = 3 * (sent + i)
                value = (slab[line : line + 1] + slab[line + 1 : line + 2]) + slab[
                    line + 2 : line + 3
                ]
                value = jnp.broadcast_to(value, (8, LANES))
            length_ref[lax.rem(wave + (waves - s), waves) * kept + i] = value
    for s, part in enumerate(parts):
        low_ref[s * half : (s + 1) * half] = part[:half]
        high_ref[s * half : (s + 1) * half] = part[half : 2 * half]


def split_parts(parts, where, wave_lengths, half, sent, tokens):
    count = (len(parts) + 1) * (wave_lengths.shape[0] - sent)
    slabs = jax.ShapeDtypeStruct((len(parts) * half, ROWS, LANES), parts[0].dtype)
    return pl.pallas_call(
        functools.partial(split_kernel, half, sent, len(parts)),
        out_shape=(slabs, slabs, jax.ShapeDtypeStruct((count, 8, LANES), jnp.float32)),
        in_specs=[SMEM, SMEM] + [VMEM] * (len(parts) + len(tokens)),
        out_specs=(VMEM,) * 3,
        compiler_params=pltpu.CompilerParams(vmem_limit_bytes=VMEM_BYTES),
    )(where, wave_lengths, *parts, *tokens)


def join_kernel(count, *refs):
    start = 0
    for one in refs[:count]:
        refs[-2][start : start + one.shape[0]] = one[...]
        start += one.shape[0]
    refs[-1][...] = jnp.zeros_like(refs[-1])


def join(arrays, tokens):
    long = sum(one.shape[0] for one in arrays)
    return pl.pallas_call(
        functools.partial(join_kernel, len(arrays)),
        out_shape=(
            jax.ShapeDtypeStruct((long,) + arrays[0].shape[1:], arrays[0].dtype),
            jax.ShapeDtypeStruct((8, LANES), jnp.float32),
        ),
        in_specs=[VMEM] * (len(arrays) + len(tokens)),
        out_specs=(VMEM, VMEM),
        compiler_params=pltpu.CompilerParams(vmem_limit_bytes=VMEM_BYTES),
    )(*arrays, *tokens)


def along_wave(piece, waves):
    return [
        lax.ppermute(piece, "wave", [(i, (i + s) % waves) for i in range(waves)])
        for s in range(1, waves)
    ]


def swap(x, mask):
    groups, fields = lax.axis_size("groups"), lax.axis_size("field")
    pairs = [
        (g * fields + f, (g ^ (mask >> 2)) * fields + (f ^ (mask & 3)))
        for g in range(groups)
        for f in range(fields)
    ]
    return lax.ppermute(x, ("groups", "field"), pairs)


def gather_halves(halves, token):
    got = []
    tokens = []
    for h, (one, two) in enumerate(((2, 4), (4, 2))):
        mine = halves[h]
        both, done = join([mine, swap(mine, one)], [token])
        far = swap(both, two)
        got.append((h, both, (0, one)))
        got.append((h, far, (two, one | two)))
        got.append((h, swap(both, 1), (1, one | 1)))
        got.append((h, swap(far, 1), (two | 1, one | two | 1)))
    return got


def gather_direct(mine):
    got = [(None, mine, (0,)), (None, swap(mine, 1), (1,))]
    for mask in (6, 2, 4):
        there = swap(mine, mask)
        got.append((None, there, (mask,)))
        got.append((None, swap(there, 1), (mask | 1,)))
    return got


def spread_kernel(*refs):
    count = len(refs) // 2
    refs[-1][...] = jnp.zeros_like(refs[-1])
    for small_ref, big_ref in zip(refs[:count], refs[count:-1]):
        _, many, wide = small_ref.shape
        tall, long = many * ROWS, wide * ROWS
        down = lax.broadcasted_iota(jnp.int32, (tall, many), 0) // ROWS
        down = (down == lax.broadcasted_iota(jnp.int32, (tall, many), 1)).astype(jnp.float32)
        along = lax.broadcasted_iota(jnp.int32, (wide, long), 1) // ROWS
        along = (along == lax.broadcasted_iota(jnp.int32, (wide, long), 0)).astype(jnp.float32)
        same = (lax.broadcasted_iota(jnp.int32, (tall, long), 0) % ROWS) == (
            lax.broadcasted_iota(jnp.int32, (tall, long), 1) % ROWS
        )
        down, along = down.astype(jnp.bfloat16), along.astype(jnp.bfloat16)
        for i in range(small_ref.shape[0]):
            half = jnp.dot(down, small_ref[i], preferred_element_type=jnp.float32)
            whole = jnp.dot(half.astype(jnp.bfloat16), along, preferred_element_type=jnp.float32)
            big_ref[i] = jnp.where(same, whole, 0.0).astype(jnp.bfloat16)


def spreads(*matrices):
    return pl.pallas_call(
        spread_kernel,
        out_shape=tuple(
            jax.ShapeDtypeStruct((m.shape[0], m.shape[1] * ROWS, m.shape[2] * ROWS), jnp.bfloat16)
            for m in matrices
        )
        + (jax.ShapeDtypeStruct((8, LANES), jnp.float32),),
        compiler_params=pltpu.CompilerParams(vmem_limit_bytes=VMEM_BYTES),
    )(*matrices)


def form_paths(sizes, where, place, parts, spread, path, opening, basis, sems):
    positions, modes, waves, half, slabs, keys = sizes
    length = 2 * half if keys[0][0] is None else half
    wave, share = where[0], where[1]
    copies = [pltpu.make_async_copy(parts[0], basis.at[pl.ds(wave * slabs, slabs)], sems.at[0])]
    n = 1
    for (h, masks), part in zip(keys, parts[1:]):
        for m, mask in enumerate(masks):
            for s in range(1, waves):
                source = lax.rem(wave + (waves - s), waves)
                start = source * slabs + (share ^ mask) * (2 * half) + (h or 0) * half
                copies.append(
                    pltpu.make_async_copy(
                        part.at[pl.ds((m * (waves - 1) + s - 1) * length, length)],
                        basis.at[pl.ds(start, length)],
                        sems.at[n],
                    )
                )
                n += 1
    for copy in copies:
        copy.start()
    for copy in copies:
        copy.wait()

    lane = lax.broadcasted_iota(jnp.int32, (ROWS, LANES), 1)
    line = lax.broadcasted_iota(jnp.int32, (ROWS, LANES), 0)

    def chunk(c, carry):
        values = jnp.concatenate(
            [
                basis[pl.ds(place[c * UNITS + j, 0], modes)].reshape(modes * ROWS, LANES)
                for j in range(UNITS)
            ],
            axis=1,
        )
        found = jnp.dot(spread[0], values, preferred_element_type=jnp.float32)
        for j in range(UNITS):
            u = c * UNITS + j
            a = 2 * (line + place[u, 1]) - (PUP - 1)
            b = 2 * (lane + jnp.where(lane < 64, place[u, 2], place[u, 3])) - (PUP - 1)
            radius = a * a + b * b
            inside = (radius <= PUP * PUP) & (radius >= INNER * INNER)
            opening[u] = jnp.where(inside, 1.0, 0.0)
            for f in range(positions):
                path[u, f * ROWS : (f + 1) * ROWS] = jnp.where(
                    inside, found[f * ROWS : (f + 1) * ROWS, j * LANES : (j + 1) * LANES], 0.0
                )
        return carry

    lax.fori_loop(0, place.shape[0] // UNITS, chunk, 0)


def transform(stage, positions, rows, inverse, path, opening, row_ref, first, scratch):
    pupils, total = scratch[:2], scratch[2]
    chunks = chunks_of(stage)
    batch = max(1, positions // 2)
    width = 2 * positions * LANES // UNITS

    def finish(band, columns, value):
        start = STAGES[stage].index(band) * LANES
        for f in range(columns.start // LANES, columns.stop // LANES):
            lanes = slice(f * LANES - columns.start, (f + 1) * LANES - columns.start)
            for part in range(2):
                first[
                    f * rows : (f + 1) * rows,
                    part * WIDE + start : part * WIDE + start + LANES,
                ] = value[part * rows : (part + 1) * rows, lanes].astype(jnp.bfloat16)

    def product(c, columns):
        band, rows_band = chunks[c]
        value = jnp.dot(
            row_ref[0, rows_band], pupils[c % 2][:, columns], preferred_element_type=jnp.float32
        )
        if c > 0 and chunks[c - 1][0] == band:
            value = value + total[:, columns]
        if c + 1 < len(chunks) and chunks[c + 1][0] == band:
            total[:, columns] = value
        else:
            finish(band, columns, value)

    for c, (band, rows_band) in enumerate(chunks):
        pupil = pupils[c % 2]
        for j, row in enumerate(band_rows(rows_band)):
            real_lines = slice(2 * ROWS * j, 2 * ROWS * j + ROWS)
            imag_lines = slice(2 * ROWS * j + ROWS, 2 * ROWS * (j + 1))
            if unit_open(row, band):
                u = c * UNITS + j
                inside = opening[u]
                for f0 in range(0, positions, batch):
                    s, k = half_turn(path[u, f0 * ROWS : (f0 + batch) * ROWS] * inverse)
                    sine = s * k
                    square = s * s
                    for f in range(f0, f0 + batch):
                        columns = slice(f * LANES, (f + 1) * LANES)
                        lines = slice((f - f0) * ROWS, (f - f0 + 1) * ROWS)
                        pupil[real_lines, columns] = (inside - square[lines]).astype(jnp.bfloat16)
                        pupil[imag_lines, columns] = sine[lines].astype(jnp.bfloat16)
            else:
                empty = jnp.zeros((ROWS, positions * LANES), jnp.bfloat16)
                pupil[real_lines] = empty
                pupil[imag_lines] = empty
            if c > 0 and j % 2 == 1:
                product(c - 1, slice(j // 2 * width, (j // 2 + 1) * width))
    for n in range(positions * LANES // width):
        product(len(chunks) - 1, slice(n * width, (n + 1) * width))


def columns_of(first_a, first_b, column_ref):
    out = []
    for part in range(2):
        lanes = slice(part * PIX, (part + 1) * PIX)
        out.append(
            jnp.dot(first_a, column_ref[0, : 2 * WIDE, lanes], preferred_element_type=jnp.float32)
            + jnp.dot(
                first_b, column_ref[0, 2 * WIDE :, lanes], preferred_element_type=jnp.float32
            )
        )
    return out


def whole_kernel(stage, sizes, tokens, length_ref, place, where, *refs):
    positions, modes, waves, half, slabs, keys = sizes
    last = stage == len(STAGES) - 1
    parts, refs = refs[: 1 + len(keys)], refs[1 + len(keys) :]
    spread, row_ref, refs = refs[0], refs[1], refs[2:]
    if last:
        column_ref, before, refs = refs[0], refs[1], refs[2:]
    out_ref, path, opening, basis, sems = refs[tokens : tokens + 5]
    scratch = refs[tokens + 5 :]

    @pl.when(pl.program_id(0) == 0)
    def _():
        form_paths(sizes, where, place, parts, spread, path, opening, basis, sems)

    inverse = 1.0 / length_ref[0, :1]
    rows = PIX
    first = scratch[3] if last else out_ref.at[0]
    transform(stage, positions, rows, inverse, path, opening, row_ref, first, scratch)
    if not last:
        return
    share = rows // waves
    for f in range(positions):
        lines = slice(f * rows, (f + 1) * rows)
        real, imag = columns_of(before[0, lines], first[lines], column_ref)
        intensity = real * real + imag * imag
        level = jnp.sum(
            jnp.sum(intensity, axis=0, keepdims=True), axis=1, keepdims=True
        ) / (rows * PIX)
        spectra = (intensity / (level + EPSILON)).astype(jnp.bfloat16)
        for part in range(waves):
            out_ref[part, 0, f * share : (f + 1) * share] = spectra[
                part * share : (part + 1) * share
            ]


def rows_kernel(stage, positions, rows, length_ref, path, opening, row_ref, *refs):
    inverse = 1.0 / length_ref[0, :1]
    if stage < len(STAGES) - 1:
        refs[1][...] = jnp.zeros_like(refs[1])
        transform(
            stage, positions, rows, inverse, path, opening, row_ref, refs[0].at[0], refs[2:]
        )
        return
    column_ref, before, image_ref, sum_ref = refs[:4]
    scratch = refs[4:]
    transform(stage, positions, rows, inverse, path, opening, row_ref, scratch[3], scratch)
    real, imag = columns_of(before[0], scratch[3][...], column_ref)
    intensity = real * real + imag * imag
    image_ref[0] = intensity
    sum_ref[0] = jnp.sum(intensity.reshape(positions, rows, PIX), axis=1)


def transform_scratch(positions, rows):
    return [
        pltpu.VMEM((2 * BAND, positions * LANES), jnp.bfloat16),
        pltpu.VMEM((2 * BAND, positions * LANES), jnp.bfloat16),
        pltpu.VMEM((2 * rows, positions * LANES), jnp.float32),
        pltpu.VMEM((positions * rows, 2 * WIDE), jnp.bfloat16),
    ]


def transform_cost(stage, lengths, positions, rows):
    share = len(chunks_of(stage))
    return pl.CostEstimate(
        flops=lengths * positions * share * (rows * PUP * PUP + rows * PUP * PIX + 10**7),
        bytes_accessed=8 * 2**20,
        transcendentals=0,
    )


def by_length(array):
    return pl.BlockSpec((1,) + array.shape[1:], lambda l: (l,) + (0,) * (array.ndim - 1))


def whole_fields(stage, own, got, spread, place, where, length, tables, sizes, tokens):
    positions, modes, waves, half, slabs = sizes
    keys = tuple((h, masks) for h, _, masks in got)
    arrays = [array for _, array, _ in got]
    lengths = length.shape[0]
    units = place.shape[0]
    share = positions * PIX // waves
    any_memory = pl.BlockSpec(memory_space=pl.ANY)
    if stage < len(STAGES) - 1:
        out_shape = jax.ShapeDtypeStruct((lengths, positions * PIX, 2 * WIDE), jnp.bfloat16)
        out_spec = by_length(out_shape)
    else:
        out_shape = jax.ShapeDtypeStruct((waves, lengths, share, PIX), jnp.bfloat16)
        out_spec = pl.BlockSpec((waves, 1, share, PIX), lambda l: (0, l, 0, 0))
    return pl.pallas_call(
        functools.partial(
            whole_kernel, stage, (positions, modes, waves, half, slabs, keys), len(tokens)
        ),
        grid=(lengths,),
        out_shape=(
            out_shape,
            jax.ShapeDtypeStruct((units, positions * ROWS, LANES), jnp.float32),
            jax.ShapeDtypeStruct((units, ROWS, LANES), jnp.float32),
        ),
        in_specs=[by_length(length), SMEM, SMEM]
        + [any_memory] * (1 + len(keys))
        + [VMEM]
        + [by_length(table) for table in tables]
        + [VMEM] * len(tokens),
        out_specs=(out_spec, VMEM, VMEM),
        scratch_shapes=[
            pltpu.VMEM((waves * slabs, ROWS, LANES), jnp.bfloat16),
            pltpu.SemaphoreType.DMA((1 + sum(len(masks) for _, masks in keys) * (waves - 1),)),
        ]
        + transform_scratch(positions, PIX),
        cost_estimate=transform_cost(stage, lengths, positions, PIX),
        compiler_params=pltpu.CompilerParams(vmem_limit_bytes=VMEM_BYTES),
    )(length, place, where, own, *arrays, spread, *tables, *tokens)


def row_fields(stage, path, opening, length, tables, positions):
    lengths = length.shape[0]
    rows = tables[0].shape[2] // 2
    if stage < len(STAGES) - 1:
        out_shape = (
            jax.ShapeDtypeStruct((lengths, positions * rows, 2 * WIDE), jnp.bfloat16),
            jax.ShapeDtypeStruct((8, LANES), jnp.float32),
        )
        out_specs = (by_length(out_shape[0]), pl.BlockSpec((8, LANES), lambda l: (0, 0)))
    else:
        out_shape = (
            jax.ShapeDtypeStruct((lengths, positions * rows, PIX), jnp.float32),
            jax.ShapeDtypeStruct((lengths, positions, PIX), jnp.float32),
        )
        out_specs = tuple(by_length(one) for one in out_shape)
    return pl.pallas_call(
        functools.partial(rows_kernel, stage, positions, rows),
        grid=(lengths,),
        out_shape=out_shape,
        in_specs=[by_length(length), VMEM, VMEM] + [by_length(table) for table in tables],
        out_specs=out_specs,
        scratch_shapes=transform_scratch(positions, rows),
        cost_estimate=transform_cost(stage, lengths, positions, rows),
        compiler_params=pltpu.CompilerParams(vmem_limit_bytes=VMEM_BYTES),
    )(length, path, opening, *tables)


def mix_kernel(inverse_ref, weight_ref, sent_ref, image_ref, out_ref):
    count, templates, rows = out_ref.shape[:3]
    for i in range(count):
        f = pl.program_id(0) * count + i
        blocks = []
        for start in range(i * rows, (i + 1) * rows, ROWS):
            lines = slice(start, start + ROWS)
            blocks.append(
                jnp.concatenate(
                    [sent_ref[l, lines] for l in range(sent_ref.shape[0])]
                    + [
                        (image_ref[l, lines] * inverse_ref[l, f]).astype(jnp.bfloat16)
                        for l in range(image_ref.shape[0])
                    ],
                    axis=0,
                )
            )
        mixed = jnp.dot(
            weight_ref[i], jnp.concatenate(blocks, axis=1), preferred_element_type=jnp.float32
        ).astype(jnp.bfloat16)
        for n in range(len(blocks)):
            for j in range(templates):
                out_ref[i, j, n * ROWS : (n + 1) * ROWS] = mixed[
                    j * ROWS : (j + 1) * ROWS, n * PIX : (n + 1) * PIX
                ]


def mix(spread, inverse, sent, images, templates, rows):
    positions = spread.shape[0]
    count = 2 if positions % 2 == 0 else 1
    return pl.pallas_call(
        mix_kernel,
        grid=(positions // count,),
        out_shape=jax.ShapeDtypeStruct((positions, templates, rows, PIX), jnp.bfloat16),
        in_specs=[
            SMEM,
            pl.BlockSpec((count,) + spread.shape[1:], lambda f: (f, 0, 0)),
            pl.BlockSpec((sent.shape[0], count * rows, PIX), lambda f: (0, f, 0)),
            pl.BlockSpec((images.shape[0], count * rows, PIX), lambda f: (0, f, 0)),
        ],
        out_specs=pl.BlockSpec((count, templates, rows, PIX), lambda f: (f, 0, 0, 0)),
        compiler_params=pltpu.CompilerParams(vmem_limit_bytes=VMEM_BYTES),
    )(inverse, spread, sent, images)


def table_kernel(length_ref, y_ref, v_ref, u_ref, x_ref, row_ref, column_ref, token_ref):
    scale = (SAMPLING / (2.0 * PUP)) / length_ref[0, :1]
    scale = jnp.concatenate([scale] * (PIX // LANES), axis=1)
    token_ref[...] = jnp.zeros_like(token_ref)
    for start in range(0, PUP, ROWS):
        s, k = half_turn((y_ref[start : start + ROWS] * v_ref[...]) * scale)
        cosine, sine = 1.0 - s * s, s * k
        lower = start // WIDE * 2 * WIDE + start % WIDE
        lower, upper = slice(lower, lower + ROWS), slice(lower + WIDE, lower + WIDE + ROWS)
        column_ref[0, lower, :PIX] = cosine.astype(jnp.bfloat16)
        column_ref[0, lower, PIX:] = (-sine).astype(jnp.bfloat16)
        column_ref[0, upper, :PIX] = sine.astype(jnp.bfloat16)
        column_ref[0, upper, PIX:] = cosine.astype(jnp.bfloat16)
    rows = u_ref.shape[0]
    imag = (lax.broadcasted_iota(jnp.int32, (ROWS, 2 * BAND), 1) // ROWS) % 2 == 1
    for band in range(BANDS):
        for start in range(0, rows, ROWS):
            s, k = half_turn((u_ref[start : start + ROWS] * x_ref[band]) * scale)
            cosine, sine = 1.0 - s * s, s * k
            row_ref[0, band, start : start + ROWS] = jnp.where(imag, sine, cosine).astype(
                jnp.bfloat16
            )
            row_ref[0, band, rows + start : rows + start + ROWS] = jnp.where(
                imag, cosine, -sine
            ).astype(jnp.bfloat16)


def tables(length, first_row, rows):
    lengths = length.shape[0]
    y = 2 * np.concatenate([band_columns(band) for stage in STAGES for band in stage]) - PUP + 1
    v = np.arange(PIX) - PIX // 2
    u = first_row + jnp.arange(rows, dtype=jnp.int32) - PIX // 2
    x = np.array(
        [[row + i for row in band_rows(band) for i in range(ROWS)] for band in range(BANDS)]
    )
    x = np.repeat(x.reshape(BANDS, UNITS, 1, ROWS), 2, axis=2).reshape(BANDS, 1, 2 * BAND)
    whole = lambda *shape: pl.BlockSpec(shape, lambda l: (0,) * len(shape))
    return pl.pallas_call(
        table_kernel,
        grid=(lengths,),
        out_shape=(
            jax.ShapeDtypeStruct((lengths, BANDS, 2 * rows, 2 * BAND), jnp.bfloat16),
            jax.ShapeDtypeStruct((lengths, 2 * PUP, 2 * PIX), jnp.bfloat16),
            jax.ShapeDtypeStruct((8, LANES), jnp.float32),
        ),
        in_specs=[
            pl.BlockSpec((1, 8, LANES), lambda l: (l, 0, 0)),
            whole(PUP, 1),
            whole(1, PIX),
            whole(rows, 1),
            whole(BANDS, 1, 2 * BAND),
        ],
        out_specs=(
            pl.BlockSpec((1, BANDS, 2 * rows, 2 * BAND), lambda l: (l, 0, 0, 0)),
            pl.BlockSpec((1, 2 * PUP, 2 * PIX), lambda l: (l, 0, 0)),
            whole(8, LANES),
        ),
        cost_estimate=pl.CostEstimate(
            flops=lengths * 30 * PUP * PIX, bytes_accessed=lengths * 4 * PUP * PIX * 2, transcendentals=0
        ),
        compiler_params=pltpu.CompilerParams(vmem_limit_bytes=VMEM_BYTES),
    )(
        length,
        jnp.asarray(y[:, None].astype(np.float32)),
        jnp.asarray(v[None, :].astype(np.float32)),
        u.astype(jnp.float32)[:, None],
        jnp.asarray((2 * x - PUP + 1).astype(np.float32)),
    )


def add_over_wave(x, waves):
    step = 1
    while step < waves:
        x = x + lax.ppermute(x, "wave", [(i, i ^ step) for i in range(waves)])
        step *= 2
    return x


def local(mode_basis, coef_table, table_index, wave_lengths, sed_table, template_ids):
    waves = lax.axis_size("wave")
    mine = lax.axis_index("wave")
    modes = mode_basis.shape[0]
    positions = table_index.shape[0]
    rows = PIX // waves
    lengths = wave_lengths.shape[0]
    sent_lengths = lengths // 2

    share = (lax.axis_index("groups") % 2) * 4 + lax.axis_index("field") % 4
    where = jnp.stack([mine, share]).astype(jnp.int32)
    plans = [layout(waves, modes, stage) for stage in range(len(STAGES))]
    owns, parts = [], []
    for stage, (half, slabs, pack, _) in enumerate(plans):
        own, piece = pack_rows(mode_basis, wave_lengths, pack, where, half, slabs, stage == 0)
        owns.append(own)
        parts.append(along_wave(piece, waves))

    selector = (
        table_index[:, None] == jnp.arange(coef_table.shape[0], dtype=jnp.int32)[None, :]
    ).astype(jnp.bfloat16)
    coeffs = jnp.dot(selector, coef_table, preferred_element_type=jnp.float32)
    one_hot = (
        template_ids[:, :, None]
        == jnp.arange(sed_table.shape[0], dtype=jnp.int32)[None, None, :]
    ).astype(jnp.float32)
    raw_weights = jnp.einsum("fjn,nl->fjl", one_hot, sed_table, precision=lax.Precision.HIGHEST)
    weights = (raw_weights / jnp.sum(raw_weights, axis=2, keepdims=True)).astype(jnp.bfloat16)
    templates = weights.shape[1]
    split = weights.reshape(positions, templates, waves, lengths)
    weights = jnp.concatenate(
        [
            split[..., :sent_lengths].reshape(positions, templates, -1),
            split[..., sent_lengths:].reshape(positions, templates, -1),
        ],
        axis=2,
    )
    path_spread, mix_spread, spread_token = spreads(coeffs.astype(jnp.bfloat16)[None], weights)
    own_length = jnp.broadcast_to(
        wave_lengths[:sent_lengths, None, None], (sent_lengths, 8, LANES)
    )
    own_row, own_column, own_token = tables(own_length, 0, PIX)

    low, high, every = split_parts(
        parts[0], where, wave_lengths, plans[0][0], sent_lengths, (spread_token, own_token)
    )
    all_row, all_column, all_token = tables(every, mine * rows, rows)
    got = gather_halves((low, high), all_token)
    second, second_token = join(parts[1], [array[0, :8] for _, array, masks in got if masks in ((2, 6), (4, 6))])

    def sizes(stage):
        half, slabs, _, _ = plans[stage]
        return positions, modes, waves, half, slabs

    before, path, opening = whole_fields(
        0, owns[0], got, path_spread, plans[0][3], where, own_length, (own_row,), sizes(0),
        (second_token,),
    )
    got = gather_direct(second)
    rows_before, rows_token = row_fields(0, path, opening, every, (all_row,), positions)
    spectra, path, opening = whole_fields(
        1, owns[1], got, path_spread, plans[1][3], where, own_length,
        (own_row, own_column, before), sizes(1), (rows_token,),
    )
    sent = lax.all_to_all(spectra, "wave", split_axis=0, concat_axis=0, tiled=True)
    sent = sent.reshape(waves * sent_lengths, positions * rows, PIX)
    images, sums = row_fields(
        1, path, opening, every, (all_row, all_column, rows_before), positions
    )
    level = add_over_wave(jnp.sum(sums, axis=2), waves) / (PIX * PIX)
    return mix(mix_spread, 1.0 / (level + EPSILON), sent, images, templates, rows)


def solution(mesh):
    return jax.shard_map(
        local,
        mesh=mesh,
        in_specs=(
            P(None, "wave", None),
            P(),
            P(("groups", "field")),
            P("wave"),
            P(),
            P(("groups", "field"), None),
        ),
        out_specs=P(("groups", "field"), None, "wave", None),
        check_vma=False,
    )
```

```python
import functools
import math

import jax
import jax.numpy as jnp
import numpy as np
from jax import lax
from jax.experimental import pallas as pl
from jax.experimental.pallas import tpu as pltpu
from jax.sharding import PartitionSpec as P

PUP = 512
PIX = 256
TWO_PI = 2.0 * math.pi
SAMPLING = 0.25
EPSILON = 1e-06
INNER = 61 * PUP // 100
BAND = 128
BANDS = PUP // BAND
ROWS = 16
LANES = 128
UNITS = BAND // ROWS
VMEM_BYTES = 60 * 2**20
SHARES = 8

SMEM = pl.BlockSpec(memory_space=pltpu.SMEM)
VMEM = pl.BlockSpec(memory_space=pltpu.VMEM)

SIN_POLY = (4.4428679, -7.30744341, 3.59478797, -0.78437376)
COS_POLY = (1.4142135, -6.97885099, 5.73946117, -1.88356298, 0.31069817)


def half_turn(turns):
    magic = jnp.float32(12582912.0)
    r = turns - ((turns + magic) - magic)
    z = r * r
    s = jnp.float32(SIN_POLY[-1])
    for value in SIN_POLY[-2::-1]:
        s = s * z + value
    k = jnp.float32(COS_POLY[-1])
    for value in COS_POLY[-2::-1]:
        k = k * z + value
    return s * r, k


def band_rows(band):
    low, high = PUP // 2 - 64 * (band + 1), PUP // 2 + 64 * band
    return [low + ROWS * i for i in range(4)] + [high + ROWS * i for i in range(4)]


def band_columns(band):
    low, high = PUP // 2 - 64 * (band + 1), PUP // 2 + 64 * band
    sides = (high, low) if band % 2 == 0 else (low, high)
    return np.concatenate([side + np.arange(64) for side in sides])


def unit_open(row, band):
    a = 2 * (row + np.arange(ROWS)) - PUP + 1
    b = 2 * band_columns(band) - PUP + 1
    radius = a[:, None] ** 2 + b[None, :] ** 2
    return bool(np.any((radius <= PUP * PUP) & (radius >= INNER * INNER)))


STAGES = ((0, 3), (1, 2))
WIDE = BANDS // len(STAGES) * LANES


def chunks_of(stage):
    return [
        (band, rows)
        for band in STAGES[stage]
        for rows in range(BANDS)
        if any(unit_open(row, band) for row in band_rows(rows))
    ]


@functools.lru_cache(None)
def layout(waves, modes, stage):
    per = PUP // waves
    lists = []
    for wave in range(waves):
        lists.append(
            [
                (band, row)
                for band in STAGES[stage]
                for row in range(wave * per, (wave + 1) * per, ROWS)
                if unit_open(row, band)
            ]
        )
    count = max(len(one) for one in lists)
    half = -(-count * modes // (2 * SHARES))
    slabs = 2 * SHARES * half
    pack = np.zeros((waves, count, 3), np.int32)
    for wave, one in enumerate(lists):
        for i, (band, row) in enumerate(one):
            columns = band_columns(band)
            pack[wave, i] = (columns[0] // LANES * LANES, columns[64] // LANES * LANES, row - wave * per)
    chunks = chunks_of(stage)
    place = np.zeros((len(chunks) * UNITS, 4), np.int32)
    for c, (band, rows) in enumerate(chunks):
        columns = band_columns(band)
        for j, row in enumerate(band_rows(rows)):
            wave = row // per
            slab = 0
            if (band, row) in lists[wave]:
                slab = wave * slabs + lists[wave].index((band, row)) * modes
            place[c * UNITS + j] = (slab, row, columns[0], columns[64] - 64)
    return half, slabs, pack, place


def pack_kernel(counts, halves, modes, where, table, lengths, basis, *refs):
    owns, piece = refs[:-1], refs[-1]
    left = lax.broadcasted_iota(jnp.int32, (ROWS, LANES), 1) < 64
    wave, share = where[0], where[1]
    start, line = 0, wave * sum(counts)
    for count, half, own in zip(counts, halves, owns):

        def unit(i, carry, own=own, line=line):
            first = pl.multiple_of(table[line + i, 0], LANES)
            second = pl.multiple_of(table[line + i, 1], LANES)
            row = pl.multiple_of(table[line + i, 2], ROWS)
            for k in range(modes):
                one = basis[k, pl.ds(row, ROWS), pl.ds(first, LANES)].astype(jnp.float32)
                two = basis[k, pl.ds(row, ROWS), pl.ds(second, LANES)].astype(jnp.float32)
                own[i * modes + k] = jnp.where(left, one, two).astype(own.dtype)
            return carry

        lax.fori_loop(0, count, unit, 0)
        for n in range(count * modes, own.shape[0]):
            own[n] = jnp.zeros((ROWS, LANES), own.dtype)
        piece[start : start + 2 * half] = own[pl.ds(share * (2 * half), 2 * half)]
        start += 2 * half
        line = line + count
    line = lax.broadcasted_iota(jnp.int32, (ROWS, LANES), 0)
    slab = jnp.zeros((ROWS, LANES), jnp.float32)
    for i in range(lengths.shape[0]):
        rest = jnp.full((ROWS, LANES), lengths[i], jnp.float32)
        for limb in range(3):
            value = rest.astype(jnp.bfloat16).astype(jnp.float32)
            slab = jnp.where(line == 3 * i + limb, value, slab)
            rest = rest - value
    piece[start] = slab.astype(piece.dtype)


def pack_rows(basis, wave_lengths, plans, where):
    table = np.concatenate([pack for _, _, pack, _ in plans], axis=1)
    counts = tuple(pack.shape[1] for _, _, pack, _ in plans)
    halves = tuple(half for half, _, _, _ in plans)
    tile = (ROWS, LANES)
    return pl.pallas_call(
        functools.partial(pack_kernel, counts, halves, basis.shape[0]),
        out_shape=tuple(jax.ShapeDtypeStruct((slabs,) + tile, basis.dtype) for _, slabs, _, _ in plans)
        + (jax.ShapeDtypeStruct((2 * sum(halves) + 1,) + tile, basis.dtype),),
        in_specs=[SMEM, SMEM, SMEM, VMEM],
        out_specs=(VMEM,) * (len(plans) + 1),
        compiler_params=pltpu.CompilerParams(vmem_limit_bytes=VMEM_BYTES),
    )(where, table.reshape(-1, 3), wave_lengths, basis)


def split_kernel(halves, sent, parts_count, where, own_lengths, *refs):
    parts, (low_ref, high_ref, second_ref, length_ref) = refs[:parts_count], refs[-4:]
    half, other = halves
    wave, waves = where[0], parts_count + 1
    kept = own_lengths.shape[0] - sent
    for s in range(waves):
        for i in range(kept):
            if s == 0:
                value = jnp.full((8, LANES), own_lengths[sent + i], jnp.float32)
            else:
                slab = parts[s - 1][2 * (half + other)].astype(jnp.float32)
                line = 3 * (sent + i)
                value = (slab[line : line + 1] + slab[line + 1 : line + 2]) + slab[
                    line + 2 : line + 3
                ]
                value = jnp.broadcast_to(value, (8, LANES))
            length_ref[lax.rem(wave + (waves - s), waves) * kept + i] = value
    for s, part in enumerate(parts):
        low_ref[s * half : (s + 1) * half] = part[:half]
        high_ref[s * half : (s + 1) * half] = part[half : 2 * half]
        second_ref[s * 2 * other : (s + 1) * 2 * other] = part[2 * half : 2 * (half + other)]


def split_parts(parts, where, wave_lengths, halves, sent, tokens):
    count = (len(parts) + 1) * (wave_lengths.shape[0] - sent)
    slabs = lambda n: jax.ShapeDtypeStruct((len(parts) * n, ROWS, LANES), parts[0].dtype)
    return pl.pallas_call(
        functools.partial(split_kernel, halves, sent, len(parts)),
        out_shape=(slabs(halves[0]), slabs(halves[0]), slabs(2 * halves[1]), jax.ShapeDtypeStruct((count, 8, LANES), jnp.float32)),
        in_specs=[SMEM, SMEM] + [VMEM] * (len(parts) + len(tokens)),
        out_specs=(VMEM,) * 4,
        compiler_params=pltpu.CompilerParams(vmem_limit_bytes=VMEM_BYTES),
    )(where, wave_lengths, *parts, *tokens)


def join_kernel(pairs, *refs):
    for i in range(pairs):
        one, two, out = refs[2 * i], refs[2 * i + 1], refs[i - pairs]
        out[: one.shape[0]] = one[...]
        out[one.shape[0] :] = two[...]


def join(pairs, token):
    return pl.pallas_call(
        functools.partial(join_kernel, len(pairs)),
        out_shape=tuple(
            jax.ShapeDtypeStruct((2 * one.shape[0],) + one.shape[1:], one.dtype) for one, _ in pairs
        ),
        in_specs=[VMEM] * (2 * len(pairs) + 1),
        out_specs=(VMEM,) * len(pairs),
        compiler_params=pltpu.CompilerParams(vmem_limit_bytes=VMEM_BYTES),
    )(*[one for pair in pairs for one in pair], token)


def along_wave(piece, waves):
    return [
        lax.ppermute(piece, "wave", [(i, (i + s) % waves) for i in range(waves)])
        for s in range(1, waves)
    ]


def swap(x, mask):
    groups, fields = lax.axis_size("groups"), lax.axis_size("field")
    pairs = [
        (g * fields + f, (g ^ (mask >> 2)) * fields + (f ^ (mask & 3)))
        for g in range(groups)
        for f in range(fields)
    ]
    return lax.ppermute(x, ("groups", "field"), pairs)


def after(arrays, tokens):
    any_memory = pl.BlockSpec(memory_space=pl.ANY)
    return pl.pallas_call(
        lambda *refs: None,
        out_shape=tuple(jax.ShapeDtypeStruct(x.shape, x.dtype) for x in arrays),
        in_specs=[any_memory] * len(arrays) + [VMEM] * len(tokens),
        out_specs=(any_memory,) * len(arrays),
        input_output_aliases={i: i for i in range(len(arrays))},
    )(*arrays, *tokens)


def gather_halves(halves, token):
    got = []
    routes = ((2, 4), (4, 2))
    joined = join([(mine, swap(mine, one)) for mine, (one, _) in zip(halves, routes)], token)
    for h, (both, (one, two)) in enumerate(zip(joined, routes)):
        far = swap(both, two)
        got.append((h, both, (0, one)))
        got.append((h, far, (two, one | two)))
        got.append((h, swap(both, 1), (1, one | 1)))
        got.append((h, swap(far, 1), (two | 1, one | two | 1)))
    return got


def send_direct(mine):
    return [(None, mine, (0,)), (None, swap(mine, 1), (1,))], [
        (mask, swap(mine, mask)) for mask in (6, 2, 4)
    ]


def end_direct(got, there, token):
    arrays = after([array for _, array in there], [token])
    for (mask, _), array in zip(there, arrays):
        got = got + [(None, array, (mask,)), (None, swap(array, 1), (mask | 1,))]
    return got


def spread_kernel(*refs):
    count = len(refs) // 2
    refs[-1][...] = jnp.zeros_like(refs[-1])
    for small_ref, big_ref in zip(refs[:count], refs[count:-1]):
        _, many, wide = small_ref.shape
        tall, long = many * ROWS, wide * ROWS
        down = lax.broadcasted_iota(jnp.int32, (tall, many), 0) // ROWS
        down = (down == lax.broadcasted_iota(jnp.int32, (tall, many), 1)).astype(jnp.float32)
        along = lax.broadcasted_iota(jnp.int32, (wide, long), 1) // ROWS
        along = (along == lax.broadcasted_iota(jnp.int32, (wide, long), 0)).astype(jnp.float32)
        same = (lax.broadcasted_iota(jnp.int32, (tall, long), 0) % ROWS) == (
            lax.broadcasted_iota(jnp.int32, (tall, long), 1) % ROWS
        )
        down, along = down.astype(jnp.bfloat16), along.astype(jnp.bfloat16)
        for i in range(small_ref.shape[0]):
            half = jnp.dot(down, small_ref[i], preferred_element_type=jnp.float32)
            whole = jnp.dot(half.astype(jnp.bfloat16), along, preferred_element_type=jnp.float32)
            big_ref[i] = jnp.where(same, whole, 0.0).astype(jnp.bfloat16)


def spreads(*matrices):
    return pl.pallas_call(
        spread_kernel,
        out_shape=tuple(
            jax.ShapeDtypeStruct((m.shape[0], m.shape[1] * ROWS, m.shape[2] * ROWS), jnp.bfloat16)
            for m in matrices
        )
        + (jax.ShapeDtypeStruct((8, LANES), jnp.float32),),
        compiler_params=pltpu.CompilerParams(vmem_limit_bytes=VMEM_BYTES),
    )(*matrices)


def form_paths(sizes, where, place, parts, spread, path, opening, basis, sems):
    positions, modes, waves, half, slabs, keys = sizes
    length = 2 * half if keys[0][0] is None else half
    wave, share = where[0], where[1]
    copies = [pltpu.make_async_copy(parts[0], basis.at[pl.ds(wave * slabs, slabs)], sems.at[0])]
    n = 1
    for (h, masks), part in zip(keys, parts[1:]):
        for m, mask in enumerate(masks):
            for s in range(1, waves):
                source = lax.rem(wave + (waves - s), waves)
                start = source * slabs + (share ^ mask) * (2 * half) + (h or 0) * half
                copies.append(
                    pltpu.make_async_copy(
                        part.at[pl.ds((m * (waves - 1) + s - 1) * length, length)],
                        basis.at[pl.ds(start, length)],
                        sems.at[n],
                    )
                )
                n += 1
    for copy in copies:
        copy.start()
    for copy in copies:
        copy.wait()

    lane = lax.broadcasted_iota(jnp.int32, (ROWS, LANES), 1)
    line = lax.broadcasted_iota(jnp.int32, (ROWS, LANES), 0)

    def chunk(c, carry):
        values = jnp.concatenate(
            [
                basis[pl.ds(place[c * UNITS + j, 0], modes)].reshape(modes * ROWS, LANES)
                for j in range(UNITS)
            ],
            axis=1,
        )
        found = jnp.dot(spread[0], values, preferred_element_type=jnp.float32)
        for j in range(UNITS):
            u = c * UNITS + j
            a = 2 * (line + place[u, 1]) - (PUP - 1)
            b = 2 * (lane + jnp.where(lane < 64, place[u, 2], place[u, 3])) - (PUP - 1)
            radius = a * a + b * b
            inside = (radius <= PUP * PUP) & (radius >= INNER * INNER)
            opening[u] = jnp.where(inside, 1.0, 0.0)
            for f in range(positions):
                path[u, f * ROWS : (f + 1) * ROWS] = jnp.where(
                    inside, found[f * ROWS : (f + 1) * ROWS, j * LANES : (j + 1) * LANES], 0.0
                )
        return carry

    lax.fori_loop(0, place.shape[0] // UNITS, chunk, 0)


def transform(stage, positions, rows, inverse, path, opening, row_ref, first, scratch):
    pupils, total = scratch[:2], scratch[2]
    chunks = chunks_of(stage)
    batch = max(1, positions // 2)
    width = 2 * positions * LANES // UNITS

    def finish(band, columns, value):
        start = STAGES[stage].index(band) * LANES
        for f in range(columns.start // LANES, columns.stop // LANES):
            lanes = slice(f * LANES - columns.start, (f + 1) * LANES - columns.start)
            for part in range(2):
                first[
                    f * rows : (f + 1) * rows,
                    part * WIDE + start : part * WIDE + start + LANES,
                ] = value[part * rows : (part + 1) * rows, lanes].astype(jnp.bfloat16)

    def product(c, columns):
        band, rows_band = chunks[c]
        value = jnp.dot(
            row_ref[0, rows_band], pupils[c % 2][:, columns], preferred_element_type=jnp.float32
        )
        if c > 0 and chunks[c - 1][0] == band:
            value = value + total[:, columns]
        if c + 1 < len(chunks) and chunks[c + 1][0] == band:
            total[:, columns] = value
        else:
            finish(band, columns, value)

    for c, (band, rows_band) in enumerate(chunks):
        pupil = pupils[c % 2]
        for j, row in enumerate(band_rows(rows_band)):
            real_lines = slice(2 * ROWS * j, 2 * ROWS * j + ROWS)
            imag_lines = slice(2 * ROWS * j + ROWS, 2 * ROWS * (j + 1))
            if unit_open(row, band):
                u = c * UNITS + j
                inside = opening[u]
                for f0 in range(0, positions, batch):
                    s, k = half_turn(path[u, f0 * ROWS : (f0 + batch) * ROWS] * inverse)
                    sine = s * k
                    square = s * s
                    for f in range(f0, f0 + batch):
                        columns = slice(f * LANES, (f + 1) * LANES)
                        lines = slice((f - f0) * ROWS, (f - f0 + 1) * ROWS)
                        pupil[real_lines, columns] = (inside - square[lines]).astype(jnp.bfloat16)
                        pupil[imag_lines, columns] = sine[lines].astype(jnp.bfloat16)
            else:
                empty = jnp.zeros((ROWS, positions * LANES), jnp.bfloat16)
                pupil[real_lines] = empty
                pupil[imag_lines] = empty
            if c > 0 and j % 2 == 1:
                product(c - 1, slice(j // 2 * width, (j // 2 + 1) * width))
    for n in range(positions * LANES // width):
        product(len(chunks) - 1, slice(n * width, (n + 1) * width))


def columns_of(first_a, first_b, column_ref):
    out = []
    for part in range(2):
        lanes = slice(part * PIX, (part + 1) * PIX)
        out.append(
            jnp.dot(first_a, column_ref[0, : 2 * WIDE, lanes], preferred_element_type=jnp.float32)
            + jnp.dot(
                first_b, column_ref[0, 2 * WIDE :, lanes], preferred_element_type=jnp.float32
            )
        )
    return out


def whole_kernel(stage, sizes, tokens, length_ref, place, where, *refs):
    positions, modes, waves, half, slabs, keys = sizes
    last = stage == len(STAGES) - 1
    parts, refs = refs[: 1 + len(keys)], refs[1 + len(keys) :]
    spread, row_ref, refs = refs[0], refs[1], refs[2:]
    if last:
        column_ref, before, refs = refs[0], refs[1], refs[2:]
    out_ref, path, opening, basis, sems = refs[tokens : tokens + 5]
    scratch = refs[tokens + 5 :]

    @pl.when(pl.program_id(0) == 0)
    def _():
        form_paths(sizes, where, place, parts, spread, path, opening, basis, sems)

    inverse = 1.0 / length_ref[0, :1]
    rows = PIX
    first = scratch[3] if last else out_ref.at[0]
    transform(stage, positions, rows, inverse, path, opening, row_ref, first, scratch)
    if not last:
        return
    share = rows // waves
    for f in range(positions):
        lines = slice(f * rows, (f + 1) * rows)
        real, imag = columns_of(before[0, lines], first[lines], column_ref)
        intensity = real * real + imag * imag
        level = jnp.sum(
            jnp.sum(intensity, axis=0, keepdims=True), axis=1, keepdims=True
        ) / (rows * PIX)
        spectra = (intensity / (level + EPSILON)).astype(jnp.bfloat16)
        for part in range(waves):
            out_ref[part, 0, f * share : (f + 1) * share] = spectra[
                part * share : (part + 1) * share
            ]


def rows_kernel(stage, positions, rows, length_ref, path, opening, row_ref, *refs):
    inverse = 1.0 / length_ref[0, :1]
    if stage < len(STAGES) - 1:
        refs[1][...] = jnp.zeros_like(refs[1])
        transform(
            stage, positions, rows, inverse, path, opening, row_ref, refs[0].at[0], refs[2:]
        )
        return
    column_ref, before, image_ref, sum_ref = refs[:4]
    scratch = refs[4:]
    transform(stage, positions, rows, inverse, path, opening, row_ref, scratch[3], scratch)
    real, imag = columns_of(before[0], scratch[3][...], column_ref)
    intensity = real * real + imag * imag
    image_ref[0] = intensity
    sums = jnp.sum(intensity.reshape(positions, rows, PIX), axis=1)
    sum_ref[0] = jnp.broadcast_to(jnp.sum(sums, axis=1, keepdims=True), (positions, LANES))


def transform_scratch(positions, rows):
    return [
        pltpu.VMEM((2 * BAND, positions * LANES), jnp.bfloat16),
        pltpu.VMEM((2 * BAND, positions * LANES), jnp.bfloat16),
        pltpu.VMEM((2 * rows, positions * LANES), jnp.float32),
        pltpu.VMEM((positions * rows, 2 * WIDE), jnp.bfloat16),
    ]


def transform_cost(stage, lengths, positions, rows):
    share = len(chunks_of(stage))
    return pl.CostEstimate(
        flops=lengths * positions * share * (rows * PUP * PUP + rows * PUP * PIX + 10**7),
        bytes_accessed=8 * 2**20,
        transcendentals=0,
    )


def by_length(array, start=0):
    return pl.BlockSpec(
        (1,) + array.shape[1:], lambda l: (l + start,) + (0,) * (len(array.shape) - 1)
    )


def whole_fields(stage, own, got, spread, place, where, length, tables, sizes, tokens):
    positions, modes, waves, half, slabs = sizes
    keys = tuple((h, masks) for h, _, masks in got)
    arrays = [array for _, array, _ in got]
    lengths = length.shape[0]
    units = place.shape[0]
    share = positions * PIX // waves
    any_memory = pl.BlockSpec(memory_space=pl.ANY)
    if stage < len(STAGES) - 1:
        out_shape = jax.ShapeDtypeStruct((lengths, positions * PIX, 2 * WIDE), jnp.bfloat16)
        out_spec = by_length(out_shape)
    else:
        out_shape = jax.ShapeDtypeStruct((waves, lengths, share, PIX), jnp.bfloat16)
        out_spec = pl.BlockSpec((waves, 1, share, PIX), lambda l: (0, l, 0, 0))
    return pl.pallas_call(
        functools.partial(
            whole_kernel, stage, (positions, modes, waves, half, slabs, keys), len(tokens)
        ),
        grid=(lengths,),
        out_shape=(
            out_shape,
            jax.ShapeDtypeStruct((units, positions * ROWS, LANES), jnp.float32),
            jax.ShapeDtypeStruct((units, ROWS, LANES), jnp.float32),
        ),
        in_specs=[by_length(length), SMEM, SMEM]
        + [any_memory] * (1 + len(keys))
        + [VMEM]
        + [by_length(table) for table in tables]
        + [VMEM] * len(tokens),
        out_specs=(out_spec, VMEM, VMEM),
        scratch_shapes=[
            pltpu.VMEM((waves * slabs, ROWS, LANES), jnp.bfloat16),
            pltpu.SemaphoreType.DMA((1 + sum(len(masks) for _, masks in keys) * (waves - 1),)),
        ]
        + transform_scratch(positions, PIX),
        cost_estimate=transform_cost(stage, lengths, positions, PIX),
        compiler_params=pltpu.CompilerParams(vmem_limit_bytes=VMEM_BYTES),
    )(length, place, where, own, *arrays, spread, *tables, *tokens)


def row_fields(stage, path, opening, length, tables, positions, part):
    start, stop, _ = part.indices(length.shape[0])
    lengths = stop - start
    rows = tables[0].shape[2] // 2
    if stage < len(STAGES) - 1:
        out_shape = (
            jax.ShapeDtypeStruct((lengths, positions * rows, 2 * WIDE), jnp.bfloat16),
            jax.ShapeDtypeStruct((8, LANES), jnp.float32),
        )
        out_specs = (by_length(out_shape[0]), pl.BlockSpec((8, LANES), lambda l: (0, 0)))
    else:
        out_shape = (
            jax.ShapeDtypeStruct((lengths, positions * rows, PIX), jnp.float32),
            jax.ShapeDtypeStruct((lengths, positions, LANES), jnp.float32),
        )
        out_specs = tuple(by_length(one) for one in out_shape)
    return pl.pallas_call(
        functools.partial(rows_kernel, stage, positions, rows),
        grid=(lengths,),
        out_shape=out_shape,
        in_specs=[by_length(length, start), VMEM, VMEM]
        + [by_length(table, start) for table in tables],
        out_specs=out_specs,
        scratch_shapes=transform_scratch(positions, rows),
        cost_estimate=transform_cost(stage, lengths, positions, rows),
        compiler_params=pltpu.CompilerParams(vmem_limit_bytes=VMEM_BYTES),
    )(length, path, opening, *tables)


def mix_kernel(sum_ref, weight_ref, sent_ref, image_ref, out_ref):
    count, templates, rows = out_ref.shape[:3]
    for i in range(count):
        f = pl.program_id(0) * count + i
        inverse = [
            1.0 / (sum_ref[l, pl.ds(f, 1)] / (PIX * PIX) + EPSILON)
            for l in range(image_ref.shape[0])
        ]
        inverse = [jnp.concatenate([one] * (PIX // LANES), axis=1) for one in inverse]
        blocks = []
        for start in range(i * rows, (i + 1) * rows, ROWS):
            lines = slice(start, start + ROWS)
            blocks.append(
                jnp.concatenate(
                    [sent_ref[l, lines] for l in range(sent_ref.shape[0])]
                    + [
                        (image_ref[l, lines] * inverse[l]).astype(jnp.bfloat16)
                        for l in range(image_ref.shape[0])
                    ],
                    axis=0,
                )
            )
        mixed = jnp.dot(
            weight_ref[i], jnp.concatenate(blocks, axis=1), preferred_element_type=jnp.float32
        ).astype(jnp.bfloat16)
        for n in range(len(blocks)):
            for j in range(templates):
                out_ref[i, j, n * ROWS : (n + 1) * ROWS] = mixed[
                    j * ROWS : (j + 1) * ROWS, n * PIX : (n + 1) * PIX
                ]


def mix(spread, sums, sent, images, templates, rows):
    positions = spread.shape[0]
    count = 2 if positions % 2 == 0 else 1
    return pl.pallas_call(
        mix_kernel,
        grid=(positions // count,),
        out_shape=jax.ShapeDtypeStruct((positions, templates, rows, PIX), jnp.bfloat16),
        in_specs=[
            VMEM,
            pl.BlockSpec((count,) + spread.shape[1:], lambda f: (f, 0, 0)),
            pl.BlockSpec((sent.shape[0], count * rows, PIX), lambda f: (0, f, 0)),
            pl.BlockSpec((images.shape[0], count * rows, PIX), lambda f: (0, f, 0)),
        ],
        out_specs=pl.BlockSpec((count, templates, rows, PIX), lambda f: (f, 0, 0, 0)),
        compiler_params=pltpu.CompilerParams(vmem_limit_bytes=24 * 2**20),
    )(sums, spread, sent, images)


def table_kernel(length_ref, y_ref, v_ref, u_ref, x_ref, row_ref, column_ref, token_ref):
    scale = (SAMPLING / (2.0 * PUP)) / length_ref[0, :1]
    scale = jnp.concatenate([scale] * (PIX // LANES), axis=1)
    token_ref[...] = jnp.zeros_like(token_ref)
    for start in range(0, PUP, ROWS):
        s, k = half_turn((y_ref[start : start + ROWS] * v_ref[...]) * scale)
        cosine, sine = 1.0 - s * s, s * k
        lower = start // WIDE * 2 * WIDE + start % WIDE
        lower, upper = slice(lower, lower + ROWS), slice(lower + WIDE, lower + WIDE + ROWS)
        column_ref[0, lower, :PIX] = cosine.astype(jnp.bfloat16)
        column_ref[0, lower, PIX:] = (-sine).astype(jnp.bfloat16)
        column_ref[0, upper, :PIX] = sine.astype(jnp.bfloat16)
        column_ref[0, upper, PIX:] = cosine.astype(jnp.bfloat16)
    rows = u_ref.shape[0]
    imag = (lax.broadcasted_iota(jnp.int32, (ROWS, 2 * BAND), 1) // ROWS) % 2 == 1
    for band in range(BANDS):
        for start in range(0, rows, ROWS):
            s, k = half_turn((u_ref[start : start + ROWS] * x_ref[band]) * scale)
            cosine, sine = 1.0 - s * s, s * k
            row_ref[0, band, start : start + ROWS] = jnp.where(imag, sine, cosine).astype(
                jnp.bfloat16
            )
            row_ref[0, band, rows + start : rows + start + ROWS] = jnp.where(
                imag, cosine, -sine
            ).astype(jnp.bfloat16)


def tables(length, first_row, rows):
    lengths = length.shape[0]
    y = 2 * np.concatenate([band_columns(band) for stage in STAGES for band in stage]) - PUP + 1
    v = np.arange(PIX) - PIX // 2
    u = first_row + jnp.arange(rows, dtype=jnp.int32) - PIX // 2
    x = np.array(
        [[row + i for row in band_rows(band) for i in range(ROWS)] for band in range(BANDS)]
    )
    x = np.repeat(x.reshape(BANDS, UNITS, 1, ROWS), 2, axis=2).reshape(BANDS, 1, 2 * BAND)
    whole = lambda *shape: pl.BlockSpec(shape, lambda l: (0,) * len(shape))
    return pl.pallas_call(
        table_kernel,
        grid=(lengths,),
        out_shape=(
            jax.ShapeDtypeStruct((lengths, BANDS, 2 * rows, 2 * BAND), jnp.bfloat16),
            jax.ShapeDtypeStruct((lengths, 2 * PUP, 2 * PIX), jnp.bfloat16),
            jax.ShapeDtypeStruct((8, LANES), jnp.float32),
        ),
        in_specs=[
            pl.BlockSpec((1, 8, LANES), lambda l: (l, 0, 0)),
            whole(PUP, 1),
            whole(1, PIX),
            whole(rows, 1),
            whole(BANDS, 1, 2 * BAND),
        ],
        out_specs=(
            pl.BlockSpec((1, BANDS, 2 * rows, 2 * BAND), lambda l: (l, 0, 0, 0)),
            pl.BlockSpec((1, 2 * PUP, 2 * PIX), lambda l: (l, 0, 0)),
            whole(8, LANES),
        ),
        cost_estimate=pl.CostEstimate(
            flops=lengths * 30 * PUP * PIX, bytes_accessed=lengths * 4 * PUP * PIX * 2, transcendentals=0
        ),
        compiler_params=pltpu.CompilerParams(vmem_limit_bytes=VMEM_BYTES),
    )(
        length,
        jnp.asarray(y[:, None].astype(np.float32)),
        jnp.asarray(v[None, :].astype(np.float32)),
        u.astype(jnp.float32)[:, None],
        jnp.asarray((2 * x - PUP + 1).astype(np.float32)),
    )


def add_over_wave(x, waves):
    step = 1
    while step < waves:
        x = x + lax.ppermute(x, "wave", [(i, i ^ step) for i in range(waves)])
        step *= 2
    return x


def local(mode_basis, coef_table, table_index, wave_lengths, sed_table, template_ids):
    waves = lax.axis_size("wave")
    mine = lax.axis_index("wave")
    modes = mode_basis.shape[0]
    positions = table_index.shape[0]
    rows = PIX // waves
    lengths = wave_lengths.shape[0]
    sent_lengths = lengths // 2

    share = (lax.axis_index("groups") % 2) * 4 + lax.axis_index("field") % 4
    where = jnp.stack([mine, share]).astype(jnp.int32)
    plans = [layout(waves, modes, stage) for stage in range(len(STAGES))]
    *owns, piece = pack_rows(mode_basis, wave_lengths, plans, where)
    parts = along_wave(piece, waves)

    selector = (
        table_index[:, None] == jnp.arange(coef_table.shape[0], dtype=jnp.int32)[None, :]
    ).astype(jnp.bfloat16)
    coeffs = jnp.dot(selector, coef_table, preferred_element_type=jnp.float32)
    one_hot = (
        template_ids[:, :, None]
        == jnp.arange(sed_table.shape[0], dtype=jnp.int32)[None, None, :]
    ).astype(jnp.float32)
    raw_weights = jnp.einsum("fjn,nl->fjl", one_hot, sed_table, precision=lax.Precision.HIGHEST)
    weights = (raw_weights / jnp.sum(raw_weights, axis=2, keepdims=True)).astype(jnp.bfloat16)
    templates = weights.shape[1]
    split = weights.reshape(positions, templates, waves, lengths)
    weights = jnp.concatenate(
        [
            split[..., :sent_lengths].reshape(positions, templates, -1),
            split[..., sent_lengths:].reshape(positions, templates, -1),
        ],
        axis=2,
    )
    path_spread, mix_spread, spread_token = spreads(coeffs.astype(jnp.bfloat16)[None], weights)
    own_length = jnp.broadcast_to(
        wave_lengths[:sent_lengths, None, None], (sent_lengths, 8, LANES)
    )
    own_row, own_column, own_token = tables(own_length, 0, PIX)

    low, high, second, every = split_parts(
        parts,
        where,
        wave_lengths,
        (plans[0][0], plans[1][0]),
        sent_lengths,
        (spread_token, own_token),
    )
    all_row, all_column, all_token = tables(every, mine * rows, rows)
    got = gather_halves((low, high), all_token)
    (second,) = after(
        [second], [array[0, :8] for _, array, masks in got if masks in ((2, 6), (4, 6))]
    )

    def sizes(stage):
        half, slabs, _, _ = plans[stage]
        return positions, modes, waves, half, slabs

    before, path, opening = whole_fields(
        0, owns[0], got, path_spread, plans[0][3], where, own_length, (own_row,), sizes(0),
        (second[0, :8],),
    )
    got, there = send_direct(second)
    cut = every.shape[0] // 2
    rows_before = []
    for n, part in enumerate((slice(0, cut), slice(cut, None))):
        one, rows_token = row_fields(0, path, opening, every, (all_row,), positions, part)
        rows_before.append(one)
        if n == 0:
            got = end_direct(got, there, rows_token)
    spectra, path, opening = whole_fields(
        1, owns[1], got, path_spread, plans[1][3], where, own_length,
        (own_row, own_column, before), sizes(1), (rows_token,),
    )
    sent = lax.all_to_all(spectra, "wave", split_axis=0, concat_axis=0, tiled=True)
    sent = sent.reshape(waves * sent_lengths, positions * rows, PIX)
    images, sums = row_fields(
        1,
        path,
        opening,
        every,
        (all_row, all_column, jnp.concatenate(rows_before)),
        positions,
        slice(None),
    )
    return mix(mix_spread, add_over_wave(sums, waves), sent, images, templates, rows)


def solution(mesh):
    return jax.shard_map(
        local,
        mesh=mesh,
        in_specs=(
            P(None, "wave", None),
            P(),
            P(("groups", "field")),
            P("wave"),
            P(),
            P(("groups", "field"), None),
        ),
        out_specs=P(("groups", "field"), None, "wave", None),
        check_vma=False,
    )
```

```python
import functools
import math

import jax
import jax.numpy as jnp
import numpy as np
from jax import lax
from jax.experimental import pallas as pl
from jax.experimental.pallas import tpu as pltpu
from jax.sharding import PartitionSpec as P

PUP = 512
PIX = 256
TWO_PI = 2.0 * math.pi
SAMPLING = 0.25
EPSILON = 1e-06
INNER = 61 * PUP // 100
BAND = 128
BANDS = PUP // BAND
ROWS = 16
LANES = 128
UNITS = BAND // ROWS
VMEM_BYTES = 60 * 2**20
SHARES = 8

SMEM = pl.BlockSpec(memory_space=pltpu.SMEM)
VMEM = pl.BlockSpec(memory_space=pltpu.VMEM)

SIN_POLY = (4.4428679, -7.30744341, 3.59478797, -0.78437376)
COS_POLY = (1.4142135, -6.97885099, 5.73946117, -1.88356298, 0.31069817)


def half_turn(turns):
    magic = jnp.float32(12582912.0)
    r = turns - ((turns + magic) - magic)
    z = r * r
    s = jnp.float32(SIN_POLY[-1])
    for value in SIN_POLY[-2::-1]:
        s = s * z + value
    k = jnp.float32(COS_POLY[-1])
    for value in COS_POLY[-2::-1]:
        k = k * z + value
    return s * r, k


def band_rows(band):
    low, high = PUP // 2 - 64 * (band + 1), PUP // 2 + 64 * band
    return [low + ROWS * i for i in range(4)] + [high + ROWS * i for i in range(4)]


def band_columns(band):
    low, high = PUP // 2 - 64 * (band + 1), PUP // 2 + 64 * band
    sides = (high, low) if band % 2 == 0 else (low, high)
    return np.concatenate([side + np.arange(64) for side in sides])


def unit_open(row, band):
    a = 2 * (row + np.arange(ROWS)) - PUP + 1
    b = 2 * band_columns(band) - PUP + 1
    radius = a[:, None] ** 2 + b[None, :] ** 2
    return bool(np.any((radius <= PUP * PUP) & (radius >= INNER * INNER)))


CHUNKS = [
    (band, rows)
    for band in range(BANDS)
    for rows in range(BANDS)
    if any(unit_open(row, band) for row in band_rows(rows))
]


@functools.lru_cache(None)
def layout(waves, modes):
    per = PUP // waves
    lists = []
    for wave in range(waves):
        lists.append(
            [
                (band, row)
                for band in range(BANDS)
                for row in range(wave * per, (wave + 1) * per, ROWS)
                if unit_open(row, band)
            ]
        )
    count = max(len(one) for one in lists)
    half = -(-count * modes // (2 * SHARES))
    slabs = 2 * SHARES * half
    pack = np.zeros((waves, count, 3), np.int32)
    for wave, one in enumerate(lists):
        for i, (band, row) in enumerate(one):
            columns = band_columns(band)
            pack[wave, i] = (columns[0] // LANES * LANES, columns[64] // LANES * LANES, row - wave * per)
    place = np.zeros((len(CHUNKS) * UNITS, 4), np.int32)
    for c, (band, rows) in enumerate(CHUNKS):
        columns = band_columns(band)
        for j, row in enumerate(band_rows(rows)):
            wave = row // per
            slab = 0
            if (band, row) in lists[wave]:
                slab = wave * slabs + lists[wave].index((band, row)) * modes
            place[c * UNITS + j] = (slab, row, columns[0], columns[64] - 64)
    return half, slabs, pack, place


def pack_kernel(count, half, modes, where, table, lengths, basis, own, piece):
    left = lax.broadcasted_iota(jnp.int32, (ROWS, LANES), 1) < 64
    wave, share = where[0], where[1]

    def unit(i, carry):
        first = pl.multiple_of(table[wave * count + i, 0], LANES)
        second = pl.multiple_of(table[wave * count + i, 1], LANES)
        row = pl.multiple_of(table[wave * count + i, 2], ROWS)
        for k in range(modes):
            one = basis[k, pl.ds(row, ROWS), pl.ds(first, LANES)].astype(jnp.float32)
            two = basis[k, pl.ds(row, ROWS), pl.ds(second, LANES)].astype(jnp.float32)
            own[i * modes + k] = jnp.where(left, one, two).astype(own.dtype)
        return carry

    lax.fori_loop(0, count, unit, 0)
    for n in range(count * modes, own.shape[0]):
        own[n] = jnp.zeros((ROWS, LANES), own.dtype)
    piece[: 2 * half] = own[pl.ds(share * (2 * half), 2 * half)]
    line = lax.broadcasted_iota(jnp.int32, (ROWS, LANES), 0)
    slab = jnp.zeros((ROWS, LANES), jnp.float32)
    for i in range(lengths.shape[0]):
        rest = jnp.full((ROWS, LANES), lengths[i], jnp.float32)
        for limb in range(3):
            value = rest.astype(jnp.bfloat16).astype(jnp.float32)
            slab = jnp.where(line == 3 * i + limb, value, slab)
            rest = rest - value
    piece[2 * half] = slab.astype(piece.dtype)


def pack_rows(basis, wave_lengths, plan, where):
    half, slabs, table, _ = plan
    tile = (ROWS, LANES)
    return pl.pallas_call(
        functools.partial(pack_kernel, table.shape[1], half, basis.shape[0]),
        out_shape=(
            jax.ShapeDtypeStruct((slabs,) + tile, basis.dtype),
            jax.ShapeDtypeStruct((2 * half + 1,) + tile, basis.dtype),
        ),
        in_specs=[SMEM, SMEM, SMEM, VMEM],
        out_specs=(VMEM, VMEM),
        compiler_params=pltpu.CompilerParams(vmem_limit_bytes=VMEM_BYTES),
    )(where, table.reshape(-1, 3), wave_lengths, basis)


def split_kernel(half, sent, parts_count, where, own_lengths, *refs):
    parts, (low_ref, high_ref, length_ref) = refs[:parts_count], refs[-3:]
    wave, waves = where[0], parts_count + 1
    kept = own_lengths.shape[0] - sent
    for s in range(waves):
        for i in range(kept):
            if s == 0:
                value = jnp.full((8, LANES), own_lengths[sent + i], jnp.float32)
            else:
                slab = parts[s - 1][2 * half].astype(jnp.float32)
                line = 3 * (sent + i)
                value = (slab[line : line + 1] + slab[line + 1 : line + 2]) + slab[
                    line + 2 : line + 3
                ]
                value = jnp.broadcast_to(value, (8, LANES))
            length_ref[lax.rem(wave + (waves - s), waves) * kept + i] = value
    for s, part in enumerate(parts):
        low_ref[s * half : (s + 1) * half] = part[:half]
        high_ref[s * half : (s + 1) * half] = part[half : 2 * half]


def split_parts(parts, where, wave_lengths, half, sent, tokens):
    count = (len(parts) + 1) * (wave_lengths.shape[0] - sent)
    slabs = jax.ShapeDtypeStruct((len(parts) * half, ROWS, LANES), parts[0].dtype)
    return pl.pallas_call(
        functools.partial(split_kernel, half, sent, len(parts)),
        out_shape=(slabs, slabs, jax.ShapeDtypeStruct((count, 8, LANES), jnp.float32)),
        in_specs=[SMEM, SMEM] + [VMEM] * (len(parts) + len(tokens)),
        out_specs=(VMEM,) * 3,
        compiler_params=pltpu.CompilerParams(vmem_limit_bytes=VMEM_BYTES),
    )(where, wave_lengths, *parts, *tokens)


def join_kernel(pairs, *refs):
    for i in range(pairs):
        one, two, out = refs[2 * i], refs[2 * i + 1], refs[i - pairs]
        out[: one.shape[0]] = one[...]
        out[one.shape[0] :] = two[...]


def join(pairs, token):
    return pl.pallas_call(
        functools.partial(join_kernel, len(pairs)),
        out_shape=tuple(
            jax.ShapeDtypeStruct((2 * one.shape[0],) + one.shape[1:], one.dtype) for one, _ in pairs
        ),
        in_specs=[VMEM] * (2 * len(pairs) + 1),
        out_specs=(VMEM,) * len(pairs),
        compiler_params=pltpu.CompilerParams(vmem_limit_bytes=VMEM_BYTES),
    )(*[one for pair in pairs for one in pair], token)


def along_wave(piece, waves):
    return [
        lax.ppermute(piece, "wave", [(i, (i + s) % waves) for i in range(waves)])
        for s in range(1, waves)
    ]


def swap(x, mask):
    groups, fields = lax.axis_size("groups"), lax.axis_size("field")
    pairs = [
        (g * fields + f, (g ^ (mask >> 2)) * fields + (f ^ (mask & 3)))
        for g in range(groups)
        for f in range(fields)
    ]
    return lax.ppermute(x, ("groups", "field"), pairs)


def gather_halves(halves, token):
    got = []
    routes = ((2, 4), (4, 2))
    joined = join([(mine, swap(mine, one)) for mine, (one, _) in zip(halves, routes)], token)
    for h, (both, (one, two)) in enumerate(zip(joined, routes)):
        far = swap(both, two)
        got.append((h, both, (0, one)))
        got.append((h, far, (two, one | two)))
        got.append((h, swap(both, 1), (1, one | 1)))
        got.append((h, swap(far, 1), (two | 1, one | two | 1)))
    return got


def spread_kernel(*refs):
    count = len(refs) // 2
    refs[-1][...] = jnp.zeros_like(refs[-1])
    for small_ref, big_ref in zip(refs[:count], refs[count:-1]):
        _, many, wide = small_ref.shape
        tall, long = many * ROWS, wide * ROWS
        down = lax.broadcasted_iota(jnp.int32, (tall, many), 0) // ROWS
        down = (down == lax.broadcasted_iota(jnp.int32, (tall, many), 1)).astype(jnp.float32)
        along = lax.broadcasted_iota(jnp.int32, (wide, long), 1) // ROWS
        along = (along == lax.broadcasted_iota(jnp.int32, (wide, long), 0)).astype(jnp.float32)
        same = (lax.broadcasted_iota(jnp.int32, (tall, long), 0) % ROWS) == (
            lax.broadcasted_iota(jnp.int32, (tall, long), 1) % ROWS
        )
        down, along = down.astype(jnp.bfloat16), along.astype(jnp.bfloat16)
        for i in range(small_ref.shape[0]):
            half = jnp.dot(down, small_ref[i], preferred_element_type=jnp.float32)
            whole = jnp.dot(half.astype(jnp.bfloat16), along, preferred_element_type=jnp.float32)
            big_ref[i] = jnp.where(same, whole, 0.0).astype(jnp.bfloat16)


def spreads(*matrices):
    return pl.pallas_call(
        spread_kernel,
        out_shape=tuple(
            jax.ShapeDtypeStruct((m.shape[0], m.shape[1] * ROWS, m.shape[2] * ROWS), jnp.bfloat16)
            for m in matrices
        )
        + (jax.ShapeDtypeStruct((8, LANES), jnp.float32),),
        compiler_params=pltpu.CompilerParams(vmem_limit_bytes=VMEM_BYTES),
    )(*matrices)


def form_paths(sizes, where, place, parts, spread, path, opening, basis, sems):
    positions, modes, waves, half, slabs, keys = sizes
    wave, share = where[0], where[1]
    copies = [pltpu.make_async_copy(parts[0], basis.at[pl.ds(wave * slabs, slabs)], sems.at[0])]
    n = 1
    for (h, masks), part in zip(keys, parts[1:]):
        for m, mask in enumerate(masks):
            for s in range(1, waves):
                source = lax.rem(wave + (waves - s), waves)
                start = source * slabs + (share ^ mask) * (2 * half) + h * half
                copies.append(
                    pltpu.make_async_copy(
                        part.at[pl.ds((m * (waves - 1) + s - 1) * half, half)],
                        basis.at[pl.ds(start, half)],
                        sems.at[n],
                    )
                )
                n += 1
    for copy in copies:
        copy.start()
    for copy in copies:
        copy.wait()

    lane = lax.broadcasted_iota(jnp.int32, (ROWS, LANES), 1)
    line = lax.broadcasted_iota(jnp.int32, (ROWS, LANES), 0)

    def chunk(c, carry):
        values = jnp.concatenate(
            [
                basis[pl.ds(place[c * UNITS + j, 0], modes)].reshape(modes * ROWS, LANES)
                for j in range(UNITS)
            ],
            axis=1,
        )
        found = jnp.dot(spread[0], values, preferred_element_type=jnp.float32)
        for j in range(UNITS):
            u = c * UNITS + j
            a = 2 * (line + place[u, 1]) - (PUP - 1)
            b = 2 * (lane + jnp.where(lane < 64, place[u, 2], place[u, 3])) - (PUP - 1)
            radius = a * a + b * b
            inside = (radius <= PUP * PUP) & (radius >= INNER * INNER)
            opening[u] = jnp.where(inside, 1.0, 0.0)
            for f in range(positions):
                path[u, f * ROWS : (f + 1) * ROWS] = jnp.where(
                    inside, found[f * ROWS : (f + 1) * ROWS, j * LANES : (j + 1) * LANES], 0.0
                )
        return carry

    lax.fori_loop(0, place.shape[0] // UNITS, chunk, 0)


def transform(positions, rows, inverse, path, opening, row_ref, scratch, wait=None):
    pupils, total, first = scratch[:2], scratch[2], scratch[3]
    batch = max(1, positions // 2)
    width = 2 * positions * LANES // UNITS

    def finish(band, columns, value):
        for f in range(columns.start // LANES, columns.stop // LANES):
            lanes = slice(f * LANES - columns.start, (f + 1) * LANES - columns.start)
            for part in range(2):
                first[
                    f * rows : (f + 1) * rows,
                    part * PUP + band * LANES : part * PUP + (band + 1) * LANES,
                ] = value[part * rows : (part + 1) * rows, lanes].astype(jnp.bfloat16)

    def product(c, columns):
        band, rows_band = CHUNKS[c]
        value = jnp.dot(
            row_ref[0, rows_band], pupils[c % 2][:, columns], preferred_element_type=jnp.float32
        )
        if c > 0 and CHUNKS[c - 1][0] == band:
            value = value + total[:, columns]
        if c + 1 < len(CHUNKS) and CHUNKS[c + 1][0] == band:
            total[:, columns] = value
        else:
            finish(band, columns, value)

    for c, (band, rows_band) in enumerate(CHUNKS):
        pupil = pupils[c % 2]
        if wait is not None:
            wait(c)
        for j, row in enumerate(band_rows(rows_band)):
            real_lines = slice(2 * ROWS * j, 2 * ROWS * j + ROWS)
            imag_lines = slice(2 * ROWS * j + ROWS, 2 * ROWS * (j + 1))
            if unit_open(row, band):
                u = c * UNITS + j
                inside = opening[u]
                for f0 in range(0, positions, batch):
                    s, k = half_turn(path[u, f0 * ROWS : (f0 + batch) * ROWS] * inverse)
                    sine = s * k
                    square = s * s
                    for f in range(f0, f0 + batch):
                        columns = slice(f * LANES, (f + 1) * LANES)
                        lines = slice((f - f0) * ROWS, (f - f0 + 1) * ROWS)
                        pupil[real_lines, columns] = (inside - square[lines]).astype(jnp.bfloat16)
                        pupil[imag_lines, columns] = sine[lines].astype(jnp.bfloat16)
            else:
                empty = jnp.zeros((ROWS, positions * LANES), jnp.bfloat16)
                pupil[real_lines] = empty
                pupil[imag_lines] = empty
            if c > 0 and j % 2 == 1:
                product(c - 1, slice(j // 2 * width, (j // 2 + 1) * width))
    for n in range(positions * LANES // width):
        product(len(CHUNKS) - 1, slice(n * width, (n + 1) * width))


def columns_of(first, column_ref):
    return [
        jnp.dot(
            first, column_ref[0, :, part * PIX : (part + 1) * PIX], preferred_element_type=jnp.float32
        )
        for part in range(2)
    ]


def chunk_copies(source, target, sems):
    return [
        pltpu.make_async_copy(
            source.at[pl.ds(c * UNITS, UNITS)], target.at[pl.ds(c * UNITS, UNITS)], sems.at[c]
        )
        for c in range(len(CHUNKS))
    ]


def whole_kernel(sizes, length_ref, place, where, *refs):
    positions, modes, waves, half, slabs, keys = sizes
    parts, refs = refs[: 1 + len(keys)], refs[1 + len(keys) :]
    spread, row_ref, column_ref, out_ref, path_out, opening, path, basis, sems, path_sems = refs[:10]
    scratch = refs[10:]
    copies = chunk_copies(path, path_out, path_sems)

    @pl.when(pl.program_id(0) == 0)
    def _():
        form_paths(sizes, where, place, parts, spread, path, opening, basis, sems)
        for copy in copies:
            copy.start()

    rows = PIX
    transform(positions, rows, 1.0 / length_ref[0, :1], path, opening, row_ref, scratch)
    first = scratch[3]
    share = rows // waves
    for f in range(positions):
        real, imag = columns_of(first[f * rows : (f + 1) * rows], column_ref)
        intensity = real * real + imag * imag
        level = jnp.sum(
            jnp.sum(intensity, axis=0, keepdims=True), axis=1, keepdims=True
        ) / (rows * PIX)
        spectra = (intensity / (level + EPSILON)).astype(jnp.bfloat16)
        for part in range(waves):
            out_ref[part, 0, f * share : (f + 1) * share] = spectra[
                part * share : (part + 1) * share
            ]

    @pl.when(pl.program_id(0) == pl.num_programs(0) - 1)
    def _():
        for copy in copies:
            copy.wait()


def rows_kernel(positions, rows, length_ref, path_in, opening, row_ref, column_ref, *refs):
    image_ref, sum_ref, path, path_sems = refs[:4]
    scratch = refs[4:]
    copies = chunk_copies(path_in, path, path_sems)
    begin = pl.program_id(0) == 0

    @pl.when(begin)
    def _():
        for copy in copies:
            copy.start()

    def wait(c):
        @pl.when(begin)
        def _():
            copies[c].wait()

    transform(positions, rows, 1.0 / length_ref[0, :1], path, opening, row_ref, scratch, wait)
    real, imag = columns_of(scratch[3][...], column_ref)
    intensity = real * real + imag * imag
    image_ref[0] = intensity
    sums = jnp.sum(intensity.reshape(positions, rows, PIX), axis=1)
    sum_ref[0] = jnp.broadcast_to(jnp.sum(sums, axis=1, keepdims=True), (positions, LANES))


def transform_scratch(positions, rows):
    return [
        pltpu.VMEM((2 * BAND, positions * LANES), jnp.bfloat16),
        pltpu.VMEM((2 * BAND, positions * LANES), jnp.bfloat16),
        pltpu.VMEM((2 * rows, positions * LANES), jnp.float32),
        pltpu.VMEM((positions * rows, 2 * PUP), jnp.bfloat16),
    ]


def transform_cost(lengths, positions, rows):
    return pl.CostEstimate(
        flops=lengths * positions * (rows * 8 * PUP * PUP + rows * 8 * PUP * PIX + 10**8),
        bytes_accessed=8 * 2**20,
        transcendentals=0,
    )


def by_length(array):
    return pl.BlockSpec((1,) + array.shape[1:], lambda l: (l,) + (0,) * (len(array.shape) - 1))


def path_shape(positions):
    return (len(CHUNKS) * UNITS, positions * ROWS, LANES)


def whole_fields(own, got, spread, place, where, length, tables, sizes):
    positions, modes, waves, half, slabs = sizes
    keys = tuple((h, masks) for h, _, masks in got)
    arrays = [array for _, array, _ in got]
    lengths = length.shape[0]
    share = positions * PIX // waves
    any_memory = pl.BlockSpec(memory_space=pl.ANY)
    return pl.pallas_call(
        functools.partial(whole_kernel, (positions, modes, waves, half, slabs, keys)),
        grid=(lengths,),
        out_shape=(
            jax.ShapeDtypeStruct((waves, lengths, share, PIX), jnp.bfloat16),
            jax.ShapeDtypeStruct(path_shape(positions), jnp.float32),
            jax.ShapeDtypeStruct((place.shape[0], ROWS, LANES), jnp.float32),
        ),
        in_specs=[by_length(length), SMEM, SMEM]
        + [any_memory] * (1 + len(keys))
        + [VMEM]
        + [by_length(table) for table in tables],
        out_specs=(
            pl.BlockSpec((waves, 1, share, PIX), lambda l: (0, l, 0, 0)),
            any_memory,
            VMEM,
        ),
        scratch_shapes=[
            pltpu.VMEM(path_shape(positions), jnp.float32),
            pltpu.VMEM((waves * slabs, ROWS, LANES), jnp.bfloat16),
            pltpu.SemaphoreType.DMA((1 + sum(len(masks) for _, masks in keys) * (waves - 1),)),
            pltpu.SemaphoreType.DMA((len(CHUNKS),)),
        ]
        + transform_scratch(positions, PIX),
        cost_estimate=transform_cost(lengths, positions, PIX),
        compiler_params=pltpu.CompilerParams(vmem_limit_bytes=VMEM_BYTES),
    )(length, place, where, own, *arrays, spread, *tables)


def row_fields(path, opening, length, tables, positions):
    lengths = length.shape[0]
    rows = tables[0].shape[2] // 2
    out_shape = (
        jax.ShapeDtypeStruct((lengths, positions * rows, PIX), jnp.float32),
        jax.ShapeDtypeStruct((lengths, positions, LANES), jnp.float32),
    )
    return pl.pallas_call(
        functools.partial(rows_kernel, positions, rows),
        grid=(lengths,),
        out_shape=out_shape,
        in_specs=[by_length(length), pl.BlockSpec(memory_space=pl.ANY), VMEM]
        + [by_length(table) for table in tables],
        out_specs=tuple(by_length(one) for one in out_shape),
        scratch_shapes=[
            pltpu.VMEM(path_shape(positions), jnp.float32),
            pltpu.SemaphoreType.DMA((len(CHUNKS),)),
        ]
        + transform_scratch(positions, rows),
        cost_estimate=transform_cost(lengths, positions, rows),
        compiler_params=pltpu.CompilerParams(vmem_limit_bytes=VMEM_BYTES),
    )(length, path, opening, *tables)


def mix_kernel(sum_ref, weight_ref, sent_ref, image_ref, out_ref):
    count, templates, rows = out_ref.shape[:3]
    for i in range(count):
        f = pl.program_id(0) * count + i
        inverse = [
            1.0 / (sum_ref[l, pl.ds(f, 1)] / (PIX * PIX) + EPSILON)
            for l in range(image_ref.shape[0])
        ]
        inverse = [jnp.concatenate([one] * (PIX // LANES), axis=1) for one in inverse]
        blocks = []
        for start in range(i * rows, (i + 1) * rows, ROWS):
            lines = slice(start, start + ROWS)
            blocks.append(
                jnp.concatenate(
                    [sent_ref[l, lines] for l in range(sent_ref.shape[0])]
                    + [
                        (image_ref[l, lines] * inverse[l]).astype(jnp.bfloat16)
                        for l in range(image_ref.shape[0])
                    ],
                    axis=0,
                )
            )
        mixed = jnp.dot(
            weight_ref[i], jnp.concatenate(blocks, axis=1), preferred_element_type=jnp.float32
        ).astype(jnp.bfloat16)
        for n in range(len(blocks)):
            for j in range(templates):
                out_ref[i, j, n * ROWS : (n + 1) * ROWS] = mixed[
                    j * ROWS : (j + 1) * ROWS, n * PIX : (n + 1) * PIX
                ]


def mix(spread, sums, sent, images, templates, rows):
    positions = spread.shape[0]
    count = 2 if positions % 2 == 0 else 1
    return pl.pallas_call(
        mix_kernel,
        grid=(positions // count,),
        out_shape=jax.ShapeDtypeStruct((positions, templates, rows, PIX), jnp.bfloat16),
        in_specs=[
            VMEM,
            pl.BlockSpec((count,) + spread.shape[1:], lambda f: (f, 0, 0)),
            pl.BlockSpec((sent.shape[0], count * rows, PIX), lambda f: (0, f, 0)),
            pl.BlockSpec((images.shape[0], count * rows, PIX), lambda f: (0, f, 0)),
        ],
        out_specs=pl.BlockSpec((count, templates, rows, PIX), lambda f: (f, 0, 0, 0)),
        compiler_params=pltpu.CompilerParams(vmem_limit_bytes=24 * 2**20),
    )(sums, spread, sent, images)


def table_kernel(length_ref, y_ref, v_ref, u_ref, x_ref, row_ref, column_ref, token_ref):
    scale = (SAMPLING / (2.0 * PUP)) / length_ref[0, :1]
    scale = jnp.concatenate([scale] * (PIX // LANES), axis=1)
    token_ref[...] = jnp.zeros_like(token_ref)
    for start in range(0, PUP, ROWS):
        s, k = half_turn((y_ref[start : start + ROWS] * v_ref[...]) * scale)
        cosine, sine = 1.0 - s * s, s * k
        lower, upper = slice(start, start + ROWS), slice(PUP + start, PUP + start + ROWS)
        column_ref[0, lower, :PIX] = cosine.astype(jnp.bfloat16)
        column_ref[0, lower, PIX:] = (-sine).astype(jnp.bfloat16)
        column_ref[0, upper, :PIX] = sine.astype(jnp.bfloat16)
        column_ref[0, upper, PIX:] = cosine.astype(jnp.bfloat16)
    rows = u_ref.shape[0]
    imag = (lax.broadcasted_iota(jnp.int32, (ROWS, 2 * BAND), 1) // ROWS) % 2 == 1
    for band in range(BANDS):
        for start in range(0, rows, ROWS):
            s, k = half_turn((u_ref[start : start + ROWS] * x_ref[band]) * scale)
            cosine, sine = 1.0 - s * s, s * k
            row_ref[0, band, start : start + ROWS] = jnp.where(imag, sine, cosine).astype(
                jnp.bfloat16
            )
            row_ref[0, band, rows + start : rows + start + ROWS] = jnp.where(
                imag, cosine, -sine
            ).astype(jnp.bfloat16)


def tables(length, first_row, rows):
    lengths = length.shape[0]
    y = 2 * np.concatenate([band_columns(band) for band in range(BANDS)]) - PUP + 1
    v = np.arange(PIX) - PIX // 2
    u = first_row + jnp.arange(rows, dtype=jnp.int32) - PIX // 2
    x = np.array(
        [[row + i for row in band_rows(band) for i in range(ROWS)] for band in range(BANDS)]
    )
    x = np.repeat(x.reshape(BANDS, UNITS, 1, ROWS), 2, axis=2).reshape(BANDS, 1, 2 * BAND)
    whole = lambda *shape: pl.BlockSpec(shape, lambda l: (0,) * len(shape))
    return pl.pallas_call(
        table_kernel,
        grid=(lengths,),
        out_shape=(
            jax.ShapeDtypeStruct((lengths, BANDS, 2 * rows, 2 * BAND), jnp.bfloat16),
            jax.ShapeDtypeStruct((lengths, 2 * PUP, 2 * PIX), jnp.bfloat16),
            jax.ShapeDtypeStruct((8, LANES), jnp.float32),
        ),
        in_specs=[
            pl.BlockSpec((1, 8, LANES), lambda l: (l, 0, 0)),
            whole(PUP, 1),
            whole(1, PIX),
            whole(rows, 1),
            whole(BANDS, 1, 2 * BAND),
        ],
        out_specs=(
            pl.BlockSpec((1, BANDS, 2 * rows, 2 * BAND), lambda l: (l, 0, 0, 0)),
            pl.BlockSpec((1, 2 * PUP, 2 * PIX), lambda l: (l, 0, 0)),
            whole(8, LANES),
        ),
        cost_estimate=pl.CostEstimate(
            flops=lengths * 30 * PUP * PIX, bytes_accessed=lengths * 4 * PUP * PIX * 2, transcendentals=0
        ),
        compiler_params=pltpu.CompilerParams(vmem_limit_bytes=VMEM_BYTES),
    )(
        length,
        jnp.asarray(y[:, None].astype(np.float32)),
        jnp.asarray(v[None, :].astype(np.float32)),
        u.astype(jnp.float32)[:, None],
        jnp.asarray((2 * x - PUP + 1).astype(np.float32)),
    )


def add_over_wave(x, waves):
    step = 1
    while step < waves:
        x = x + lax.ppermute(x, "wave", [(i, i ^ step) for i in range(waves)])
        step *= 2
    return x


def local(mode_basis, coef_table, table_index, wave_lengths, sed_table, template_ids):
    waves = lax.axis_size("wave")
    mine = lax.axis_index("wave")
    modes = mode_basis.shape[0]
    positions = table_index.shape[0]
    rows = PIX // waves
    lengths = wave_lengths.shape[0]
    sent_lengths = lengths // 2

    share = (lax.axis_index("groups") % 2) * 4 + lax.axis_index("field") % 4
    where = jnp.stack([mine, share]).astype(jnp.int32)
    plan = layout(waves, modes)
    half, slabs, _, place = plan
    own, piece = pack_rows(mode_basis, wave_lengths, plan, where)
    parts = along_wave(piece, waves)

    selector = (
        table_index[:, None] == jnp.arange(coef_table.shape[0], dtype=jnp.int32)[None, :]
    ).astype(jnp.bfloat16)
    coeffs = jnp.dot(selector, coef_table, preferred_element_type=jnp.float32)
    one_hot = (
        template_ids[:, :, None]
        == jnp.arange(sed_table.shape[0], dtype=jnp.int32)[None, None, :]
    ).astype(jnp.float32)
    raw_weights = jnp.einsum("fjn,nl->fjl", one_hot, sed_table, precision=lax.Precision.HIGHEST)
    weights = (raw_weights / jnp.sum(raw_weights, axis=2, keepdims=True)).astype(jnp.bfloat16)
    templates = weights.shape[1]
    split = weights.reshape(positions, templates, waves, lengths)
    weights = jnp.concatenate(
        [
            split[..., :sent_lengths].reshape(positions, templates, -1),
            split[..., sent_lengths:].reshape(positions, templates, -1),
        ],
        axis=2,
    )
    path_spread, mix_spread, spread_token = spreads(coeffs.astype(jnp.bfloat16)[None], weights)
    own_length = jnp.broadcast_to(
        wave_lengths[:sent_lengths, None, None], (sent_lengths, 8, LANES)
    )
    own_row, own_column, own_token = tables(own_length, 0, PIX)

    low, high, every = split_parts(
        parts, where, wave_lengths, half, sent_lengths, (spread_token, own_token)
    )
    all_row, all_column, all_token = tables(every, mine * rows, rows)
    got = gather_halves((low, high), all_token)

    spectra, path, opening = whole_fields(
        own,
        got,
        path_spread,
        place,
        where,
        own_length,
        (own_row, own_column),
        (positions, modes, waves, half, slabs),
    )
    sent = lax.all_to_all(spectra, "wave", split_axis=0, concat_axis=0, tiled=True)
    sent = sent.reshape(waves * sent_lengths, positions * rows, PIX)
    images, sums = row_fields(path, opening, every, (all_row, all_column), positions)
    return mix(mix_spread, add_over_wave(sums, waves), sent, images, templates, rows)


def solution(mesh):
    return jax.shard_map(
        local,
        mesh=mesh,
        in_specs=(
            P(None, "wave", None),
            P(),
            P(("groups", "field")),
            P("wave"),
            P(),
            P(("groups", "field"), None),
        ),
        out_specs=P(("groups", "field"), None, "wave", None),
        check_vma=False,
    )
```

```python
import functools
import math

import jax
import jax.numpy as jnp
import numpy as np
from jax import lax
from jax.experimental import pallas as pl
from jax.experimental.pallas import tpu as pltpu
from jax.sharding import PartitionSpec as P

PUP = 512
PIX = 256
TWO_PI = 2.0 * math.pi
SAMPLING = 0.25
EPSILON = 1e-06
INNER = 61 * PUP // 100
BAND = 128
BANDS = PUP // BAND
ROWS = 16
LANES = 128
UNITS = BAND // ROWS
VMEM_BYTES = 60 * 2**20
SHARES = 8

SMEM = pl.BlockSpec(memory_space=pltpu.SMEM)
VMEM = pl.BlockSpec(memory_space=pltpu.VMEM)

SIN_POLY = (4.4428679, -7.30744341, 3.59478797, -0.78437376)
COS_POLY = (1.4142135, -6.97885099, 5.73946117, -1.88356298, 0.31069817)


def half_turn(turns):
    magic = jnp.float32(12582912.0)
    r = turns - ((turns + magic) - magic)
    z = r * r
    s = jnp.float32(SIN_POLY[-1])
    for value in SIN_POLY[-2::-1]:
        s = s * z + value
    k = jnp.float32(COS_POLY[-1])
    for value in COS_POLY[-2::-1]:
        k = k * z + value
    return s * r, k


def band_rows(band):
    low, high = PUP // 2 - 64 * (band + 1), PUP // 2 + 64 * band
    return [low + ROWS * i for i in range(4)] + [high + ROWS * i for i in range(4)]


def band_columns(band):
    low, high = PUP // 2 - 64 * (band + 1), PUP // 2 + 64 * band
    sides = (high, low) if band % 2 == 0 else (low, high)
    return np.concatenate([side + np.arange(64) for side in sides])


def unit_open(row, band):
    a = 2 * (row + np.arange(ROWS)) - PUP + 1
    b = 2 * band_columns(band) - PUP + 1
    radius = a[:, None] ** 2 + b[None, :] ** 2
    return bool(np.any((radius <= PUP * PUP) & (radius >= INNER * INNER)))


CHUNKS = [
    (band, rows)
    for band in range(BANDS)
    for rows in range(BANDS)
    if any(unit_open(row, band) for row in band_rows(rows))
]


@functools.lru_cache(None)
def layout(waves, modes):
    per = PUP // waves
    lists = []
    for wave in range(waves):
        lists.append(
            [
                (band, row)
                for band in range(BANDS)
                for row in range(wave * per, (wave + 1) * per, ROWS)
                if unit_open(row, band)
            ]
        )
    count = max(len(one) for one in lists)
    half = -(-count * modes // (2 * SHARES))
    slabs = 2 * SHARES * half
    pack = np.zeros((waves, count, 3), np.int32)
    for wave, one in enumerate(lists):
        for i, (band, row) in enumerate(one):
            columns = band_columns(band)
            pack[wave, i] = (columns[0] // LANES * LANES, columns[64] // LANES * LANES, row - wave * per)
    place = np.zeros((len(CHUNKS) * UNITS, 4), np.int32)
    for c, (band, rows) in enumerate(CHUNKS):
        columns = band_columns(band)
        for j, row in enumerate(band_rows(rows)):
            wave = row // per
            slab = 0
            if (band, row) in lists[wave]:
                slab = wave * slabs + lists[wave].index((band, row)) * modes
            place[c * UNITS + j] = (slab, row, columns[0], columns[64] - 64)
    return half, slabs, pack, place


def pack_slab(table, basis, line, mode):
    left = lax.broadcasted_iota(jnp.int32, (ROWS, LANES), 1) < 64
    first = pl.multiple_of(table[line, 0], LANES)
    second = pl.multiple_of(table[line, 1], LANES)
    row = pl.multiple_of(table[line, 2], ROWS)
    one = basis[mode, pl.ds(row, ROWS), pl.ds(first, LANES)].astype(jnp.float32)
    two = basis[mode, pl.ds(row, ROWS), pl.ds(second, LANES)].astype(jnp.float32)
    return jnp.where(left, one, two).astype(basis.dtype)


def own_kernel(count, where, table, basis, _, own, token):
    modes = basis.shape[0]
    token[...] = jnp.zeros_like(token)

    def unit(i, carry):
        for k in range(modes):
            own[i * modes + k] = pack_slab(table, basis, where[0] * count + i, k)
        return carry

    lax.fori_loop(0, count, unit, 0)
    for n in range(count * modes, own.shape[0]):
        own[n] = jnp.zeros((ROWS, LANES), own.dtype)


def piece_kernel(count, half, where, table, lengths, basis, piece, token):
    modes = basis.shape[0]
    token[...] = jnp.zeros_like(token)

    def pair(i, carry):
        for m in (2 * i, 2 * i + 1):
            n = where[1] * (2 * half) + m
            unit = n // modes
            mode = n - unit * modes
            unit = jnp.minimum(unit, count - 1)
            piece[m] = pack_slab(table, basis, where[0] * count + unit, mode)
        return carry

    lax.fori_loop(0, half, pair, 0)
    line = lax.broadcasted_iota(jnp.int32, (ROWS, LANES), 0)
    slab = jnp.zeros((ROWS, LANES), jnp.float32)
    for i in range(lengths.shape[0]):
        rest = jnp.full((ROWS, LANES), lengths[i], jnp.float32)
        for limb in range(3):
            value = rest.astype(jnp.bfloat16).astype(jnp.float32)
            slab = jnp.where(line == 3 * i + limb, value, slab)
            rest = rest - value
    piece[2 * half] = slab.astype(piece.dtype)


def pack_rows(basis, wave_lengths, plan, where):
    half, slabs, table, _ = plan
    count, table = table.shape[1], table.reshape(-1, 3)
    params = pltpu.CompilerParams(vmem_limit_bytes=VMEM_BYTES)
    piece, token = pl.pallas_call(
        functools.partial(piece_kernel, count, half),
        out_shape=(
            jax.ShapeDtypeStruct((2 * half + 1, ROWS, LANES), basis.dtype),
            jax.ShapeDtypeStruct((8, LANES), jnp.float32),
        ),
        in_specs=[SMEM, SMEM, SMEM, VMEM],
        out_specs=(VMEM, VMEM),
        compiler_params=params,
    )(where, table, wave_lengths, basis)
    own, token = pl.pallas_call(
        functools.partial(own_kernel, count),
        out_shape=(
            jax.ShapeDtypeStruct((slabs, ROWS, LANES), basis.dtype),
            jax.ShapeDtypeStruct((8, LANES), jnp.float32),
        ),
        in_specs=[SMEM, SMEM, VMEM, VMEM],
        out_specs=(VMEM, VMEM),
        compiler_params=params,
    )(where, table, basis, token)
    return own, piece, token


def split_kernel(half, sent, parts_count, where, own_lengths, *refs):
    parts, (low_ref, high_ref, length_ref, inverse_ref) = refs[:parts_count], refs[-4:]
    wave, waves = where[0], parts_count + 1
    kept = own_lengths.shape[0] - sent
    for s in range(waves):
        for i in range(kept):
            if s == 0:
                value = jnp.full((8, LANES), own_lengths[sent + i], jnp.float32)
            else:
                slab = parts[s - 1][2 * half].astype(jnp.float32)
                line = 3 * (sent + i)
                value = (slab[line : line + 1] + slab[line + 1 : line + 2]) + slab[
                    line + 2 : line + 3
                ]
                value = jnp.broadcast_to(value, (8, LANES))
            place = lax.rem(wave + (waves - s), waves) * kept + i
            length_ref[place] = value
            inverse_ref[place] = (1.0 / value)[0, 0]
    for s, part in enumerate(parts):
        low_ref[s * half : (s + 1) * half] = part[:half]
        high_ref[s * half : (s + 1) * half] = part[half : 2 * half]


def split_parts(parts, where, wave_lengths, half, sent, tokens):
    count = (len(parts) + 1) * (wave_lengths.shape[0] - sent)
    slabs = jax.ShapeDtypeStruct((len(parts) * half, ROWS, LANES), parts[0].dtype)
    return pl.pallas_call(
        functools.partial(split_kernel, half, sent, len(parts)),
        out_shape=(
            slabs,
            slabs,
            jax.ShapeDtypeStruct((count, 8, LANES), jnp.float32),
            jax.ShapeDtypeStruct((count,), jnp.float32),
        ),
        in_specs=[SMEM, SMEM] + [VMEM] * (len(parts) + len(tokens)),
        out_specs=(VMEM,) * 3 + (SMEM,),
        compiler_params=pltpu.CompilerParams(vmem_limit_bytes=VMEM_BYTES),
    )(where, wave_lengths, *parts, *tokens)


def after(arrays, tokens):
    any_memory = pl.BlockSpec(memory_space=pl.ANY)
    return pl.pallas_call(
        lambda *refs: None,
        out_shape=tuple(jax.ShapeDtypeStruct(x.shape, x.dtype) for x in arrays),
        in_specs=[any_memory] * len(arrays) + [VMEM] * len(tokens),
        out_specs=(any_memory,) * len(arrays),
        input_output_aliases={i: i for i in range(len(arrays))},
    )(*arrays, *tokens)


def along_wave(piece, waves):
    return [
        lax.ppermute(piece, "wave", [(i, (i + s) % waves) for i in range(waves)])
        for s in range(1, waves)
    ]


def swap(x, mask):
    groups, fields = lax.axis_size("groups"), lax.axis_size("field")
    pairs = [
        (g * fields + f, (g ^ (mask >> 2)) * fields + (f ^ (mask & 3)))
        for g in range(groups)
        for f in range(fields)
    ]
    return lax.ppermute(x, ("groups", "field"), pairs)


def gather_halves(halves, token):
    routes = ((2, 4), (4, 2))
    near = [swap(mine, mask) for mine, route in zip(halves, routes) for mask in route]
    near = after(near, [token])
    got = [(h, mine, 0) for h, mine in enumerate(halves)]
    for h, (one, two) in enumerate(routes):
        got.append((h, near[2 * h], one))
        got.append((h, near[2 * h + 1], two))
        got.append((h, swap(near[2 * h], two), one | two))
    return got + [(h, swap(array, 1), mask | 1) for h, array, mask in got]


def spread_kernel(*refs):
    count = len(refs) // 2
    refs[-1][...] = jnp.zeros_like(refs[-1])
    for small_ref, big_ref in zip(refs[:count], refs[count:-1]):
        _, many, wide = small_ref.shape
        tall, long = many * ROWS, wide * ROWS
        down = lax.broadcasted_iota(jnp.int32, (tall, many), 0) // ROWS
        down = (down == lax.broadcasted_iota(jnp.int32, (tall, many), 1)).astype(jnp.float32)
        along = lax.broadcasted_iota(jnp.int32, (wide, long), 1) // ROWS
        along = (along == lax.broadcasted_iota(jnp.int32, (wide, long), 0)).astype(jnp.float32)
        same = (lax.broadcasted_iota(jnp.int32, (tall, long), 0) % ROWS) == (
            lax.broadcasted_iota(jnp.int32, (tall, long), 1) % ROWS
        )
        down, along = down.astype(jnp.bfloat16), along.astype(jnp.bfloat16)
        for i in range(small_ref.shape[0]):
            half = jnp.dot(down, small_ref[i], preferred_element_type=jnp.float32)
            whole = jnp.dot(half.astype(jnp.bfloat16), along, preferred_element_type=jnp.float32)
            big_ref[i] = jnp.where(same, whole, 0.0).astype(jnp.bfloat16)


def spreads(*matrices):
    return pl.pallas_call(
        spread_kernel,
        out_shape=tuple(
            jax.ShapeDtypeStruct((m.shape[0], m.shape[1] * ROWS, m.shape[2] * ROWS), jnp.bfloat16)
            for m in matrices
        )
        + (jax.ShapeDtypeStruct((8, LANES), jnp.float32),),
        compiler_params=pltpu.CompilerParams(vmem_limit_bytes=VMEM_BYTES),
    )(*matrices)


def form_paths(sizes, where, place, parts, spread, path, opening, basis, sems):
    positions, modes, waves, half, slabs, keys = sizes
    wave, share = where[0], where[1]
    copies = [pltpu.make_async_copy(parts[0], basis.at[pl.ds(wave * slabs, slabs)], sems.at[0])]
    n = 1
    for (h, mask), part in zip(keys, parts[1:]):
        for s in range(1, waves):
            source = lax.rem(wave + (waves - s), waves)
            start = source * slabs + (share ^ mask) * (2 * half) + h * half
            copies.append(
                pltpu.make_async_copy(
                    part.at[pl.ds((s - 1) * half, half)], basis.at[pl.ds(start, half)], sems.at[n]
                )
            )
            n += 1
    for copy in copies:
        copy.start()
    for copy in copies:
        copy.wait()

    lane = lax.broadcasted_iota(jnp.int32, (ROWS, LANES), 1)
    line = lax.broadcasted_iota(jnp.int32, (ROWS, LANES), 0)

    def chunk(c, carry):
        values = jnp.concatenate(
            [
                basis[pl.ds(place[c * UNITS + j, 0], modes)].reshape(modes * ROWS, LANES)
                for j in range(UNITS)
            ],
            axis=1,
        )
        found = jnp.dot(spread[0], values, preferred_element_type=jnp.float32)
        for j in range(UNITS):
            u = c * UNITS + j
            a = 2 * (line + place[u, 1]) - (PUP - 1)
            b = 2 * (lane + jnp.where(lane < 64, place[u, 2], place[u, 3])) - (PUP - 1)
            radius = a * a + b * b
            inside = (radius <= PUP * PUP) & (radius >= INNER * INNER)
            opening[u] = jnp.where(inside, 1.0, 0.0)
            for f in range(positions):
                path[u, f * ROWS : (f + 1) * ROWS] = jnp.where(
                    inside, found[f * ROWS : (f + 1) * ROWS, j * LANES : (j + 1) * LANES], 0.0
                )
        return carry

    lax.fori_loop(0, place.shape[0] // UNITS, chunk, 0)


def transform(positions, rows, inverse, path, opening, row_ref, scratch, wait=None):
    pupils, total, first = scratch[:2], scratch[2], scratch[3]
    batch = max(1, positions // 2)
    width = 2 * positions * LANES // UNITS

    def finish(band, columns, value):
        for f in range(columns.start // LANES, columns.stop // LANES):
            lanes = slice(f * LANES - columns.start, (f + 1) * LANES - columns.start)
            for part in range(2):
                first[
                    f * rows : (f + 1) * rows,
                    part * PUP + band * LANES : part * PUP + (band + 1) * LANES,
                ] = value[part * rows : (part + 1) * rows, lanes].astype(jnp.bfloat16)

    def product(c, columns):
        band, rows_band = CHUNKS[c]
        value = jnp.dot(
            row_ref[0, rows_band], pupils[c % 2][:, columns], preferred_element_type=jnp.float32
        )
        if c > 0 and CHUNKS[c - 1][0] == band:
            value = value + total[:, columns]
        if c + 1 < len(CHUNKS) and CHUNKS[c + 1][0] == band:
            total[:, columns] = value
        else:
            finish(band, columns, value)

    for c, (band, rows_band) in enumerate(CHUNKS):
        pupil = pupils[c % 2]
        if wait is not None:
            wait(c)
        for j, row in enumerate(band_rows(rows_band)):
            real_lines = slice(2 * ROWS * j, 2 * ROWS * j + ROWS)
            imag_lines = slice(2 * ROWS * j + ROWS, 2 * ROWS * (j + 1))
            if unit_open(row, band):
                u = c * UNITS + j
                inside = opening[u]
                for f0 in range(0, positions, batch):
                    s, k = half_turn(path[u, f0 * ROWS : (f0 + batch) * ROWS] * inverse)
                    sine = s * k
                    square = s * s
                    for f in range(f0, f0 + batch):
                        columns = slice(f * LANES, (f + 1) * LANES)
                        lines = slice((f - f0) * ROWS, (f - f0 + 1) * ROWS)
                        pupil[real_lines, columns] = (inside - square[lines]).astype(jnp.bfloat16)
                        pupil[imag_lines, columns] = sine[lines].astype(jnp.bfloat16)
            else:
                empty = jnp.zeros((ROWS, positions * LANES), jnp.bfloat16)
                pupil[real_lines] = empty
                pupil[imag_lines] = empty
            if c > 0 and j % 2 == 1:
                product(c - 1, slice(j // 2 * width, (j // 2 + 1) * width))
    for n in range(positions * LANES // width):
        product(len(CHUNKS) - 1, slice(n * width, (n + 1) * width))


def columns_of(first, column_ref):
    return [
        jnp.dot(
            first, column_ref[0, :, part * PIX : (part + 1) * PIX], preferred_element_type=jnp.float32
        )
        for part in range(2)
    ]


def chunk_copies(source, target, sems):
    return [
        pltpu.make_async_copy(
            source.at[pl.ds(c * UNITS, UNITS)], target.at[pl.ds(c * UNITS, UNITS)], sems.at[c]
        )
        for c in range(len(CHUNKS))
    ]


def whole_kernel(sizes, inverse_ref, place, where, *refs):
    positions, modes, waves, half, slabs, keys = sizes
    parts, refs = refs[: 1 + len(keys)], refs[1 + len(keys) :]
    spread, row_ref, column_ref, out_ref, path_out, opening, path, basis, sems, path_sems = refs[:10]
    scratch = refs[10:]
    copies = chunk_copies(path, path_out, path_sems)

    @pl.when(pl.program_id(0) == 0)
    def _():
        form_paths(sizes, where, place, parts, spread, path, opening, basis, sems)
        for copy in copies:
            copy.start()

    rows = PIX
    inverse = inverse_ref[pl.program_id(0)]
    transform(positions, rows, inverse, path, opening, row_ref, scratch)
    first = scratch[3]
    share = rows // waves
    for f in range(positions):
        real, imag = columns_of(first[f * rows : (f + 1) * rows], column_ref)
        intensity = real * real + imag * imag
        level = jnp.sum(
            jnp.sum(intensity, axis=0, keepdims=True), axis=1, keepdims=True
        ) / (rows * PIX)
        spectra = (intensity / (level + EPSILON)).astype(jnp.bfloat16)
        for part in range(waves):
            out_ref[part, 0, f * share : (f + 1) * share] = spectra[
                part * share : (part + 1) * share
            ]

    @pl.when(pl.program_id(0) == pl.num_programs(0) - 1)
    def _():
        for copy in copies:
            copy.wait()


def rows_kernel(positions, rows, inverse_ref, path_in, opening, row_ref, column_ref, *refs):
    image_ref, sum_ref, path, path_sems = refs[:4]
    scratch = refs[4:]
    copies = chunk_copies(path_in, path, path_sems)
    begin = pl.program_id(0) == 0

    @pl.when(begin)
    def _():
        for copy in copies:
            copy.start()

    def wait(c):
        if c > 0 and CHUNKS[c - 1][0] == CHUNKS[c][0]:
            return

        @pl.when(begin)
        def _():
            for copy, chunk in zip(copies, CHUNKS):
                if chunk[0] == CHUNKS[c][0]:
                    copy.wait()

    inverse = inverse_ref[pl.program_id(0)]
    transform(positions, rows, inverse, path, opening, row_ref, scratch, wait)
    real, imag = columns_of(scratch[3][...], column_ref)
    intensity = real * real + imag * imag
    image_ref[0] = intensity
    sums = jnp.sum(intensity.reshape(positions, rows, PIX), axis=1)
    sum_ref[0] = jnp.broadcast_to(jnp.sum(sums, axis=1, keepdims=True), (positions, LANES))


def transform_scratch(positions, rows):
    return [
        pltpu.VMEM((2 * BAND, positions * LANES), jnp.bfloat16),
        pltpu.VMEM((2 * BAND, positions * LANES), jnp.bfloat16),
        pltpu.VMEM((2 * rows, positions * LANES), jnp.float32),
        pltpu.VMEM((positions * rows, 2 * PUP), jnp.bfloat16),
    ]


def transform_cost(lengths, positions, rows):
    return pl.CostEstimate(
        flops=lengths * positions * (rows * 8 * PUP * PUP + rows * 8 * PUP * PIX + 10**8),
        bytes_accessed=8 * 2**20,
        transcendentals=0,
    )


def by_length(array):
    return pl.BlockSpec((1,) + array.shape[1:], lambda l: (l,) + (0,) * (len(array.shape) - 1))


def path_shape(positions):
    return (len(CHUNKS) * UNITS, positions * ROWS, LANES)


def whole_fields(own, got, spread, place, where, inverse, tables, sizes):
    positions, modes, waves, half, slabs = sizes
    keys = tuple((h, mask) for h, _, mask in got)
    arrays = [array for _, array, _ in got]
    lengths = inverse.shape[0]
    share = positions * PIX // waves
    any_memory = pl.BlockSpec(memory_space=pl.ANY)
    return pl.pallas_call(
        functools.partial(whole_kernel, (positions, modes, waves, half, slabs, keys)),
        grid=(lengths,),
        out_shape=(
            jax.ShapeDtypeStruct((waves, lengths, share, PIX), jnp.bfloat16),
            jax.ShapeDtypeStruct(path_shape(positions), jnp.float32),
            jax.ShapeDtypeStruct((place.shape[0], ROWS, LANES), jnp.float32),
        ),
        in_specs=[SMEM, SMEM, SMEM]
        + [any_memory] * (1 + len(keys))
        + [VMEM]
        + [by_length(table) for table in tables],
        out_specs=(
            pl.BlockSpec((waves, 1, share, PIX), lambda l: (0, l, 0, 0)),
            any_memory,
            VMEM,
        ),
        scratch_shapes=[
            pltpu.VMEM(path_shape(positions), jnp.float32),
            pltpu.VMEM((waves * slabs, ROWS, LANES), jnp.bfloat16),
            pltpu.SemaphoreType.DMA((1 + len(keys) * (waves - 1),)),
            pltpu.SemaphoreType.DMA((len(CHUNKS),)),
        ]
        + transform_scratch(positions, PIX),
        cost_estimate=transform_cost(lengths, positions, PIX),
        compiler_params=pltpu.CompilerParams(vmem_limit_bytes=VMEM_BYTES),
    )(inverse, place, where, own, *arrays, spread, *tables)


def row_fields(path, opening, inverse, tables, positions):
    lengths = inverse.shape[0]
    rows = tables[0].shape[2] // 2
    out_shape = (
        jax.ShapeDtypeStruct((lengths, positions * rows, PIX), jnp.float32),
        jax.ShapeDtypeStruct((lengths, positions, LANES), jnp.float32),
    )
    return pl.pallas_call(
        functools.partial(rows_kernel, positions, rows),
        grid=(lengths,),
        out_shape=out_shape,
        in_specs=[SMEM, pl.BlockSpec(memory_space=pl.ANY), VMEM]
        + [by_length(table) for table in tables],
        out_specs=tuple(by_length(one) for one in out_shape),
        scratch_shapes=[
            pltpu.VMEM(path_shape(positions), jnp.float32),
            pltpu.SemaphoreType.DMA((len(CHUNKS),)),
        ]
        + transform_scratch(positions, rows),
        cost_estimate=transform_cost(lengths, positions, rows),
        compiler_params=pltpu.CompilerParams(vmem_limit_bytes=VMEM_BYTES),
    )(inverse, path, opening, *tables)


def mix_kernel(sum_ref, weight_ref, sent_ref, image_ref, out_ref):
    count, templates, rows = out_ref.shape[:3]
    for i in range(count):
        f = pl.program_id(0) * count + i
        inverse = [
            1.0 / (sum_ref[l, pl.ds(f, 1)] / (PIX * PIX) + EPSILON)
            for l in range(image_ref.shape[0])
        ]
        inverse = [jnp.concatenate([one] * (PIX // LANES), axis=1) for one in inverse]
        blocks = []
        for start in range(i * rows, (i + 1) * rows, ROWS):
            lines = slice(start, start + ROWS)
            blocks.append(
                jnp.concatenate(
                    [sent_ref[l, lines] for l in range(sent_ref.shape[0])]
                    + [
                        (image_ref[l, lines] * inverse[l]).astype(jnp.bfloat16)
                        for l in range(image_ref.shape[0])
                    ],
                    axis=0,
                )
            )
        mixed = jnp.dot(
            weight_ref[i], jnp.concatenate(blocks, axis=1), preferred_element_type=jnp.float32
        ).astype(jnp.bfloat16)
        for n in range(len(blocks)):
            for j in range(templates):
                out_ref[i, j, n * ROWS : (n + 1) * ROWS] = mixed[
                    j * ROWS : (j + 1) * ROWS, n * PIX : (n + 1) * PIX
                ]


def mix(spread, sums, sent, images, templates, rows):
    positions = spread.shape[0]
    count = 2 if positions % 2 == 0 else 1
    return pl.pallas_call(
        mix_kernel,
        grid=(positions // count,),
        out_shape=jax.ShapeDtypeStruct((positions, templates, rows, PIX), jnp.bfloat16),
        in_specs=[
            VMEM,
            pl.BlockSpec((count,) + spread.shape[1:], lambda f: (f, 0, 0)),
            pl.BlockSpec((sent.shape[0], count * rows, PIX), lambda f: (0, f, 0)),
            pl.BlockSpec((images.shape[0], count * rows, PIX), lambda f: (0, f, 0)),
        ],
        out_specs=pl.BlockSpec((count, templates, rows, PIX), lambda f: (f, 0, 0, 0)),
        compiler_params=pltpu.CompilerParams(vmem_limit_bytes=24 * 2**20),
    )(sums, spread, sent, images)


def table_kernel(length_ref, y_ref, v_ref, u_ref, x_ref, row_ref, column_ref, token_ref):
    scale = (SAMPLING / (2.0 * PUP)) / length_ref[0, :1]
    scale = jnp.concatenate([scale] * (PIX // LANES), axis=1)
    token_ref[...] = jnp.zeros_like(token_ref)
    for start in range(0, PUP, ROWS):
        s, k = half_turn((y_ref[start : start + ROWS] * v_ref[...]) * scale)
        cosine, sine = 1.0 - s * s, s * k
        lower, upper = slice(start, start + ROWS), slice(PUP + start, PUP + start + ROWS)
        column_ref[0, lower, :PIX] = cosine.astype(jnp.bfloat16)
        column_ref[0, lower, PIX:] = (-sine).astype(jnp.bfloat16)
        column_ref[0, upper, :PIX] = sine.astype(jnp.bfloat16)
        column_ref[0, upper, PIX:] = cosine.astype(jnp.bfloat16)
    rows = u_ref.shape[0]
    imag = (lax.broadcasted_iota(jnp.int32, (ROWS, 2 * BAND), 1) // ROWS) % 2 == 1
    for band in range(BANDS):
        for start in range(0, rows, ROWS):
            s, k = half_turn((u_ref[start : start + ROWS] * x_ref[band]) * scale)
            cosine, sine = 1.0 - s * s, s * k
            row_ref[0, band, start : start + ROWS] = jnp.where(imag, sine, cosine).astype(
                jnp.bfloat16
            )
            row_ref[0, band, rows + start : rows + start + ROWS] = jnp.where(
                imag, cosine, -sine
            ).astype(jnp.bfloat16)


def tables(length, first_row, rows):
    lengths = length.shape[0]
    y = 2 * np.concatenate([band_columns(band) for band in range(BANDS)]) - PUP + 1
    v = np.arange(PIX) - PIX // 2
    u = first_row + jnp.arange(rows, dtype=jnp.int32) - PIX // 2
    x = np.array(
        [[row + i for row in band_rows(band) for i in range(ROWS)] for band in range(BANDS)]
    )
    x = np.repeat(x.reshape(BANDS, UNITS, 1, ROWS), 2, axis=2).reshape(BANDS, 1, 2 * BAND)
    whole = lambda *shape: pl.BlockSpec(shape, lambda l: (0,) * len(shape))
    return pl.pallas_call(
        table_kernel,
        grid=(lengths,),
        out_shape=(
            jax.ShapeDtypeStruct((lengths, BANDS, 2 * rows, 2 * BAND), jnp.bfloat16),
            jax.ShapeDtypeStruct((lengths, 2 * PUP, 2 * PIX), jnp.bfloat16),
            jax.ShapeDtypeStruct((8, LANES), jnp.float32),
        ),
        in_specs=[
            pl.BlockSpec((1, 8, LANES), lambda l: (l, 0, 0)),
            whole(PUP, 1),
            whole(1, PIX),
            whole(rows, 1),
            whole(BANDS, 1, 2 * BAND),
        ],
        out_specs=(
            pl.BlockSpec((1, BANDS, 2 * rows, 2 * BAND), lambda l: (l, 0, 0, 0)),
            pl.BlockSpec((1, 2 * PUP, 2 * PIX), lambda l: (l, 0, 0)),
            whole(8, LANES),
        ),
        cost_estimate=pl.CostEstimate(
            flops=lengths * 30 * PUP * PIX, bytes_accessed=lengths * 4 * PUP * PIX * 2, transcendentals=0
        ),
        compiler_params=pltpu.CompilerParams(vmem_limit_bytes=VMEM_BYTES),
    )(
        length,
        jnp.asarray(y[:, None].astype(np.float32)),
        jnp.asarray(v[None, :].astype(np.float32)),
        u.astype(jnp.float32)[:, None],
        jnp.asarray((2 * x - PUP + 1).astype(np.float32)),
    )


def add_over_wave(x, waves):
    step = 1
    while step < waves:
        x = x + lax.ppermute(x, "wave", [(i, i ^ step) for i in range(waves)])
        step *= 2
    return x


def local(mode_basis, coef_table, table_index, wave_lengths, sed_table, template_ids):
    waves = lax.axis_size("wave")
    mine = lax.axis_index("wave")
    modes = mode_basis.shape[0]
    positions = table_index.shape[0]
    rows = PIX // waves
    lengths = wave_lengths.shape[0]
    sent_lengths = lengths // 2

    share = (lax.axis_index("groups") % 2) * 4 + lax.axis_index("field") % 4
    where = jnp.stack([mine, share]).astype(jnp.int32)
    plan = layout(waves, modes)
    half, slabs, _, place = plan
    own, piece, packed = pack_rows(mode_basis, wave_lengths, plan, where)
    parts = along_wave(piece, waves)

    selector = (
        table_index[:, None] == jnp.arange(coef_table.shape[0], dtype=jnp.int32)[None, :]
    ).astype(jnp.bfloat16)
    coeffs = jnp.dot(selector, coef_table, preferred_element_type=jnp.float32)
    one_hot = (
        template_ids[:, :, None]
        == jnp.arange(sed_table.shape[0], dtype=jnp.int32)[None, None, :]
    ).astype(jnp.float32)
    raw_weights = jnp.einsum("fjn,nl->fjl", one_hot, sed_table, precision=lax.Precision.HIGHEST)
    weights = (raw_weights / jnp.sum(raw_weights, axis=2, keepdims=True)).astype(jnp.bfloat16)
    templates = weights.shape[1]
    split = weights.reshape(positions, templates, waves, lengths)
    weights = jnp.concatenate(
        [
            split[..., :sent_lengths].reshape(positions, templates, -1),
            split[..., sent_lengths:].reshape(positions, templates, -1),
        ],
        axis=2,
    )
    path_spread, mix_spread, spread_token = spreads(coeffs.astype(jnp.bfloat16)[None], weights)
    own_length = jnp.broadcast_to(
        wave_lengths[:sent_lengths, None, None], (sent_lengths, 8, LANES)
    )
    own_row, own_column, own_token = tables(own_length, 0, PIX)

    low, high, every, inverse = split_parts(
        parts, where, wave_lengths, half, sent_lengths, (spread_token, own_token, packed)
    )
    all_row, all_column, all_token = tables(every, mine * rows, rows)
    got = gather_halves((low, high), all_token)

    spectra, path, opening = whole_fields(
        own,
        got,
        path_spread,
        place,
        where,
        1.0 / wave_lengths[:sent_lengths],
        (own_row, own_column),
        (positions, modes, waves, half, slabs),
    )
    sent = lax.all_to_all(spectra, "wave", split_axis=0, concat_axis=0, tiled=True)
    sent = sent.reshape(waves * sent_lengths, positions * rows, PIX)
    images, sums = row_fields(path, opening, inverse, (all_row, all_column), positions)
    return mix(mix_spread, add_over_wave(sums, waves), sent, images, templates, rows)


def solution(mesh):
    return jax.shard_map(
        local,
        mesh=mesh,
        in_specs=(
            P(None, "wave", None),
            P(),
            P(("groups", "field")),
            P("wave"),
            P(),
            P(("groups", "field"), None),
        ),
        out_specs=P(("groups", "field"), None, "wave", None),
        check_vma=False,
    )
```

```python
import functools
import math

import jax
import jax.numpy as jnp
import numpy as np
from jax import lax
from jax.experimental import pallas as pl
from jax.experimental.pallas import tpu as pltpu
from jax.sharding import PartitionSpec as P

PUP = 512
PIX = 256
TWO_PI = 2.0 * math.pi
SAMPLING = 0.25
EPSILON = 1e-06
INNER = 61 * PUP // 100
BAND = 128
BANDS = PUP // BAND
ROWS = 16
LANES = 128
UNITS = BAND // ROWS
VMEM_BYTES = 60 * 2**20
SHARES = 8

SMEM = pl.BlockSpec(memory_space=pltpu.SMEM)
VMEM = pl.BlockSpec(memory_space=pltpu.VMEM)

SIN_POLY = (4.4428679, -7.30744341, 3.59478797, -0.78437376)
COS_POLY = (1.4142135, -6.97885099, 5.73946117, -1.88356298, 0.31069817)


def half_turn(turns):
    magic = jnp.float32(12582912.0)
    r = turns - ((turns + magic) - magic)
    z = r * r
    s = jnp.float32(SIN_POLY[-1])
    for value in SIN_POLY[-2::-1]:
        s = s * z + value
    k = jnp.float32(COS_POLY[-1])
    for value in COS_POLY[-2::-1]:
        k = k * z + value
    return s * r, k


def band_rows(band):
    low, high = PUP // 2 - 64 * (band + 1), PUP // 2 + 64 * band
    return [low + ROWS * i for i in range(4)] + [high + ROWS * i for i in range(4)]


def band_columns(band):
    low, high = PUP // 2 - 64 * (band + 1), PUP // 2 + 64 * band
    sides = (high, low) if band % 2 == 0 else (low, high)
    return np.concatenate([side + np.arange(64) for side in sides])


def unit_open(row, band):
    a = 2 * (row + np.arange(ROWS)) - PUP + 1
    b = 2 * band_columns(band) - PUP + 1
    radius = a[:, None] ** 2 + b[None, :] ** 2
    return bool(np.any((radius <= PUP * PUP) & (radius >= INNER * INNER)))


CHUNKS = [
    (band, rows)
    for band in range(BANDS)
    for rows in range(BANDS)
    if any(unit_open(row, band) for row in band_rows(rows))
]


@functools.lru_cache(None)
def layout(waves, modes):
    per = PUP // waves
    lists = []
    for wave in range(waves):
        lists.append(
            [
                (band, row)
                for band in range(BANDS)
                for row in range(wave * per, (wave + 1) * per, ROWS)
                if unit_open(row, band)
            ]
        )
    count = max(len(one) for one in lists)
    half = -(-count * modes // (2 * SHARES))
    slabs = 2 * SHARES * half
    pack = np.zeros((waves, count, 3), np.int32)
    for wave, one in enumerate(lists):
        for i, (band, row) in enumerate(one):
            columns = band_columns(band)
            pack[wave, i] = (columns[0] // LANES * LANES, columns[64] // LANES * LANES, row - wave * per)
    place = np.zeros((len(CHUNKS) * UNITS, 4), np.int32)
    for c, (band, rows) in enumerate(CHUNKS):
        columns = band_columns(band)
        for j, row in enumerate(band_rows(rows)):
            wave = row // per
            slab = 0
            if (band, row) in lists[wave]:
                slab = wave * slabs + lists[wave].index((band, row)) * modes
            place[c * UNITS + j] = (slab, row, columns[0], columns[64] - 64)
    return half, slabs, pack, place


def pack_slab(table, basis, line, mode):
    left = lax.broadcasted_iota(jnp.int32, (ROWS, LANES), 1) < 64
    first = pl.multiple_of(table[line, 0], LANES)
    second = pl.multiple_of(table[line, 1], LANES)
    row = pl.multiple_of(table[line, 2], ROWS)
    one = basis[mode, pl.ds(row, ROWS), pl.ds(first, LANES)].astype(jnp.float32)
    two = basis[mode, pl.ds(row, ROWS), pl.ds(second, LANES)].astype(jnp.float32)
    return jnp.where(left, one, two).astype(basis.dtype)


def own_kernel(count, where, table, basis, _, own, token):
    modes = basis.shape[0]
    token[...] = jnp.zeros_like(token)

    def unit(i, carry):
        for k in range(modes):
            own[i * modes + k] = pack_slab(table, basis, where[0] * count + i, k)
        return carry

    lax.fori_loop(0, count, unit, 0)
    for n in range(count * modes, own.shape[0]):
        own[n] = jnp.zeros((ROWS, LANES), own.dtype)


def piece_kernel(count, half, where, table, lengths, basis, piece, token):
    modes = basis.shape[0]
    token[...] = jnp.zeros_like(token)

    def pair(i, carry):
        for m in (2 * i, 2 * i + 1):
            n = where[1] * (2 * half) + m
            unit = n // modes
            mode = n - unit * modes
            unit = jnp.minimum(unit, count - 1)
            piece[m] = pack_slab(table, basis, where[0] * count + unit, mode)
        return carry

    lax.fori_loop(0, half, pair, 0)
    line = lax.broadcasted_iota(jnp.int32, (ROWS, LANES), 0)
    slab = jnp.zeros((ROWS, LANES), jnp.float32)
    for i in range(lengths.shape[0]):
        rest = jnp.full((ROWS, LANES), lengths[i], jnp.float32)
        for limb in range(3):
            value = rest.astype(jnp.bfloat16).astype(jnp.float32)
            slab = jnp.where(line == 3 * i + limb, value, slab)
            rest = rest - value
    piece[2 * half] = slab.astype(piece.dtype)


def pack_rows(basis, wave_lengths, plan, where):
    half, slabs, table, _ = plan
    count, table = table.shape[1], table.reshape(-1, 3)
    params = pltpu.CompilerParams(vmem_limit_bytes=VMEM_BYTES)
    piece, token = pl.pallas_call(
        functools.partial(piece_kernel, count, half),
        out_shape=(
            jax.ShapeDtypeStruct((2 * half + 1, ROWS, LANES), basis.dtype),
            jax.ShapeDtypeStruct((8, LANES), jnp.float32),
        ),
        in_specs=[SMEM, SMEM, SMEM, VMEM],
        out_specs=(VMEM, VMEM),
        compiler_params=params,
    )(where, table, wave_lengths, basis)
    own, token = pl.pallas_call(
        functools.partial(own_kernel, count),
        out_shape=(
            jax.ShapeDtypeStruct((slabs, ROWS, LANES), basis.dtype),
            jax.ShapeDtypeStruct((8, LANES), jnp.float32),
        ),
        in_specs=[SMEM, SMEM, VMEM, VMEM],
        out_specs=(VMEM, VMEM),
        compiler_params=params,
    )(where, table, basis, token)
    return own, piece, token


def split_kernel(half, count, *refs):
    parts, (low_ref, high_ref) = refs[:count], refs[-2:]
    for s, part in enumerate(parts):
        low_ref[s * half : (s + 1) * half] = part[:half]
        high_ref[s * half : (s + 1) * half] = part[half : 2 * half]


def split_parts(parts, half, tokens):
    slabs = jax.ShapeDtypeStruct((len(parts) * half, ROWS, LANES), parts[0].dtype)
    return pl.pallas_call(
        functools.partial(split_kernel, half, len(parts)),
        out_shape=(slabs, slabs),
        in_specs=[VMEM] * (len(parts) + len(tokens)),
        out_specs=(VMEM,) * 2,
        compiler_params=pltpu.CompilerParams(vmem_limit_bytes=VMEM_BYTES),
    )(*parts, *tokens)


def lengths_kernel(sent, where, own_lengths, *refs):
    parts, (length_ref, inverse_ref) = refs[:-2], refs[-2:]
    wave, waves = where[0], len(parts) + 1
    kept = own_lengths.shape[0] - sent
    for s in range(waves):
        for i in range(kept):
            if s == 0:
                value = jnp.full((8, LANES), own_lengths[sent + i], jnp.float32)
            else:
                slab = parts[s - 1][0].astype(jnp.float32)
                line = 3 * (sent + i)
                value = (slab[line : line + 1] + slab[line + 1 : line + 2]) + slab[
                    line + 2 : line + 3
                ]
                value = jnp.broadcast_to(value, (8, LANES))
            place = lax.rem(wave + (waves - s), waves) * kept + i
            length_ref[place] = value
            inverse_ref[place] = (1.0 / value)[0, 0]


def kept_lengths(parts, where, wave_lengths, half, sent):
    count = (len(parts) + 1) * (wave_lengths.shape[0] - sent)
    last = pl.BlockSpec((1, ROWS, LANES), lambda i: (2 * half, 0, 0))
    return pl.pallas_call(
        functools.partial(lengths_kernel, sent),
        grid=(1,),
        out_shape=(
            jax.ShapeDtypeStruct((count, 8, LANES), jnp.float32),
            jax.ShapeDtypeStruct((count,), jnp.float32),
        ),
        in_specs=[SMEM, SMEM] + [last] * len(parts),
        out_specs=(VMEM, SMEM),
        compiler_params=pltpu.CompilerParams(vmem_limit_bytes=VMEM_BYTES),
    )(where, wave_lengths, *parts)


def after(arrays, tokens):
    any_memory = pl.BlockSpec(memory_space=pl.ANY)
    return pl.pallas_call(
        lambda *refs: None,
        out_shape=tuple(jax.ShapeDtypeStruct(x.shape, x.dtype) for x in arrays),
        in_specs=[any_memory] * len(arrays) + [VMEM] * len(tokens),
        out_specs=(any_memory,) * len(arrays),
        input_output_aliases={i: i for i in range(len(arrays))},
    )(*arrays, *tokens)


def along_wave(piece, waves):
    return [
        lax.ppermute(piece, "wave", [(i, (i + s) % waves) for i in range(waves)])
        for s in range(1, waves)
    ]


def swap(x, mask):
    groups, fields = lax.axis_size("groups"), lax.axis_size("field")
    pairs = [
        (g * fields + f, (g ^ (mask >> 2)) * fields + (f ^ (mask & 3)))
        for g in range(groups)
        for f in range(fields)
    ]
    return lax.ppermute(x, ("groups", "field"), pairs)


def gather_halves(halves, half, shifts, tokens):
    routes = ((2, 4), (4, 2))
    near = [swap(mine, mask) for mine, route in zip(halves, routes) for mask in route]
    near = after(near + list(halves), tokens)
    got = [(h, mine, 0) for h, mine in enumerate(near[4:])]
    for h, (one, two) in enumerate(routes):
        got.append((h, near[2 * h], one))
        got.append((h, near[2 * h + 1], two))
        got.append((h, swap(near[2 * h], two), one | two))
    got = got + [(h, swap(array, 1), mask | 1) for h, array, mask in got]
    return [((shifts, h * half, half, half, mask), array) for h, array, mask in got]


def gather_direct(pieces, half, shifts, tokens):
    masks = (6, 2, 4)
    near = after([swap(pieces, mask) for mask in masks], tokens)
    got = [(0, pieces)] + list(zip(masks, near))
    got = got + [(mask | 1, swap(array, 1)) for mask, array in got]
    return [((shifts, 0, 2 * half, 2 * half + 1, mask), array) for mask, array in got]


def spread_kernel(*refs):
    count = len(refs) // 2
    refs[-1][...] = jnp.zeros_like(refs[-1])
    for small_ref, big_ref in zip(refs[:count], refs[count:-1]):
        _, many, wide = small_ref.shape
        tall, long = many * ROWS, wide * ROWS
        down = lax.broadcasted_iota(jnp.int32, (tall, many), 0) // ROWS
        down = (down == lax.broadcasted_iota(jnp.int32, (tall, many), 1)).astype(jnp.float32)
        along = lax.broadcasted_iota(jnp.int32, (wide, long), 1) // ROWS
        along = (along == lax.broadcasted_iota(jnp.int32, (wide, long), 0)).astype(jnp.float32)
        same = (lax.broadcasted_iota(jnp.int32, (tall, long), 0) % ROWS) == (
            lax.broadcasted_iota(jnp.int32, (tall, long), 1) % ROWS
        )
        down, along = down.astype(jnp.bfloat16), along.astype(jnp.bfloat16)
        for i in range(small_ref.shape[0]):
            half = jnp.dot(down, small_ref[i], preferred_element_type=jnp.float32)
            whole = jnp.dot(half.astype(jnp.bfloat16), along, preferred_element_type=jnp.float32)
            big_ref[i] = jnp.where(same, whole, 0.0).astype(jnp.bfloat16)


def spreads(*matrices):
    return pl.pallas_call(
        spread_kernel,
        out_shape=tuple(
            jax.ShapeDtypeStruct((m.shape[0], m.shape[1] * ROWS, m.shape[2] * ROWS), jnp.bfloat16)
            for m in matrices
        )
        + (jax.ShapeDtypeStruct((8, LANES), jnp.float32),),
        compiler_params=pltpu.CompilerParams(vmem_limit_bytes=VMEM_BYTES),
    )(*matrices)


def form_paths(sizes, where, place, parts, spread, path, opening, basis, sems):
    positions, modes, waves, half, slabs, keys = sizes
    wave, share = where[0], where[1]
    copies = [pltpu.make_async_copy(parts[0], basis.at[pl.ds(wave * slabs, slabs)], sems.at[0])]
    n = 1
    for (shifts, offset, length, stride, mask), part in zip(keys, parts[1:]):
        for i, s in enumerate(shifts):
            source = lax.rem(wave + (waves - s), waves)
            start = source * slabs + (share ^ mask) * (2 * half) + offset
            copies.append(
                pltpu.make_async_copy(
                    part.at[pl.ds(i * stride, length)], basis.at[pl.ds(start, length)], sems.at[n]
                )
            )
            n += 1
    for copy in copies:
        copy.start()
    for copy in copies:
        copy.wait()

    lane = lax.broadcasted_iota(jnp.int32, (ROWS, LANES), 1)
    line = lax.broadcasted_iota(jnp.int32, (ROWS, LANES), 0)

    def chunk(c, carry):
        values = jnp.concatenate(
            [
                basis[pl.ds(place[c * UNITS + j, 0], modes)].reshape(modes * ROWS, LANES)
                for j in range(UNITS)
            ],
            axis=1,
        )
        found = jnp.dot(spread[0], values, preferred_element_type=jnp.float32)
        for j in range(UNITS):
            u = c * UNITS + j
            a = 2 * (line + place[u, 1]) - (PUP - 1)
            b = 2 * (lane + jnp.where(lane < 64, place[u, 2], place[u, 3])) - (PUP - 1)
            radius = a * a + b * b
            inside = (radius <= PUP * PUP) & (radius >= INNER * INNER)
            opening[u] = jnp.where(inside, 1.0, 0.0)
            for f in range(positions):
                path[u, f * ROWS : (f + 1) * ROWS] = jnp.where(
                    inside, found[f * ROWS : (f + 1) * ROWS, j * LANES : (j + 1) * LANES], 0.0
                )
        return carry

    lax.fori_loop(0, place.shape[0] // UNITS, chunk, 0)


def transform(positions, rows, inverse, path, opening, row_ref, scratch, wait=None):
    pupils, total, first = scratch[:2], scratch[2], scratch[3]
    batch = max(1, positions // 2)
    width = 2 * positions * LANES // UNITS

    def finish(band, columns, value):
        for f in range(columns.start // LANES, columns.stop // LANES):
            lanes = slice(f * LANES - columns.start, (f + 1) * LANES - columns.start)
            for part in range(2):
                first[
                    f * rows : (f + 1) * rows,
                    part * PUP + band * LANES : part * PUP + (band + 1) * LANES,
                ] = value[part * rows : (part + 1) * rows, lanes].astype(jnp.bfloat16)

    def product(c, columns):
        band, rows_band = CHUNKS[c]
        value = jnp.dot(
            row_ref[0, rows_band], pupils[c % 2][:, columns], preferred_element_type=jnp.float32
        )
        if c > 0 and CHUNKS[c - 1][0] == band:
            value = value + total[:, columns]
        if c + 1 < len(CHUNKS) and CHUNKS[c + 1][0] == band:
            total[:, columns] = value
        else:
            finish(band, columns, value)

    for c, (band, rows_band) in enumerate(CHUNKS):
        pupil = pupils[c % 2]
        if wait is not None:
            wait(c)
        for j, row in enumerate(band_rows(rows_band)):
            real_lines = slice(2 * ROWS * j, 2 * ROWS * j + ROWS)
            imag_lines = slice(2 * ROWS * j + ROWS, 2 * ROWS * (j + 1))
            if unit_open(row, band):
                u = c * UNITS + j
                inside = opening[u]
                for f0 in range(0, positions, batch):
                    s, k = half_turn(path[u, f0 * ROWS : (f0 + batch) * ROWS] * inverse)
                    sine = s * k
                    square = s * s
                    for f in range(f0, f0 + batch):
                        columns = slice(f * LANES, (f + 1) * LANES)
                        lines = slice((f - f0) * ROWS, (f - f0 + 1) * ROWS)
                        pupil[real_lines, columns] = (inside - square[lines]).astype(jnp.bfloat16)
                        pupil[imag_lines, columns] = sine[lines].astype(jnp.bfloat16)
            else:
                empty = jnp.zeros((ROWS, positions * LANES), jnp.bfloat16)
                pupil[real_lines] = empty
                pupil[imag_lines] = empty
            if c > 0 and j % 2 == 1:
                product(c - 1, slice(j // 2 * width, (j // 2 + 1) * width))
    for n in range(positions * LANES // width):
        product(len(CHUNKS) - 1, slice(n * width, (n + 1) * width))


def columns_of(first, column_ref):
    return [
        jnp.dot(
            first, column_ref[0, :, part * PIX : (part + 1) * PIX], preferred_element_type=jnp.float32
        )
        for part in range(2)
    ]


def chunk_copies(source, target, sems):
    return [
        pltpu.make_async_copy(
            source.at[pl.ds(c * UNITS, UNITS)], target.at[pl.ds(c * UNITS, UNITS)], sems.at[c]
        )
        for c in range(len(CHUNKS))
    ]


def whole_kernel(sizes, inverse_ref, place, where, *refs):
    positions, modes, waves, half, slabs, keys = sizes
    parts, refs = refs[: 1 + len(keys)], refs[1 + len(keys) :]
    spread, row_ref, column_ref, out_ref, path_out, opening, path, basis, sems, path_sems = refs[:10]
    scratch = refs[10:]
    copies = chunk_copies(path, path_out, path_sems)

    @pl.when(pl.program_id(0) == 0)
    def _():
        form_paths(sizes, where, place, parts, spread, path, opening, basis, sems)
        for copy in copies:
            copy.start()

    rows = PIX
    inverse = inverse_ref[pl.program_id(0)]
    transform(positions, rows, inverse, path, opening, row_ref, scratch)
    first = scratch[3]
    share = rows // waves
    for f in range(positions):
        real, imag = columns_of(first[f * rows : (f + 1) * rows], column_ref)
        intensity = real * real + imag * imag
        level = jnp.sum(
            jnp.sum(intensity, axis=0, keepdims=True), axis=1, keepdims=True
        ) / (rows * PIX)
        spectra = (intensity / (level + EPSILON)).astype(jnp.bfloat16)
        for part in range(waves):
            out_ref[part, 0, f * share : (f + 1) * share] = spectra[
                part * share : (part + 1) * share
            ]

    @pl.when(pl.program_id(0) == pl.num_programs(0) - 1)
    def _():
        for copy in copies:
            copy.wait()


def rows_kernel(positions, rows, inverse_ref, path_in, opening, row_ref, column_ref, *refs):
    image_ref, sum_ref, path, path_sems = refs[:4]
    scratch = refs[4:]
    copies = chunk_copies(path_in, path, path_sems)
    begin = pl.program_id(0) == 0

    @pl.when(begin)
    def _():
        for copy in copies:
            copy.start()

    def wait(c):
        if c > 0 and CHUNKS[c - 1][0] == CHUNKS[c][0]:
            return

        @pl.when(begin)
        def _():
            for copy, chunk in zip(copies, CHUNKS):
                if chunk[0] == CHUNKS[c][0]:
                    copy.wait()

    inverse = inverse_ref[pl.program_id(0)]
    transform(positions, rows, inverse, path, opening, row_ref, scratch, wait)
    real, imag = columns_of(scratch[3][...], column_ref)
    intensity = real * real + imag * imag
    image_ref[0] = intensity
    sums = jnp.sum(intensity.reshape(positions, rows, PIX), axis=1)
    sum_ref[0] = jnp.broadcast_to(jnp.sum(sums, axis=1, keepdims=True), (positions, LANES))


def transform_scratch(positions, rows):
    return [
        pltpu.VMEM((2 * BAND, positions * LANES), jnp.bfloat16),
        pltpu.VMEM((2 * BAND, positions * LANES), jnp.bfloat16),
        pltpu.VMEM((2 * rows, positions * LANES), jnp.float32),
        pltpu.VMEM((positions * rows, 2 * PUP), jnp.bfloat16),
    ]


def transform_cost(lengths, positions, rows):
    return pl.CostEstimate(
        flops=lengths * positions * (rows * 8 * PUP * PUP + rows * 8 * PUP * PIX + 10**8),
        bytes_accessed=8 * 2**20,
        transcendentals=0,
    )


def by_length(array):
    return pl.BlockSpec((1,) + array.shape[1:], lambda l: (l,) + (0,) * (len(array.shape) - 1))


def path_shape(positions):
    return (len(CHUNKS) * UNITS, positions * ROWS, LANES)


def whole_fields(own, got, spread, place, where, inverse, tables, sizes):
    positions, modes, waves, half, slabs = sizes
    keys = tuple(key for key, _ in got)
    arrays = [array for _, array in got]
    lengths = inverse.shape[0]
    share = positions * PIX // waves
    any_memory = pl.BlockSpec(memory_space=pl.ANY)
    return pl.pallas_call(
        functools.partial(whole_kernel, (positions, modes, waves, half, slabs, keys)),
        grid=(lengths,),
        out_shape=(
            jax.ShapeDtypeStruct((waves, lengths, share, PIX), jnp.bfloat16),
            jax.ShapeDtypeStruct(path_shape(positions), jnp.float32),
            jax.ShapeDtypeStruct((place.shape[0], ROWS, LANES), jnp.float32),
        ),
        in_specs=[SMEM, SMEM, SMEM]
        + [any_memory] * (1 + len(keys))
        + [VMEM]
        + [by_length(table) for table in tables],
        out_specs=(
            pl.BlockSpec((waves, 1, share, PIX), lambda l: (0, l, 0, 0)),
            any_memory,
            VMEM,
        ),
        scratch_shapes=[
            pltpu.VMEM(path_shape(positions), jnp.float32),
            pltpu.VMEM((waves * slabs, ROWS, LANES), jnp.bfloat16),
            pltpu.SemaphoreType.DMA((1 + sum(len(key[0]) for key in keys),)),
            pltpu.SemaphoreType.DMA((len(CHUNKS),)),
        ]
        + transform_scratch(positions, PIX),
        cost_estimate=transform_cost(lengths, positions, PIX),
        compiler_params=pltpu.CompilerParams(vmem_limit_bytes=VMEM_BYTES),
    )(inverse, place, where, own, *arrays, spread, *tables)


def row_fields(path, opening, inverse, tables, positions):
    lengths = inverse.shape[0]
    rows = tables[0].shape[2] // 2
    out_shape = (
        jax.ShapeDtypeStruct((lengths, positions * rows, PIX), jnp.float32),
        jax.ShapeDtypeStruct((lengths, positions, LANES), jnp.float32),
    )
    return pl.pallas_call(
        functools.partial(rows_kernel, positions, rows),
        grid=(lengths,),
        out_shape=out_shape,
        in_specs=[SMEM, pl.BlockSpec(memory_space=pl.ANY), VMEM]
        + [by_length(table) for table in tables],
        out_specs=tuple(by_length(one) for one in out_shape),
        scratch_shapes=[
            pltpu.VMEM(path_shape(positions), jnp.float32),
            pltpu.SemaphoreType.DMA((len(CHUNKS),)),
        ]
        + transform_scratch(positions, rows),
        cost_estimate=transform_cost(lengths, positions, rows),
        compiler_params=pltpu.CompilerParams(vmem_limit_bytes=VMEM_BYTES),
    )(inverse, path, opening, *tables)


def mix_kernel(sum_ref, weight_ref, sent_ref, image_ref, out_ref):
    count, templates, rows = out_ref.shape[:3]
    for i in range(count):
        f = pl.program_id(0) * count + i
        inverse = [
            1.0 / (sum_ref[l, pl.ds(f, 1)] / (PIX * PIX) + EPSILON)
            for l in range(image_ref.shape[0])
        ]
        inverse = [jnp.concatenate([one] * (PIX // LANES), axis=1) for one in inverse]
        blocks = []
        for start in range(i * rows, (i + 1) * rows, ROWS):
            lines = slice(start, start + ROWS)
            blocks.append(
                jnp.concatenate(
                    [sent_ref[l, lines] for l in range(sent_ref.shape[0])]
                    + [
                        (image_ref[l, lines] * inverse[l]).astype(jnp.bfloat16)
                        for l in range(image_ref.shape[0])
                    ],
                    axis=0,
                )
            )
        mixed = jnp.dot(
            weight_ref[i], jnp.concatenate(blocks, axis=1), preferred_element_type=jnp.float32
        ).astype(jnp.bfloat16)
        for n in range(len(blocks)):
            for j in range(templates):
                out_ref[i, j, n * ROWS : (n + 1) * ROWS] = mixed[
                    j * ROWS : (j + 1) * ROWS, n * PIX : (n + 1) * PIX
                ]


def mix(spread, sums, sent, images, templates, rows):
    positions = spread.shape[0]
    count = 2 if positions % 2 == 0 else 1
    return pl.pallas_call(
        mix_kernel,
        grid=(positions // count,),
        out_shape=jax.ShapeDtypeStruct((positions, templates, rows, PIX), jnp.bfloat16),
        in_specs=[
            VMEM,
            pl.BlockSpec((count,) + spread.shape[1:], lambda f: (f, 0, 0)),
            pl.BlockSpec((sent.shape[0], count * rows, PIX), lambda f: (0, f, 0)),
            pl.BlockSpec((images.shape[0], count * rows, PIX), lambda f: (0, f, 0)),
        ],
        out_specs=pl.BlockSpec((count, templates, rows, PIX), lambda f: (f, 0, 0, 0)),
        compiler_params=pltpu.CompilerParams(vmem_limit_bytes=24 * 2**20),
    )(sums, spread, sent, images)


def table_kernel(length_ref, y_ref, v_ref, u_ref, x_ref, row_ref, column_ref, token_ref):
    scale = (SAMPLING / (2.0 * PUP)) / length_ref[0, :1]
    scale = jnp.concatenate([scale] * (PIX // LANES), axis=1)
    token_ref[...] = jnp.zeros_like(token_ref)
    for start in range(0, PUP, ROWS):
        s, k = half_turn((y_ref[start : start + ROWS] * v_ref[...]) * scale)
        cosine, sine = 1.0 - s * s, s * k
        lower, upper = slice(start, start + ROWS), slice(PUP + start, PUP + start + ROWS)
        column_ref[0, lower, :PIX] = cosine.astype(jnp.bfloat16)
        column_ref[0, lower, PIX:] = (-sine).astype(jnp.bfloat16)
        column_ref[0, upper, :PIX] = sine.astype(jnp.bfloat16)
        column_ref[0, upper, PIX:] = cosine.astype(jnp.bfloat16)
    rows = u_ref.shape[0]
    imag = (lax.broadcasted_iota(jnp.int32, (ROWS, 2 * BAND), 1) // ROWS) % 2 == 1
    for band in range(BANDS):
        for start in range(0, rows, ROWS):
            s, k = half_turn((u_ref[start : start + ROWS] * x_ref[band]) * scale)
            cosine, sine = 1.0 - s * s, s * k
            row_ref[0, band, start : start + ROWS] = jnp.where(imag, sine, cosine).astype(
                jnp.bfloat16
            )
            row_ref[0, band, rows + start : rows + start + ROWS] = jnp.where(
                imag, cosine, -sine
            ).astype(jnp.bfloat16)


def tables(length, first_row, rows):
    lengths = length.shape[0]
    y = 2 * np.concatenate([band_columns(band) for band in range(BANDS)]) - PUP + 1
    v = np.arange(PIX) - PIX // 2
    u = first_row + jnp.arange(rows, dtype=jnp.int32) - PIX // 2
    x = np.array(
        [[row + i for row in band_rows(band) for i in range(ROWS)] for band in range(BANDS)]
    )
    x = np.repeat(x.reshape(BANDS, UNITS, 1, ROWS), 2, axis=2).reshape(BANDS, 1, 2 * BAND)
    whole = lambda *shape: pl.BlockSpec(shape, lambda l: (0,) * len(shape))
    return pl.pallas_call(
        table_kernel,
        grid=(lengths,),
        out_shape=(
            jax.ShapeDtypeStruct((lengths, BANDS, 2 * rows, 2 * BAND), jnp.bfloat16),
            jax.ShapeDtypeStruct((lengths, 2 * PUP, 2 * PIX), jnp.bfloat16),
            jax.ShapeDtypeStruct((8, LANES), jnp.float32),
        ),
        in_specs=[
            pl.BlockSpec((1, 8, LANES), lambda l: (l, 0, 0)),
            whole(PUP, 1),
            whole(1, PIX),
            whole(rows, 1),
            whole(BANDS, 1, 2 * BAND),
        ],
        out_specs=(
            pl.BlockSpec((1, BANDS, 2 * rows, 2 * BAND), lambda l: (l, 0, 0, 0)),
            pl.BlockSpec((1, 2 * PUP, 2 * PIX), lambda l: (l, 0, 0)),
            whole(8, LANES),
        ),
        cost_estimate=pl.CostEstimate(
            flops=lengths * 30 * PUP * PIX, bytes_accessed=lengths * 4 * PUP * PIX * 2, transcendentals=0
        ),
        compiler_params=pltpu.CompilerParams(vmem_limit_bytes=VMEM_BYTES),
    )(
        length,
        jnp.asarray(y[:, None].astype(np.float32)),
        jnp.asarray(v[None, :].astype(np.float32)),
        u.astype(jnp.float32)[:, None],
        jnp.asarray((2 * x - PUP + 1).astype(np.float32)),
    )


def add_over_wave(x, waves):
    step = 1
    while step < waves:
        x = x + lax.ppermute(x, "wave", [(i, i ^ step) for i in range(waves)])
        step *= 2
    return x


def local(mode_basis, coef_table, table_index, wave_lengths, sed_table, template_ids):
    waves = lax.axis_size("wave")
    mine = lax.axis_index("wave")
    modes = mode_basis.shape[0]
    positions = table_index.shape[0]
    rows = PIX // waves
    lengths = wave_lengths.shape[0]
    sent_lengths = lengths // 2

    share = (lax.axis_index("groups") % 2) * 4 + lax.axis_index("field") % 4
    where = jnp.stack([mine, share]).astype(jnp.int32)
    plan = layout(waves, modes)
    half, slabs, _, place = plan
    own, piece, packed = pack_rows(mode_basis, wave_lengths, plan, where)
    parts = along_wave(piece, waves)

    selector = (
        table_index[:, None] == jnp.arange(coef_table.shape[0], dtype=jnp.int32)[None, :]
    ).astype(jnp.bfloat16)
    coeffs = jnp.dot(selector, coef_table, preferred_element_type=jnp.float32)
    one_hot = (
        template_ids[:, :, None]
        == jnp.arange(sed_table.shape[0], dtype=jnp.int32)[None, None, :]
    ).astype(jnp.float32)
    raw_weights = jnp.einsum("fjn,nl->fjl", one_hot, sed_table, precision=lax.Precision.HIGHEST)
    weights = (raw_weights / jnp.sum(raw_weights, axis=2, keepdims=True)).astype(jnp.bfloat16)
    templates = weights.shape[1]
    split = weights.reshape(positions, templates, waves, lengths)
    weights = jnp.concatenate(
        [
            split[..., :sent_lengths].reshape(positions, templates, -1),
            split[..., sent_lengths:].reshape(positions, templates, -1),
        ],
        axis=2,
    )
    path_spread, mix_spread, spread_token = spreads(coeffs.astype(jnp.bfloat16)[None], weights)
    own_length = jnp.broadcast_to(
        wave_lengths[:sent_lengths, None, None], (sent_lengths, 8, LANES)
    )
    own_row, own_column, own_token = tables(own_length, 0, PIX)

    far = tuple(s for s in range(1, waves) if min(s, waves - s) > waves // 4)
    near = tuple(s for s in range(1, waves) if s not in far)
    halves = split_parts([parts[s - 1] for s in near], half, [packed])
    got = gather_halves(halves, half, near, [own_token, spread_token])
    every, inverse = kept_lengths(parts, where, wave_lengths, half, sent_lengths)
    all_row, all_column, all_token = tables(every, mine * rows, rows)
    pieces = [parts[s - 1] for s in far]
    pieces = pieces[0] if len(pieces) == 1 else jnp.concatenate(pieces)
    got = got + gather_direct(pieces, half, far, [all_token])

    spectra, path, opening = whole_fields(
        own,
        got,
        path_spread,
        place,
        where,
        1.0 / wave_lengths[:sent_lengths],
        (own_row, own_column),
        (positions, modes, waves, half, slabs),
    )
    sent = lax.all_to_all(spectra, "wave", split_axis=0, concat_axis=0, tiled=True)
    sent = sent.reshape(waves * sent_lengths, positions * rows, PIX)
    images, sums = row_fields(path, opening, inverse, (all_row, all_column), positions)
    return mix(mix_spread, add_over_wave(sums, waves), sent, images, templates, rows)


def solution(mesh):
    return jax.shard_map(
        local,
        mesh=mesh,
        in_specs=(
            P(None, "wave", None),
            P(),
            P(("groups", "field")),
            P("wave"),
            P(),
            P(("groups", "field"), None),
        ),
        out_specs=P(("groups", "field"), None, "wave", None),
        check_vma=False,
    )
```

```python
import functools
import math

import jax
import jax.numpy as jnp
import numpy as np
from jax import lax
from jax.experimental import pallas as pl
from jax.experimental.pallas import tpu as pltpu
from jax.sharding import PartitionSpec as P

PUP = 512
PIX = 256
TWO_PI = 2.0 * math.pi
SAMPLING = 0.25
EPSILON = 1e-06
INNER = 61 * PUP // 100
BAND = 128
BANDS = PUP // BAND
ROWS = 16
LANES = 128
UNITS = BAND // ROWS
VMEM_BYTES = 60 * 2**20
SHARES = 8

SMEM = pl.BlockSpec(memory_space=pltpu.SMEM)
VMEM = pl.BlockSpec(memory_space=pltpu.VMEM)

SIN_POLY = (4.4428679, -7.30744341, 3.59478797, -0.78437376)
COS_POLY = (1.4142135, -6.97885099, 5.73946117, -1.88356298, 0.31069817)


def half_turn(turns):
    magic = jnp.float32(12582912.0)
    r = turns - ((turns + magic) - magic)
    z = r * r
    s = jnp.float32(SIN_POLY[-1])
    for value in SIN_POLY[-2::-1]:
        s = s * z + value
    k = jnp.float32(COS_POLY[-1])
    for value in COS_POLY[-2::-1]:
        k = k * z + value
    return s * r, k


def band_rows(band):
    low, high = PUP // 2 - 64 * (band + 1), PUP // 2 + 64 * band
    return [low + ROWS * i for i in range(4)] + [high + ROWS * i for i in range(4)]


def band_columns(band):
    low, high = PUP // 2 - 64 * (band + 1), PUP // 2 + 64 * band
    sides = (high, low) if band % 2 == 0 else (low, high)
    return np.concatenate([side + np.arange(64) for side in sides])


def unit_open(row, band):
    a = 2 * (row + np.arange(ROWS)) - PUP + 1
    b = 2 * band_columns(band) - PUP + 1
    radius = a[:, None] ** 2 + b[None, :] ** 2
    return bool(np.any((radius <= PUP * PUP) & (radius >= INNER * INNER)))


CHUNKS = [
    (band, rows)
    for band in range(BANDS)
    for rows in range(BANDS)
    if any(unit_open(row, band) for row in band_rows(rows))
]


@functools.lru_cache(None)
def layout(waves, modes):
    per = PUP // waves
    lists = []
    for wave in range(waves):
        lists.append(
            [
                (band, row)
                for band in range(BANDS)
                for row in range(wave * per, (wave + 1) * per, ROWS)
                if unit_open(row, band)
            ]
        )
    count = max(len(one) for one in lists)
    half = -(-count * modes // (2 * SHARES))
    slabs = 2 * SHARES * half
    pack = np.zeros((waves, count, 3), np.int32)
    for wave, one in enumerate(lists):
        for i, (band, row) in enumerate(one):
            columns = band_columns(band)
            pack[wave, i] = (columns[0] // LANES * LANES, columns[64] // LANES * LANES, row - wave * per)
    place = np.zeros((len(CHUNKS) * UNITS, 4), np.int32)
    for c, (band, rows) in enumerate(CHUNKS):
        columns = band_columns(band)
        for j, row in enumerate(band_rows(rows)):
            wave = row // per
            slab = 0
            if (band, row) in lists[wave]:
                slab = wave * slabs + lists[wave].index((band, row)) * modes
            place[c * UNITS + j] = (slab, row, columns[0], columns[64] - 64)
    return half, slabs, pack, place


def pack_slab(table, basis, line, mode):
    left = lax.broadcasted_iota(jnp.int32, (ROWS, LANES), 1) < 64
    first = pl.multiple_of(table[line, 0], LANES)
    second = pl.multiple_of(table[line, 1], LANES)
    row = pl.multiple_of(table[line, 2], ROWS)
    one = basis[mode, pl.ds(row, ROWS), pl.ds(first, LANES)].astype(jnp.float32)
    two = basis[mode, pl.ds(row, ROWS), pl.ds(second, LANES)].astype(jnp.float32)
    return jnp.where(left, one, two).astype(basis.dtype)


def own_kernel(count, where, table, basis, _, own, token):
    modes = basis.shape[0]
    token[...] = jnp.zeros_like(token)

    def unit(i, carry):
        for k in range(modes):
            own[i * modes + k] = pack_slab(table, basis, where[0] * count + i, k)
        return carry

    lax.fori_loop(0, count, unit, 0)
    for n in range(count * modes, own.shape[0]):
        own[n] = jnp.zeros((ROWS, LANES), own.dtype)


def piece_kernel(count, half, where, table, lengths, basis, piece, token):
    modes = basis.shape[0]
    token[...] = jnp.zeros_like(token)

    def pair(i, carry):
        for m in (2 * i, 2 * i + 1):
            n = where[1] * (2 * half) + m
            unit = n // modes
            mode = n - unit * modes
            unit = jnp.minimum(unit, count - 1)
            piece[m] = pack_slab(table, basis, where[0] * count + unit, mode)
        return carry

    lax.fori_loop(0, half, pair, 0)
    line = lax.broadcasted_iota(jnp.int32, (ROWS, LANES), 0)
    slab = jnp.zeros((ROWS, LANES), jnp.float32)
    for i in range(lengths.shape[0]):
        rest = jnp.full((ROWS, LANES), lengths[i], jnp.float32)
        for limb in range(3):
            value = rest.astype(jnp.bfloat16).astype(jnp.float32)
            slab = jnp.where(line == 3 * i + limb, value, slab)
            rest = rest - value
    piece[2 * half] = slab.astype(piece.dtype)


def pack_rows(basis, wave_lengths, plan, where):
    half, slabs, table, _ = plan
    count, table = table.shape[1], table.reshape(-1, 3)
    params = pltpu.CompilerParams(vmem_limit_bytes=VMEM_BYTES)
    piece, token = pl.pallas_call(
        functools.partial(piece_kernel, count, half),
        out_shape=(
            jax.ShapeDtypeStruct((2 * half + 1, ROWS, LANES), basis.dtype),
            jax.ShapeDtypeStruct((8, LANES), jnp.float32),
        ),
        in_specs=[SMEM, SMEM, SMEM, VMEM],
        out_specs=(VMEM, VMEM),
        compiler_params=params,
    )(where, table, wave_lengths, basis)
    own, token = pl.pallas_call(
        functools.partial(own_kernel, count),
        out_shape=(
            jax.ShapeDtypeStruct((slabs, ROWS, LANES), basis.dtype),
            jax.ShapeDtypeStruct((8, LANES), jnp.float32),
        ),
        in_specs=[SMEM, SMEM, VMEM, VMEM],
        out_specs=(VMEM, VMEM),
        compiler_params=params,
    )(where, table, basis, token)
    return own, piece, token


def split_kernel(half, count, *refs):
    parts, (low_ref, high_ref) = refs[:count], refs[-2:]
    for s, part in enumerate(parts):
        low_ref[s * half : (s + 1) * half] = part[:half]
        high_ref[s * half : (s + 1) * half] = part[half : 2 * half]


def split_parts(parts, half, tokens):
    slabs = jax.ShapeDtypeStruct((len(parts) * half, ROWS, LANES), parts[0].dtype)
    return pl.pallas_call(
        functools.partial(split_kernel, half, len(parts)),
        out_shape=(slabs, slabs),
        in_specs=[VMEM] * (len(parts) + len(tokens)),
        out_specs=(VMEM,) * 2,
        compiler_params=pltpu.CompilerParams(vmem_limit_bytes=VMEM_BYTES),
    )(*parts, *tokens)


def lengths_kernel(sent, where, own_lengths, *refs):
    parts, (length_ref, inverse_ref) = refs[:-2], refs[-2:]
    wave, waves = where[0], len(parts) + 1
    kept = own_lengths.shape[0] - sent
    for s in range(waves):
        for i in range(kept):
            if s == 0:
                value = jnp.full((8, LANES), own_lengths[sent + i], jnp.float32)
            else:
                slab = parts[s - 1][0].astype(jnp.float32)
                line = 3 * (sent + i)
                value = (slab[line : line + 1] + slab[line + 1 : line + 2]) + slab[
                    line + 2 : line + 3
                ]
                value = jnp.broadcast_to(value, (8, LANES))
            place = lax.rem(wave + (waves - s), waves) * kept + i
            length_ref[place] = value
            inverse_ref[place] = (1.0 / value)[0, 0]


def kept_lengths(parts, where, wave_lengths, half, sent):
    count = (len(parts) + 1) * (wave_lengths.shape[0] - sent)
    last = pl.BlockSpec((1, ROWS, LANES), lambda i: (2 * half, 0, 0))
    return pl.pallas_call(
        functools.partial(lengths_kernel, sent),
        grid=(1,),
        out_shape=(
            jax.ShapeDtypeStruct((count, 8, LANES), jnp.float32),
            jax.ShapeDtypeStruct((count,), jnp.float32),
        ),
        in_specs=[SMEM, SMEM] + [last] * len(parts),
        out_specs=(VMEM, SMEM),
        compiler_params=pltpu.CompilerParams(vmem_limit_bytes=VMEM_BYTES),
    )(where, wave_lengths, *parts)


def after(arrays, tokens):
    any_memory = pl.BlockSpec(memory_space=pl.ANY)
    return pl.pallas_call(
        lambda *refs: None,
        out_shape=tuple(jax.ShapeDtypeStruct(x.shape, x.dtype) for x in arrays),
        in_specs=[any_memory] * len(arrays) + [VMEM] * len(tokens),
        out_specs=(any_memory,) * len(arrays),
        input_output_aliases={i: i for i in range(len(arrays))},
    )(*arrays, *tokens)


def along_wave(piece, waves):
    return [
        lax.ppermute(piece, "wave", [(i, (i + s) % waves) for i in range(waves)])
        for s in range(1, waves)
    ]


def swap(x, mask):
    groups, fields = lax.axis_size("groups"), lax.axis_size("field")
    pairs = [
        (g * fields + f, (g ^ (mask >> 2)) * fields + (f ^ (mask & 3)))
        for g in range(groups)
        for f in range(fields)
    ]
    return lax.ppermute(x, ("groups", "field"), pairs)


def gather_halves(halves, half, shifts, tokens):
    routes = ((2, 4), (4, 2))
    near = [swap(mine, mask) for mine, route in zip(halves, routes) for mask in route]
    near = after(near + list(halves), tokens)
    got = [(h, mine, 0) for h, mine in enumerate(near[4:])]
    for h, (one, two) in enumerate(routes):
        got.append((h, near[2 * h], one))
        got.append((h, near[2 * h + 1], two))
        got.append((h, swap(near[2 * h], two), one | two))
    got = got + [(h, swap(array, 1), mask | 1) for h, array, mask in got]
    return [((shifts, h * half, half, half, mask), array) for h, array, mask in got]


def gather_direct(pieces, half, shifts, tokens):
    masks = (6, 2, 4)
    near = after([swap(pieces, mask) for mask in masks], tokens)
    got = [(0, pieces)] + list(zip(masks, near))
    got = got + [(mask | 1, swap(array, 1)) for mask, array in got]
    return [((shifts, 0, 2 * half, 2 * half + 1, mask), array) for mask, array in got]


def spread_kernel(*refs):
    count = len(refs) // 2
    refs[-1][...] = jnp.zeros_like(refs[-1])
    for small_ref, big_ref in zip(refs[:count], refs[count:-1]):
        _, many, wide = small_ref.shape
        tall, long = many * ROWS, wide * ROWS
        down = lax.broadcasted_iota(jnp.int32, (tall, many), 0) // ROWS
        down = (down == lax.broadcasted_iota(jnp.int32, (tall, many), 1)).astype(jnp.float32)
        along = lax.broadcasted_iota(jnp.int32, (wide, long), 1) // ROWS
        along = (along == lax.broadcasted_iota(jnp.int32, (wide, long), 0)).astype(jnp.float32)
        same = (lax.broadcasted_iota(jnp.int32, (tall, long), 0) % ROWS) == (
            lax.broadcasted_iota(jnp.int32, (tall, long), 1) % ROWS
        )
        down, along = down.astype(jnp.bfloat16), along.astype(jnp.bfloat16)
        for i in range(small_ref.shape[0]):
            half = jnp.dot(down, small_ref[i], preferred_element_type=jnp.float32)
            whole = jnp.dot(half.astype(jnp.bfloat16), along, preferred_element_type=jnp.float32)
            big_ref[i] = jnp.where(same, whole, 0.0).astype(jnp.bfloat16)


def spreads(*matrices):
    return pl.pallas_call(
        spread_kernel,
        out_shape=tuple(
            jax.ShapeDtypeStruct((m.shape[0], m.shape[1] * ROWS, m.shape[2] * ROWS), jnp.bfloat16)
            for m in matrices
        )
        + (jax.ShapeDtypeStruct((8, LANES), jnp.float32),),
        compiler_params=pltpu.CompilerParams(vmem_limit_bytes=VMEM_BYTES),
    )(*matrices)


def form_paths(sizes, where, place, parts, spread, path, opening, basis, sems):
    positions, modes, waves, half, slabs, keys = sizes
    wave, share = where[0], where[1]
    copies = [pltpu.make_async_copy(parts[0], basis.at[pl.ds(wave * slabs, slabs)], sems.at[0])]
    n = 1
    for (shifts, offset, length, stride, mask), part in zip(keys, parts[1:]):
        for i, s in enumerate(shifts):
            source = lax.rem(wave + (waves - s), waves)
            start = source * slabs + (share ^ mask) * (2 * half) + offset
            copies.append(
                pltpu.make_async_copy(
                    part.at[pl.ds(i * stride, length)], basis.at[pl.ds(start, length)], sems.at[n]
                )
            )
            n += 1
    for copy in copies:
        copy.start()
    for copy in copies:
        copy.wait()

    lane = lax.broadcasted_iota(jnp.int32, (ROWS, LANES), 1)
    line = lax.broadcasted_iota(jnp.int32, (ROWS, LANES), 0)

    def chunk(c, carry):
        values = jnp.concatenate(
            [
                basis[pl.ds(place[c * UNITS + j, 0], modes)].reshape(modes * ROWS, LANES)
                for j in range(UNITS)
            ],
            axis=1,
        )
        found = jnp.dot(spread[0], values, preferred_element_type=jnp.float32)
        for j in range(UNITS):
            u = c * UNITS + j
            a = 2 * (line + place[u, 1]) - (PUP - 1)
            b = 2 * (lane + jnp.where(lane < 64, place[u, 2], place[u, 3])) - (PUP - 1)
            radius = a * a + b * b
            inside = (radius <= PUP * PUP) & (radius >= INNER * INNER)
            opening[u] = jnp.where(inside, 1.0, 0.0)
            for f in range(positions):
                path[u, f * ROWS : (f + 1) * ROWS] = jnp.where(
                    inside, found[f * ROWS : (f + 1) * ROWS, j * LANES : (j + 1) * LANES], 0.0
                )
        return carry

    lax.fori_loop(0, place.shape[0] // UNITS, chunk, 0)


def transform(positions, rows, inverse, path, opening, row_ref, scratch, wait=None):
    pupils, total, first = scratch[:2], scratch[2], scratch[3]
    batch = max(1, positions // 2)
    width = 2 * positions * LANES // UNITS

    def finish(band, columns, value):
        for f in range(columns.start // LANES, columns.stop // LANES):
            lanes = slice(f * LANES - columns.start, (f + 1) * LANES - columns.start)
            for part in range(2):
                first[
                    f * rows : (f + 1) * rows,
                    part * PUP + band * LANES : part * PUP + (band + 1) * LANES,
                ] = value[part * rows : (part + 1) * rows, lanes].astype(jnp.bfloat16)

    def product(c, columns):
        band, rows_band = CHUNKS[c]
        value = jnp.dot(
            row_ref[0, rows_band], pupils[c % 2][:, columns], preferred_element_type=jnp.float32
        )
        if c > 0 and CHUNKS[c - 1][0] == band:
            value = value + total[:, columns]
        if c + 1 < len(CHUNKS) and CHUNKS[c + 1][0] == band:
            total[:, columns] = value
        else:
            finish(band, columns, value)

    for c, (band, rows_band) in enumerate(CHUNKS):
        pupil = pupils[c % 2]
        if wait is not None:
            wait(c)
        for j, row in enumerate(band_rows(rows_band)):
            real_lines = slice(2 * ROWS * j, 2 * ROWS * j + ROWS)
            imag_lines = slice(2 * ROWS * j + ROWS, 2 * ROWS * (j + 1))
            if unit_open(row, band):
                u = c * UNITS + j
                inside = opening[u]
                for f0 in range(0, positions, batch):
                    s, k = half_turn(path[u, f0 * ROWS : (f0 + batch) * ROWS] * inverse)
                    sine = s * k
                    square = s * s
                    for f in range(f0, f0 + batch):
                        columns = slice(f * LANES, (f + 1) * LANES)
                        lines = slice((f - f0) * ROWS, (f - f0 + 1) * ROWS)
                        pupil[real_lines, columns] = (inside - square[lines]).astype(jnp.bfloat16)
                        pupil[imag_lines, columns] = sine[lines].astype(jnp.bfloat16)
            else:
                empty = jnp.zeros((ROWS, positions * LANES), jnp.bfloat16)
                pupil[real_lines] = empty
                pupil[imag_lines] = empty
            if c > 0 and j % 2 == 1:
                product(c - 1, slice(j // 2 * width, (j // 2 + 1) * width))
    for n in range(positions * LANES // width):
        product(len(CHUNKS) - 1, slice(n * width, (n + 1) * width))


def columns_of(first, column_ref):
    return [
        jnp.dot(
            first, column_ref[0, :, part * PIX : (part + 1) * PIX], preferred_element_type=jnp.float32
        )
        for part in range(2)
    ]


def chunk_copies(source, target, sems):
    return [
        pltpu.make_async_copy(
            source.at[pl.ds(c * UNITS, UNITS)], target.at[pl.ds(c * UNITS, UNITS)], sems.at[c]
        )
        for c in range(len(CHUNKS))
    ]


def whole_kernel(sizes, inverse_ref, place, where, *refs):
    positions, modes, waves, half, slabs, keys = sizes
    parts, refs = refs[: 1 + len(keys)], refs[1 + len(keys) :]
    spread, row_ref, column_ref, out_ref, path_out, opening, path, basis, sems, path_sems = refs[:10]
    scratch = refs[10:]
    copies = chunk_copies(path, path_out, path_sems)

    @pl.when(pl.program_id(0) == 0)
    def _():
        form_paths(sizes, where, place, parts, spread, path, opening, basis, sems)
        for copy in copies:
            copy.start()

    rows = PIX
    inverse = inverse_ref[pl.program_id(0)]
    transform(positions, rows, inverse, path, opening, row_ref, scratch)
    first = scratch[3]
    share = rows // waves
    for f in range(positions):
        real, imag = columns_of(first[f * rows : (f + 1) * rows], column_ref)
        intensity = real * real + imag * imag
        level = jnp.sum(
            jnp.sum(intensity, axis=0, keepdims=True), axis=1, keepdims=True
        ) / (rows * PIX)
        spectra = (intensity / (level + EPSILON)).astype(jnp.bfloat16)
        for part in range(waves):
            out_ref[part, 0, f * share : (f + 1) * share] = spectra[
                part * share : (part + 1) * share
            ]

    @pl.when(pl.program_id(0) == pl.num_programs(0) - 1)
    def _():
        for copy in copies:
            copy.wait()


def rows_kernel(positions, rows, inverse_ref, path_in, opening, row_ref, column_ref, *refs):
    image_ref, sum_ref, path, path_sems = refs[:4]
    scratch = refs[4:]
    copies = chunk_copies(path_in, path, path_sems)
    begin = pl.program_id(0) == 0

    @pl.when(begin)
    def _():
        for copy in copies:
            copy.start()

    def wait(c):
        if c > 0 and CHUNKS[c - 1][0] == CHUNKS[c][0]:
            return

        @pl.when(begin)
        def _():
            for copy, chunk in zip(copies, CHUNKS):
                if chunk[0] == CHUNKS[c][0]:
                    copy.wait()

    inverse = inverse_ref[pl.program_id(0)]
    transform(positions, rows, inverse, path, opening, row_ref, scratch, wait)
    real, imag = columns_of(scratch[3][...], column_ref)
    intensity = real * real + imag * imag
    image_ref[0] = intensity
    sums = jnp.sum(intensity.reshape(positions, rows, PIX), axis=1)
    sum_ref[0] = jnp.broadcast_to(jnp.sum(sums, axis=1, keepdims=True), (positions, LANES))


def transform_scratch(positions, rows):
    return [
        pltpu.VMEM((2 * BAND, positions * LANES), jnp.bfloat16),
        pltpu.VMEM((2 * BAND, positions * LANES), jnp.bfloat16),
        pltpu.VMEM((2 * rows, positions * LANES), jnp.float32),
        pltpu.VMEM((positions * rows, 2 * PUP), jnp.bfloat16),
    ]


def transform_cost(lengths, positions, rows):
    return pl.CostEstimate(
        flops=lengths * positions * (rows * 8 * PUP * PUP + rows * 8 * PUP * PIX + 10**8),
        bytes_accessed=8 * 2**20,
        transcendentals=0,
    )


def by_length(array):
    return pl.BlockSpec((1,) + array.shape[1:], lambda l: (l,) + (0,) * (len(array.shape) - 1))


def path_shape(positions):
    return (len(CHUNKS) * UNITS, positions * ROWS, LANES)


def whole_fields(own, got, spread, place, where, inverse, tables, sizes):
    positions, modes, waves, half, slabs = sizes
    keys = tuple(key for key, _ in got)
    arrays = [array for _, array in got]
    lengths = inverse.shape[0]
    share = positions * PIX // waves
    any_memory = pl.BlockSpec(memory_space=pl.ANY)
    return pl.pallas_call(
        functools.partial(whole_kernel, (positions, modes, waves, half, slabs, keys)),
        grid=(lengths,),
        out_shape=(
            jax.ShapeDtypeStruct((waves, lengths, share, PIX), jnp.bfloat16),
            jax.ShapeDtypeStruct(path_shape(positions), jnp.float32),
            jax.ShapeDtypeStruct((place.shape[0], ROWS, LANES), jnp.float32),
        ),
        in_specs=[SMEM, SMEM, SMEM]
        + [any_memory] * (1 + len(keys))
        + [VMEM]
        + [by_length(table) for table in tables],
        out_specs=(
            pl.BlockSpec((waves, 1, share, PIX), lambda l: (0, l, 0, 0)),
            any_memory,
            VMEM,
        ),
        scratch_shapes=[
            pltpu.VMEM(path_shape(positions), jnp.float32),
            pltpu.VMEM((waves * slabs, ROWS, LANES), jnp.bfloat16),
            pltpu.SemaphoreType.DMA((1 + sum(len(key[0]) for key in keys),)),
            pltpu.SemaphoreType.DMA((len(CHUNKS),)),
        ]
        + transform_scratch(positions, PIX),
        cost_estimate=transform_cost(lengths, positions, PIX),
        compiler_params=pltpu.CompilerParams(vmem_limit_bytes=VMEM_BYTES),
    )(inverse, place, where, own, *arrays, spread, *tables)


def row_fields(path, opening, inverse, tables, positions):
    lengths = inverse.shape[0]
    rows = tables[0].shape[2] // 2
    out_shape = (
        jax.ShapeDtypeStruct((lengths, positions * rows, PIX), jnp.float32),
        jax.ShapeDtypeStruct((lengths, positions, LANES), jnp.float32),
    )
    return pl.pallas_call(
        functools.partial(rows_kernel, positions, rows),
        grid=(lengths,),
        out_shape=out_shape,
        in_specs=[SMEM, pl.BlockSpec(memory_space=pl.ANY), VMEM]
        + [by_length(table) for table in tables],
        out_specs=tuple(by_length(one) for one in out_shape),
        scratch_shapes=[
            pltpu.VMEM(path_shape(positions), jnp.float32),
            pltpu.SemaphoreType.DMA((len(CHUNKS),)),
        ]
        + transform_scratch(positions, rows),
        cost_estimate=transform_cost(lengths, positions, rows),
        compiler_params=pltpu.CompilerParams(vmem_limit_bytes=VMEM_BYTES),
    )(inverse, path, opening, *tables)


def mix_kernel(sum_ref, weight_ref, sent_ref, image_ref, out_ref):
    count, templates, rows = out_ref.shape[:3]
    for i in range(count):
        f = pl.program_id(0) * count + i
        inverse = [
            1.0 / (sum_ref[l, pl.ds(f, 1)] / (PIX * PIX) + EPSILON)
            for l in range(image_ref.shape[0])
        ]
        inverse = [jnp.concatenate([one] * (PIX // LANES), axis=1) for one in inverse]
        blocks = []
        for start in range(i * rows, (i + 1) * rows, ROWS):
            lines = slice(start, start + ROWS)
            blocks.append(
                jnp.concatenate(
                    [sent_ref[l, lines] for l in range(sent_ref.shape[0])]
                    + [
                        (image_ref[l, lines] * inverse[l]).astype(jnp.bfloat16)
                        for l in range(image_ref.shape[0])
                    ],
                    axis=0,
                )
            )
        mixed = jnp.dot(
            weight_ref[i], jnp.concatenate(blocks, axis=1), preferred_element_type=jnp.float32
        ).astype(jnp.bfloat16)
        for n in range(len(blocks)):
            for j in range(templates):
                out_ref[i, j, n * ROWS : (n + 1) * ROWS] = mixed[
                    j * ROWS : (j + 1) * ROWS, n * PIX : (n + 1) * PIX
                ]


def mix(spread, sums, sent, images, templates, rows):
    positions = spread.shape[0]
    count = 2 if positions % 2 == 0 else 1
    return pl.pallas_call(
        mix_kernel,
        grid=(positions // count,),
        out_shape=jax.ShapeDtypeStruct((positions, templates, rows, PIX), jnp.bfloat16),
        in_specs=[
            VMEM,
            pl.BlockSpec((count,) + spread.shape[1:], lambda f: (f, 0, 0)),
            pl.BlockSpec((sent.shape[0], count * rows, PIX), lambda f: (0, f, 0)),
            pl.BlockSpec((images.shape[0], count * rows, PIX), lambda f: (0, f, 0)),
        ],
        out_specs=pl.BlockSpec((count, templates, rows, PIX), lambda f: (f, 0, 0, 0)),
        compiler_params=pltpu.CompilerParams(vmem_limit_bytes=24 * 2**20),
    )(sums, spread, sent, images)


def table_kernel(length_ref, y_ref, v_ref, u_ref, x_ref, row_ref, column_ref, token_ref):
    scale = (SAMPLING / (2.0 * PUP)) / length_ref[0, :1]
    scale = jnp.concatenate([scale] * (PIX // LANES), axis=1)
    token_ref[...] = jnp.zeros_like(token_ref)
    for start in range(0, PUP, ROWS):
        s, k = half_turn((y_ref[start : start + ROWS] * v_ref[...]) * scale)
        cosine, sine = 1.0 - s * s, s * k
        lower, upper = slice(start, start + ROWS), slice(PUP + start, PUP + start + ROWS)
        column_ref[0, lower, :PIX] = cosine.astype(jnp.bfloat16)
        column_ref[0, lower, PIX:] = (-sine).astype(jnp.bfloat16)
        column_ref[0, upper, :PIX] = sine.astype(jnp.bfloat16)
        column_ref[0, upper, PIX:] = cosine.astype(jnp.bfloat16)
    rows = u_ref.shape[0]
    imag = (lax.broadcasted_iota(jnp.int32, (ROWS, 2 * BAND), 1) // ROWS) % 2 == 1
    for band in range(BANDS):
        for start in range(0, rows, ROWS):
            s, k = half_turn((u_ref[start : start + ROWS] * x_ref[band]) * scale)
            cosine, sine = 1.0 - s * s, s * k
            row_ref[0, band, start : start + ROWS] = jnp.where(imag, sine, cosine).astype(
                jnp.bfloat16
            )
            row_ref[0, band, rows + start : rows + start + ROWS] = jnp.where(
                imag, cosine, -sine
            ).astype(jnp.bfloat16)


def tables(length, first_row, rows):
    lengths = length.shape[0]
    y = 2 * np.concatenate([band_columns(band) for band in range(BANDS)]) - PUP + 1
    v = np.arange(PIX) - PIX // 2
    u = first_row + jnp.arange(rows, dtype=jnp.int32) - PIX // 2
    x = np.array(
        [[row + i for row in band_rows(band) for i in range(ROWS)] for band in range(BANDS)]
    )
    x = np.repeat(x.reshape(BANDS, UNITS, 1, ROWS), 2, axis=2).reshape(BANDS, 1, 2 * BAND)
    whole = lambda *shape: pl.BlockSpec(shape, lambda l: (0,) * len(shape))
    return pl.pallas_call(
        table_kernel,
        grid=(lengths,),
        out_shape=(
            jax.ShapeDtypeStruct((lengths, BANDS, 2 * rows, 2 * BAND), jnp.bfloat16),
            jax.ShapeDtypeStruct((lengths, 2 * PUP, 2 * PIX), jnp.bfloat16),
            jax.ShapeDtypeStruct((8, LANES), jnp.float32),
        ),
        in_specs=[
            pl.BlockSpec((1, 8, LANES), lambda l: (l, 0, 0)),
            whole(PUP, 1),
            whole(1, PIX),
            whole(rows, 1),
            whole(BANDS, 1, 2 * BAND),
        ],
        out_specs=(
            pl.BlockSpec((1, BANDS, 2 * rows, 2 * BAND), lambda l: (l, 0, 0, 0)),
            pl.BlockSpec((1, 2 * PUP, 2 * PIX), lambda l: (l, 0, 0)),
            whole(8, LANES),
        ),
        cost_estimate=pl.CostEstimate(
            flops=lengths * 30 * PUP * PIX, bytes_accessed=lengths * 4 * PUP * PIX * 2, transcendentals=0
        ),
        compiler_params=pltpu.CompilerParams(vmem_limit_bytes=VMEM_BYTES),
    )(
        length,
        jnp.asarray(y[:, None].astype(np.float32)),
        jnp.asarray(v[None, :].astype(np.float32)),
        u.astype(jnp.float32)[:, None],
        jnp.asarray((2 * x - PUP + 1).astype(np.float32)),
    )


def add_over_wave(x, waves):
    step = 1
    while step < waves:
        x = x + lax.ppermute(x, "wave", [(i, i ^ step) for i in range(waves)])
        step *= 2
    return x


def local(mode_basis, coef_table, table_index, wave_lengths, sed_table, template_ids):
    waves = lax.axis_size("wave")
    mine = lax.axis_index("wave")
    modes = mode_basis.shape[0]
    positions = table_index.shape[0]
    rows = PIX // waves
    lengths = wave_lengths.shape[0]
    sent_lengths = lengths // 2

    share = (lax.axis_index("groups") % 2) * 4 + lax.axis_index("field") % 4
    where = jnp.stack([mine, share]).astype(jnp.int32)
    plan = layout(waves, modes)
    half, slabs, _, place = plan
    own, piece, packed = pack_rows(mode_basis, wave_lengths, plan, where)
    parts = along_wave(piece, waves)

    selector = (
        table_index[:, None] == jnp.arange(coef_table.shape[0], dtype=jnp.int32)[None, :]
    ).astype(jnp.bfloat16)
    coeffs = jnp.dot(selector, coef_table, preferred_element_type=jnp.float32)
    one_hot = (
        template_ids[:, :, None]
        == jnp.arange(sed_table.shape[0], dtype=jnp.int32)[None, None, :]
    ).astype(jnp.float32)
    raw_weights = jnp.einsum("fjn,nl->fjl", one_hot, sed_table, precision=lax.Precision.HIGHEST)
    weights = (raw_weights / jnp.sum(raw_weights, axis=2, keepdims=True)).astype(jnp.bfloat16)
    templates = weights.shape[1]
    split = weights.reshape(positions, templates, waves, lengths)
    weights = jnp.concatenate(
        [
            split[..., :sent_lengths].reshape(positions, templates, -1),
            split[..., sent_lengths:].reshape(positions, templates, -1),
        ],
        axis=2,
    )
    path_spread, mix_spread, spread_token = spreads(coeffs.astype(jnp.bfloat16)[None], weights)
    own_length = jnp.broadcast_to(
        wave_lengths[:sent_lengths, None, None], (sent_lengths, 8, LANES)
    )
    own_row, own_column, own_token = tables(own_length, 0, PIX)

    far = tuple(s for s in range(1, waves) if min(s, waves - s) > waves // 4)
    near = tuple(s for s in range(1, waves) if s not in far)
    halves = split_parts(
        [parts[s - 1] for s in near], half, [packed, own_token, spread_token]
    )
    every, inverse = kept_lengths(parts, where, wave_lengths, half, sent_lengths)
    all_row, all_column, all_token = tables(every, mine * rows, rows)
    got = gather_halves(halves, half, near, [all_token])
    pieces = [parts[s - 1] for s in far]
    pieces = pieces[0] if len(pieces) == 1 else jnp.concatenate(pieces)
    got = got + gather_direct(pieces, half, far, [all_token])

    spectra, path, opening = whole_fields(
        own,
        got,
        path_spread,
        place,
        where,
        1.0 / wave_lengths[:sent_lengths],
        (own_row, own_column),
        (positions, modes, waves, half, slabs),
    )
    sent = lax.all_to_all(spectra, "wave", split_axis=0, concat_axis=0, tiled=True)
    sent = sent.reshape(waves * sent_lengths, positions * rows, PIX)
    images, sums = row_fields(path, opening, inverse, (all_row, all_column), positions)
    return mix(mix_spread, add_over_wave(sums, waves), sent, images, templates, rows)


def solution(mesh):
    return jax.shard_map(
        local,
        mesh=mesh,
        in_specs=(
            P(None, "wave", None),
            P(),
            P(("groups", "field")),
            P("wave"),
            P(),
            P(("groups", "field"), None),
        ),
        out_specs=P(("groups", "field"), None, "wave", None),
        check_vma=False,
    )
```
